32 devices in a mesh: mem: 8 (over z, x), fsdp: 4 (over y, core).
Axes of the slice: x: 2, y: 2, z: 4, core: 2. Of those that a mesh axis runs over, the one named last changes fastest.
Arguments:
- queries: bfloat16 [8192, 1024], P(('mem', 'fsdp')), may hold values from -10 to 10
- keys: bfloat16 [8192, 1024], P(('mem', 'fsdp')), may hold values from -7 to 7
- values: bfloat16 [8192, 1024], P(('mem', 'fsdp')), may hold values from -6 to 6
- mem_keys: bfloat16 [32768, 1024], P('mem', 'fsdp'), may hold values from -7 to 7
- mem_values: bfloat16 [32768, 1024], P('mem', 'fsdp'), may hold values from -6 to 6
- block_ids: int32 [16, 4, 8], replicated, may hold values from 0 to 255, as said below
- gate_bias: float32 [16], replicated, may hold values from -2 to 2
- out_weight: bfloat16 [1024, 2048], P('fsdp'), may hold values from -0.59765625 to 0.59765625
- cotangent: bfloat16 [8192, 2048], P(('mem', 'fsdp')), may hold values from -6 to 6
Outputs:
- projected: bfloat16 [8192, 2048], P(('mem', 'fsdp'))
- query_grad: bfloat16 [8192, 1024], P(('mem', 'fsdp'))
- key_grad: bfloat16 [8192, 1024], P(('mem', 'fsdp'))
- value_grad: bfloat16 [8192, 1024], P(('mem', 'fsdp'))
- weight_grad: float32 [1024, 2048], P('fsdp', 'mem')
The draws below stay inside these ranges and needn't reach their ends.
Inputs may be any that keep to these rules, and one draw needn't show every extreme that they name: `block_ids`: within one segment the 32 ids are distinct, at most 8 of them lie in the blocks of one index of mem (id // 32), and some index of mem has exactly 8 of them in every segment.
All inputs are finite; a program needn't handle non-finite values.
Results may differ from the reference program's by a relative error of at most 0.022.
Values may be sent and summed in bfloat16 or wider, within the bound.
No kernel may reach another device: no remote copies, remote signals or barrier semaphores. Data moves between devices by JAX's collectives and lax.ppermute only.
A program may use at most 192 MiB of HBM per device.

```python
import jax
import jax.numpy as jnp
from jax import lax

D = 2048
H = 16
DH = 64
SEG_LEN = 512
QBLK = 128
MBLK = 128
RETR = 8
MB_DEV = 32
HD = 1024
SEGS = 16
TOKENS = 8192
QB_SEG = 4
NBLK = 256
PAIRS = 32768
CAP = 8
N_MEM = 8


def draw_block_ids(key, part):
    key = jax.random.fold_in(key, 11)
    request_count = QB_SEG * RETR
    slot_count = N_MEM * CAP
    popular_key, favorite_key, common_key, segment_key = jax.random.split(key, 4)
    popular = jax.random.randint(popular_key, (N_MEM,), 0, 3)
    favorites = jax.random.randint(favorite_key, (SEGS,), 0, N_MEM)
    common_owner = jax.random.randint(common_key, (), 0, N_MEM)
    slot_owner = jnp.arange(slot_count, dtype=jnp.int32) // CAP
    slot_copy = jnp.arange(slot_count, dtype=jnp.int32) % CAP

    def one_segment(seg_key, favorite):
        order_key, shuffle_key, base_key = jax.random.split(seg_key, 3)
        level = jnp.where(slot_owner == common_owner, 4, jnp.where(slot_owner == favorite, 3, popular[slot_owner]))
        shuffled = jax.random.permutation(order_key, slot_count)
        score = level * slot_count + shuffled
        picked_scores, picked = lax.top_k(score, request_count)
        picked = jax.random.permutation(shuffle_key, picked)
        base = jax.random.randint(base_key, (N_MEM,), 0, MB_DEV)
        owners = slot_owner[picked]
        local_block = (base[owners] + slot_copy[picked]) % MB_DEV
        return (owners * MB_DEV + local_block).reshape(QB_SEG, RETR)
    seg_keys = jax.random.split(segment_key, SEGS)
    return jax.vmap(one_segment)(seg_keys, favorites).astype(jnp.int32)


def draw_queries(key, part):
    key = jax.random.fold_in(key, 21)
    return (2.0 * jax.random.truncated_normal(key, -4.0, 4.0, (TOKENS, HD), jnp.float32)).astype(jnp.bfloat16)


def draw_keys(key, part):
    key = jax.random.fold_in(key, 31)
    return jax.random.truncated_normal(key, -4.0, 4.0, (TOKENS, HD), jnp.float32).astype(jnp.bfloat16)


def draw_mem_keys(key, part):
    key = jax.random.fold_in(key, 41)
    return jax.random.truncated_normal(key, -4.0, 4.0, (PAIRS, HD), jnp.float32).astype(jnp.bfloat16)


def raised(values, own_key, source, target, parts, factor):
    owner, partner = [(jnp.arange(values.shape[axis_at]) // (values.shape[axis_at] // parts)).reshape([-1 if axis == axis_at else 1 for axis in range(values.ndim)]) for axis_at in (source, target)]
    chosen = jax.random.permutation(own_key, parts)[partner]
    strong = (owner == chosen) | (owner == (partner + parts // 2) % parts)
    return jnp.where(strong, factor * values, values)


def levels(stream_key, shape, cuts, low, high):
    gain = 1.0
    for axis_at, blocks in cuts:
        draws = jax.random.uniform(jax.random.fold_in(jax.random.fold_in(stream_key, 6), axis_at), (blocks,), jnp.float32, low / len(cuts), high / len(cuts))
        gain = gain * jnp.repeat(jnp.exp(draws), shape[axis_at] // blocks).reshape((-1,) + (1,) * (len(shape) - 1 - axis_at))
    return gain


def normal_values(key, dims, spread, bound, cuts=(), kind=jnp.bfloat16):
    loudness = levels(key, dims, cuts, -0.22, 0.18) if cuts else 1.0
    result = jax.random.normal(key, dims, jnp.float32) * spread * loudness
    return jnp.minimum(jnp.maximum(result, -bound), bound).astype(kind)


def bell_draw_with(stream_key, dims, spread, bound, shards, heavy, held_as=jnp.bfloat16):
    values = spread * jax.random.normal(stream_key, dims, jnp.float32)
    if shards:
        values = values * levels(stream_key, dims, shards, -0.22, 0.18)
    return jnp.clip(raised(values, jax.random.fold_in(stream_key, 3), *heavy), -bound, bound).astype(held_as)


def setup_inputs(seed: int = 0) -> dict:
    seeds = jax.random.split(jax.random.key(seed), 10)
    queries = draw_queries(jax.random.fold_in(seeds[9], 71), 0)
    keys = draw_keys(jax.random.fold_in(seeds[9], 71), 0)
    values = normal_values(seeds[2], (TOKENS, HD), 1.0, 6.0, ((0, 32),))
    mem_keys = draw_mem_keys(jax.random.fold_in(seeds[9], 71), 0)
    mem_values = normal_values(seeds[4], (PAIRS, HD), 1.0, 6.0, ((0, 8), (1, 4)))
    block_ids = draw_block_ids(jax.random.fold_in(seeds[9], 71), 0)
    gate_bias = jnp.clip(jax.random.uniform(seeds[6], (H,), jnp.float32, -2.0, 2.0), -2.0, 2.0)
    out_weight = normal_values(seeds[7], (HD, D), 0.1, 0.59765625, ((0, 4),))
    cotangent = bell_draw_with(seeds[8], (TOKENS, D), 1.0, 6.0, ((0, 32),), (0, 1, 32, 2.75))
    return {"queries": queries, "keys": keys, "values": values, "mem_keys": mem_keys, "mem_values": mem_values, "block_ids": block_ids, "gate_bias": gate_bias, "out_weight": out_weight, "cotangent": cotangent}


def softmax_rows(scores):
    largest = jnp.max(scores, axis=-1, keepdims=True)
    weights = jnp.exp(scores - largest)
    return weights / jnp.sum(weights, axis=-1, keepdims=True)


def back_to_float(array):
    return lax.optimization_barrier(array.astype(jnp.bfloat16)).astype(jnp.float32)


def reference(queries, keys, values, mem_keys, mem_values, block_ids, gate_bias, out_weight, cotangent):
    scaling = DH ** -0.5
    gating = jax.nn.sigmoid(gate_bias)
    local_share = 1.0 - gating
    key_blocks = mem_keys.reshape(NBLK, MBLK, HD)
    value_blocks = mem_values.reshape(NBLK, MBLK, HD)
    causal = jnp.arange(SEG_LEN)[None, :] <= jnp.arange(SEG_LEN)[:, None]

    def one_segment(segment):
        first_row = segment * SEG_LEN
        query_part = lax.dynamic_slice_in_dim(queries, first_row, SEG_LEN, 0).astype(jnp.float32).reshape(SEG_LEN, H, DH)
        key_part = lax.dynamic_slice_in_dim(keys, first_row, SEG_LEN, 0).astype(jnp.float32).reshape(SEG_LEN, H, DH)
        value_part = lax.dynamic_slice_in_dim(values, first_row, SEG_LEN, 0).astype(jnp.float32).reshape(SEG_LEN, H, DH)
        grad_part = lax.dynamic_slice_in_dim(cotangent, first_row, SEG_LEN, 0)
        segment_ids = lax.dynamic_index_in_dim(block_ids, segment, 0, keepdims=False).reshape(-1).astype(jnp.int32)
        fetched_keys = jnp.take(key_blocks, segment_ids, axis=0).reshape(QB_SEG, RETR * MBLK, H, DH).astype(jnp.float32)
        fetched_values = jnp.take(value_blocks, segment_ids, axis=0).reshape(QB_SEG, RETR * MBLK, H, DH).astype(jnp.float32)

        local_scores = jnp.einsum("qhd,khd->hqk", query_part, key_part) * scaling
        local_scores = jnp.where(causal[None], local_scores, -1e30)
        local_weights = softmax_rows(local_scores)
        local_rounded = back_to_float(local_weights)
        local_result = jnp.einsum("hqk,khd->qhd", local_rounded, value_part)

        query_blocks = query_part.reshape(QB_SEG, QBLK, H, DH)
        memory_scores = jnp.einsum("bqhd,bkhd->bhqk", query_blocks, fetched_keys) * scaling
        memory_weights = softmax_rows(memory_scores)
        memory_rounded = back_to_float(memory_weights)
        memory_result = jnp.einsum("bhqk,bkhd->bqhd", memory_rounded, fetched_values).reshape(SEG_LEN, H, DH)

        attention = (gating[None, :, None] * memory_result + local_share[None, :, None] * local_result).astype(jnp.bfloat16)
        attention = attention.reshape(SEG_LEN, HD)
        attention_grad = lax.dot_general(grad_part, out_weight, (((1,), (1,)), ((), ())), preferred_element_type=jnp.float32)
        attention_grad = back_to_float(attention_grad).reshape(SEG_LEN, H, DH)

        value_grad = local_share[None, :, None] * jnp.einsum("hqk,qhd->khd", local_rounded, attention_grad)
        local_slope = local_share[:, None, None] * jnp.einsum("qhd,khd->hqk", attention_grad, value_part)
        local_delta = local_weights * (local_slope - jnp.sum(local_weights * local_slope, axis=-1, keepdims=True))
        local_delta = back_to_float(local_delta)
        block_grad = attention_grad.reshape(QB_SEG, QBLK, H, DH)
        memory_slope = gating[None, :, None, None] * jnp.einsum("bqhd,bkhd->bhqk", block_grad, fetched_values)
        memory_delta = memory_weights * (memory_slope - jnp.sum(memory_weights * memory_slope, axis=-1, keepdims=True))
        memory_delta = back_to_float(memory_delta)
        key_grad = scaling * jnp.einsum("hqk,qhd->khd", local_delta, query_part)
        query_grad = scaling * (jnp.einsum("hqk,khd->qhd", local_delta, key_part)
                                + jnp.einsum("bhqk,bkhd->bqhd", memory_delta, fetched_keys).reshape(SEG_LEN, H, DH))
        return (attention,
                query_grad.astype(jnp.bfloat16).reshape(SEG_LEN, HD),
                key_grad.astype(jnp.bfloat16).reshape(SEG_LEN, HD),
                value_grad.astype(jnp.bfloat16).reshape(SEG_LEN, HD))

    attention, query_grad, key_grad, value_grad = lax.map(one_segment, jnp.arange(SEGS, dtype=jnp.int32))
    attention = attention.reshape(TOKENS, HD)
    projected = jnp.dot(attention, out_weight, preferred_element_type=jnp.float32).astype(jnp.bfloat16)
    weight_grad = jnp.dot(attention.T, cotangent, preferred_element_type=jnp.float32)
    return (projected, query_grad.reshape(TOKENS, HD), key_grad.reshape(TOKENS, HD),
            value_grad.reshape(TOKENS, HD), weight_grad)
```

```python
import functools

import jax
import jax.numpy as jnp
from jax import lax
from jax.experimental import pallas as pl
from jax.experimental.pallas import tpu as pltpu
from jax.sharding import PartitionSpec as P

DH = 64
QBLK = 128
MBLK = 128
LOW = -1e30
SCALE = DH ** (-0.5)
BF = jnp.bfloat16
F32 = jnp.float32
NT = (((1,), (1,)), ((), ()))
NN = (((1,), (0,)), ((), ()))
TN = (((0,), (0,)), ((), ()))


def dot(a, b, dims):
    return lax.dot_general(a, b, dims, preferred_element_type=F32)


def spread(x):
    lane = lax.broadcasted_iota(jnp.int32, x.shape, 1)
    zero = jnp.zeros_like(x)
    return jnp.concatenate(
        [jnp.where(lane < DH, x, zero), jnp.where(lane >= DH, x, zero)], axis=0
    )


def folded(x, op):
    return op(x.reshape(x.shape[0] // 8, 8, x.shape[1]), axis=0)


def own_blocks(parts):
    rows = []
    for part in parts:
        rows.append(part[:DH, :QBLK])
        rows.append(part[DH:, QBLK:])
    return rows


def load_memory(sources, targets, sems):
    copies = []
    for number, (source, target) in enumerate(zip(sources, targets)):
        copy = pltpu.make_async_copy(source, target, sems.at[number])
        copy.start()
        copies.append(copy)
    for copy in copies:
        copy.wait()


def at_slot(slot, total, per_slot, lead=0):
    def index(s, b, *_):
        block = jnp.where(s == slot, b, jnp.where(s > slot, per_slot - 1, 0))
        return (block,) + (0,) * lead

    return index


def memory_forward(
    group, pairs, counts, lists, k_own, v_own, k_par, v_par, *rest
):
    q_refs = rest[:group]
    do_refs = rest[group : 2 * group]
    o_refs = rest[2 * group : 3 * group]
    stat_ref = rest[3 * group]
    kbuf, vbuf, qbd, dobd, scores, slopes, acc, sems = rest[3 * group + 1 :]
    slot, block = pl.program_id(0), pl.program_id(1)
    number = slot * pl.num_programs(1) + block
    rows = k_own.shape[0]
    retr = scores.shape[0]

    @pl.when(number == 0)
    def _():
        load_memory(
            (k_own, k_par, v_own, v_par),
            (
                kbuf.at[pl.ds(0, rows)],
                kbuf.at[pl.ds(rows, rows)],
                vbuf.at[pl.ds(0, rows)],
                vbuf.at[pl.ds(rows, rows)],
            ),
            sems,
        )

    for i in range(group):

        @pl.when(slot == i)
        def _():
            for t in range(pairs):
                cols = slice(t * 128, (t + 1) * 128)
                qbd[t] = spread(q_refs[i][:, cols] * SCALE)
                dobd[t] = spread(do_refs[i][:, cols])

    total = counts[number]

    def first(j, largest):
        row = pl.multiple_of(lists[number * retr + j] * MBLK, MBLK)
        out = []
        for t in range(pairs):
            cols = slice(t * 128, (t + 1) * 128)
            wide = slice(t * 256, (t + 1) * 256)
            s = dot(kbuf[pl.ds(row, MBLK), cols], qbd[t], NT)
            scores[j, :, wide] = s
            slopes[j, :, wide] = dot(vbuf[pl.ds(row, MBLK), cols], dobd[t], NT)
            out.append(jnp.maximum(largest[t], folded(s, jnp.max)))
        return tuple(out)

    largest = lax.fori_loop(0, total, first, (jnp.full((8, 256), LOW, F32),) * pairs)
    largest = [jnp.max(x, axis=0, keepdims=True) for x in largest]
    acc[...] = jnp.zeros_like(acc)

    def second(j, sums):
        row = pl.multiple_of(lists[number * retr + j] * MBLK, MBLK)
        out = []
        for t in range(pairs):
            cols = slice(t * 128, (t + 1) * 128)
            wide = slice(t * 256, (t + 1) * 256)
            p = jnp.exp(scores[j, :, wide] - largest[t])
            acc[t] += dot(vbuf[pl.ds(row, MBLK), cols], p.astype(BF), TN)
            out.append(
                (
                    sums[t][0] + folded(p, jnp.sum),
                    sums[t][1] + folded(p * slopes[j, :, wide], jnp.sum),
                )
            )
        return tuple(out)

    zero = jnp.zeros((8, 256), F32)
    sums = lax.fori_loop(0, total, second, ((zero, zero),) * pairs)
    parts = []
    for t in range(pairs):
        wide = slice(t * 256, (t + 1) * 256)
        norm = jnp.sum(sums[t][0], axis=0, keepdims=True)
        mean = jnp.sum(sums[t][1], axis=0, keepdims=True)
        some = norm > 0.0
        inverse = jnp.where(some, 1.0 / jnp.where(some, norm, 1.0), 0.0)
        lse = jnp.where(some, largest[t] + jnp.log(jnp.where(some, norm, 1.0)), LOW)
        stat_ref[0, 0, 0:1, wide] = lse
        stat_ref[0, 0, 1:2, wide] = mean * inverse
        parts.append(acc[t] * inverse)
    result = jnp.concatenate(own_blocks(parts), axis=0).astype(BF)
    for i in range(group):

        @pl.when(slot == i)
        def _():
            o_refs[i][0] = result


def merged(stat_refs):
    lses = [ref[0, 0, 0:1, :] for ref in stat_refs]
    top = functools.reduce(jnp.maximum, lses)
    shares = [jnp.exp(x - top) for x in lses]
    norm = functools.reduce(jnp.add, shares)
    return top, shares, norm


def memory_backward(
    group, pairs, counts, lists, k_own, v_own, k_par, v_par, *rest
):
    q_refs = rest[:group]
    do_refs = rest[group : 2 * group]
    stat_refs = rest[2 * group : 3 * group]
    dq_refs = rest[3 * group : 4 * group]
    kbuf, vbuf, qbd, dobd, acc, sems = rest[4 * group :]
    slot, block = pl.program_id(0), pl.program_id(1)
    number = slot * pl.num_programs(1) + block
    rows = k_own.shape[0]
    retr = lists.shape[0] // counts.shape[0]

    @pl.when(number == 0)
    def _():
        load_memory(
            (k_own, k_par, v_own, v_par),
            (
                kbuf.at[pl.ds(0, rows)],
                kbuf.at[pl.ds(rows, rows)],
                vbuf.at[pl.ds(0, rows)],
                vbuf.at[pl.ds(rows, rows)],
            ),
            sems,
        )

    for i in range(group):

        @pl.when(slot == i)
        def _():
            for t in range(pairs):
                cols = slice(t * 128, (t + 1) * 128)
                qbd[t] = spread(q_refs[i][:, cols] * SCALE)
                dobd[t] = spread(do_refs[i][:, cols])

    top, shares, norm = merged(stat_refs)
    lse = top + jnp.log(norm)
    mean = functools.reduce(
        jnp.add, [x * ref[0, 0, 1:2, :] for x, ref in zip(shares, stat_refs)]
    ) / norm
    acc[...] = jnp.zeros_like(acc)

    def step(j, carry):
        row = pl.multiple_of(lists[number * retr + j] * MBLK, MBLK)
        for t in range(pairs):
            cols = slice(t * 128, (t + 1) * 128)
            wide = slice(t * 256, (t + 1) * 256)
            keys = kbuf[pl.ds(row, MBLK), cols]
            s = dot(keys, qbd[t], NT)
            slope = dot(vbuf[pl.ds(row, MBLK), cols], dobd[t], NT)
            delta = jnp.exp(s - lse[:, wide]) * (slope - mean[:, wide])
            acc[t] += dot(keys, delta.astype(BF), TN)
        return carry

    lax.fori_loop(0, counts[number], step, 0)
    result = jnp.concatenate(own_blocks([acc[t] for t in range(pairs)]), axis=0).astype(BF)
    for i in range(group):

        @pl.when(slot == i)
        def _():
            dq_refs[i][0] = result


def local_kernel(pairs, blocks, gate, q_ref, k_ref, v_ref, do_ref, o_ref, dq_ref, dk_ref, dv_ref,
                 dk_acc, dv_acc):
    dk_acc[...] = jnp.zeros_like(dk_acc)
    dv_acc[...] = jnp.zeros_like(dv_acc)
    key_at = lax.broadcasted_iota(jnp.int32, (MBLK, 2 * QBLK), 0)
    query_at = lax.broadcasted_iota(jnp.int32, (MBLK, 2 * QBLK), 1) % QBLK
    causal = key_at <= query_at
    lane = lax.broadcasted_iota(jnp.int32, (1, 128), 1)
    shares = []
    for t in range(pairs):
        shares.append(jnp.where(lane < DH, 1.0 - gate[2 * t], 1.0 - gate[2 * t + 1]))
    for t in range(pairs):
        cols = slice(t * 128, (t + 1) * 128)
        for b in range(blocks):
            q = spread(q_ref[b * QBLK : (b + 1) * QBLK, cols] * SCALE)
            do = spread(do_ref[b * QBLK : (b + 1) * QBLK, cols])
            scores, slopes = [], []
            for n in range(b + 1):
                rows = slice(n * MBLK, (n + 1) * MBLK)
                s = dot(k_ref[rows, cols], q, NT)
                scores.append(jnp.where(causal, s, LOW) if n == b else s)
                slopes.append(dot(v_ref[rows, cols], do, NT))
            largest = functools.reduce(jnp.maximum, [folded(s, jnp.max) for s in scores])
            largest = jnp.max(largest, axis=0, keepdims=True)
            weights = [jnp.exp(s - largest) for s in scores]
            norm = functools.reduce(jnp.add, [folded(p, jnp.sum) for p in weights])
            inverse = 1.0 / jnp.sum(norm, axis=0, keepdims=True)
            weights = [p * inverse for p in weights]
            mean = functools.reduce(
                jnp.add, [folded(p * x, jnp.sum) for p, x in zip(weights, slopes)]
            )
            mean = jnp.sum(mean, axis=0, keepdims=True)
            o = jnp.zeros((128, 256), F32)
            dq = jnp.zeros((128, 256), F32)
            for n in range(b + 1):
                rows = slice(n * MBLK, (n + 1) * MBLK)
                w = weights[n].astype(BF)
                delta = (weights[n] * (slopes[n] - mean)).astype(BF)
                o += dot(v_ref[rows, cols], w, TN)
                dq += dot(k_ref[rows, cols], delta, TN)
                dv_acc[rows, cols] += dot(w, do, NN)
                dk_acc[rows, cols] += dot(delta, q, NN)
            o_pair, dq_pair = own_blocks([o]), own_blocks([dq])
            for i in range(2):
                share = 1.0 - gate[2 * t + i]
                at = slice((2 * t + i) * DH, (2 * t + i + 1) * DH)
                o_ref[b, at, :] = o_pair[i] * share
                dq_ref[b, at, :] = dq_pair[i] * (share * SCALE)
        dk_ref[:, cols] = (dk_acc[:, cols] * shares[t]).astype(BF)
        dv_ref[:, cols] = (dv_acc[:, cols] * shares[t]).astype(BF)


def attention_kernel(group, heads, gate, local_ref, *rest):
    o_refs = rest[:group]
    stat_refs = rest[group : 2 * group]
    out_ref = rest[2 * group]
    _, shares, norm = merged(stat_refs)
    rows = []
    for h in range(heads):
        at = slice(h * DH, (h + 1) * DH)
        wide = slice(h * QBLK, (h + 1) * QBLK)
        total = functools.reduce(
            jnp.add,
            [x[:, wide] * ref[0, at, :].astype(F32) for x, ref in zip(shares, o_refs)],
        )
        rows.append(total * (gate[h] / norm[:, wide]) + local_ref[0, at, :])
    out_ref[...] = jnp.concatenate(rows, axis=0).T.astype(BF)


def query_grad_kernel(group, heads, gate, local_ref, *rest):
    dq_refs = rest[:group]
    out_ref = rest[group]
    rows = []
    for h in range(heads):
        at = slice(h * DH, (h + 1) * DH)
        total = functools.reduce(jnp.add, [ref[0, at, :].astype(F32) for ref in dq_refs])
        rows.append(total * (gate[h] * SCALE) + local_ref[0, at, :])
    out_ref[...] = jnp.concatenate(rows, axis=0).T.astype(BF)


ANY = pl.BlockSpec(memory_space=pl.ANY)
SMEM = pl.BlockSpec(memory_space=pltpu.SMEM)


def block_lists(block_ids, me, group, seg_dev, per_dev):
    segments, per_seg, retr = block_ids.shape
    z = me // 2
    ids = block_ids.reshape(segments // (2 * seg_dev), 2, seg_dev * per_seg, retr)
    ids = lax.dynamic_index_in_dim(ids, me % 2, 1, keepdims=False)
    slots = (z - jnp.arange(group, dtype=jnp.int32)) % group
    ids = jnp.take(ids, slots, axis=0).reshape(group * seg_dev * per_seg, retr)
    owners = ids // per_dev
    here = owners // 2 == z
    place = ids - owners * per_dev + jnp.where(owners == me, 0, per_dev)
    position = jnp.arange(retr, dtype=jnp.int32)
    before = (position[None, :] < position[:, None])[None]
    rank = jnp.sum(jnp.logical_and(before, here[:, None, :]), axis=-1)
    chosen = jnp.logical_and(here[:, :, None], rank[:, :, None] == position)
    lists = jnp.sum(jnp.where(chosen, place[:, :, None], 0), axis=1)
    counts = jnp.sum(here, axis=-1)
    return counts.astype(jnp.int32), lists.astype(jnp.int32).reshape(-1)


def to_heads(x):
    parts = lax.axis_size("fsdp")
    rows, width = x.shape
    x = x.reshape(rows, parts, width // parts).transpose(1, 0, 2)
    x = lax.all_to_all(x, "fsdp", split_axis=0, concat_axis=0, tiled=True)
    return x.reshape(parts * rows, width // parts)


def to_tokens(x):
    parts = lax.axis_size("fsdp")
    x = x.reshape(parts, x.shape[0] // parts, x.shape[1])
    return lax.all_to_all(x, "fsdp", split_axis=0, concat_axis=0, tiled=True)


def side_by_side(x):
    parts, rows, width = x.shape
    return x.transpose(1, 0, 2).reshape(rows, parts * width)


def gather_tokens(x):
    parts = lax.axis_size("fsdp")
    if parts != 4:
        return lax.all_gather(x, "fsdp", axis=0, tiled=True)
    f = lax.axis_index("fsdp")
    rows = x.shape[0]
    far = lax.ppermute(x, "fsdp", [(i, i ^ 2) for i in range(4)])
    near = lax.ppermute(x, "fsdp", [(i, i ^ 1) for i in range(4)])
    both = lax.ppermute(far, "fsdp", [(i, i ^ 1) for i in range(4)])
    out = jnp.zeros((4 * rows, x.shape[1]), x.dtype)
    for part, at in ((x, f), (near, f ^ 1), (far, f ^ 2), (both, f ^ 3)):
        out = lax.dynamic_update_slice_in_dim(out, part, at * rows, 0)
    return out


def per_device(
    queries, keys, values, mem_keys, mem_values, block_ids, gate_bias, out_weight, cotangent
):
    n = lax.axis_size("mem")
    me = lax.axis_index("mem")
    group = n // 2
    width = mem_keys.shape[1]
    heads = width // DH
    pairs = heads // 2
    segments, per_seg, retr = block_ids.shape
    seg_dev = segments // n
    per_dev = mem_keys.shape[0] // MBLK
    blocks = seg_dev * per_seg
    tokens = blocks * QBLK
    seg_len = per_seg * QBLK
    gating = jax.nn.sigmoid(
        lax.dynamic_slice_in_dim(gate_bias, lax.axis_index("fsdp") * heads, heads)
    )

    def shifted(x, k):
        return lax.ppermute(x, "mem", [(i, (i + 2 * k) % n) for i in range(n)])

    swap = [(i, i ^ 1) for i in range(n)]
    par_keys = lax.ppermute(mem_keys, "mem", swap)
    par_values = lax.ppermute(mem_values, "mem", swap)

    q = to_heads(queries)
    q_slots = [q] + [shifted(q, k) for k in range(1, group)]
    cot = gather_tokens(cotangent)
    do = dot(cot, out_weight, NT).astype(BF)
    do_slots = [do] + [shifted(do, k) for k in range(1, group)]
    k = to_heads(keys)
    v = to_heads(values)
    full_weight = lax.all_gather(out_weight, "fsdp", axis=0, tiled=True)
    counts, lists = block_lists(block_ids, me, group, seg_dev, per_dev)

    seg_spec = pl.BlockSpec((seg_len, width), lambda s: (s, 0))
    part_spec = pl.BlockSpec((per_seg, width, QBLK), lambda s: (s, 0, 0))
    part_shape = jax.ShapeDtypeStruct((blocks, width, QBLK), F32)
    head_shape = jax.ShapeDtypeStruct((tokens, width), BF)
    o_local, dq_local, dk, dv = pl.pallas_call(
        functools.partial(local_kernel, pairs, per_seg),
        grid=(seg_dev,),
        in_specs=[SMEM, seg_spec, seg_spec, seg_spec, seg_spec],
        out_specs=[part_spec, part_spec, seg_spec, seg_spec],
        out_shape=[part_shape, part_shape, head_shape, head_shape],
        scratch_shapes=[pltpu.VMEM((seg_len, width), F32), pltpu.VMEM((seg_len, width), F32)],
        compiler_params=pltpu.CompilerParams(vmem_limit_bytes=32 * 2**20),
        name="local",
    )(gating, q, k, v, do)

    row_specs = [
        pl.BlockSpec((QBLK, width), at_slot(i, group, blocks, 1)) for i in range(group)
    ]
    t_specs = [
        pl.BlockSpec((1, width, QBLK), at_slot(i, group, blocks, 2)) for i in range(group)
    ]
    t_shape = jax.ShapeDtypeStruct((blocks, width, QBLK), BF)
    stat_block = (1, 1, 2, heads * QBLK)
    memory_rows = 2 * mem_keys.shape[0]
    buffers = [pltpu.VMEM((memory_rows, width), BF), pltpu.VMEM((memory_rows, width), BF)]
    spreads = [pltpu.VMEM((pairs, 256, 128), BF), pltpu.VMEM((pairs, 256, 128), BF)]
    acc = pltpu.VMEM((pairs, 128, 256), F32)
    limit = pltpu.CompilerParams(vmem_limit_bytes=40 * 2**20)
    memory = (mem_keys, mem_values, par_keys, par_values)
    outs = pl.pallas_call(
        functools.partial(memory_forward, group, pairs),
        grid_spec=pltpu.PrefetchScalarGridSpec(
            num_scalar_prefetch=2,
            grid=(group, blocks),
            in_specs=[ANY] * 4 + row_specs * 2,
            out_specs=t_specs + [pl.BlockSpec(stat_block, lambda s, b, *_: (s, b, 0, 0))],
            scratch_shapes=buffers
            + spreads
            + [pltpu.VMEM((retr, MBLK, heads * QBLK), F32)] * 2
            + [acc, pltpu.SemaphoreType.DMA((4,))],
        ),
        out_shape=[t_shape] * group
        + [jax.ShapeDtypeStruct((group, blocks, 2, heads * QBLK), F32)],
        compiler_params=limit,
        name="memory_forward",
    )(counts, lists, *memory, *q_slots, *do_slots)
    o_slots, stats = outs[:group], outs[group]
    stat_slots = [stats] + [shifted(stats, k) for k in range(1, group)]
    o_home = [o_slots[0]] + [shifted(o_slots[k], -k) for k in range(1, group)]

    stat_specs = [
        pl.BlockSpec(stat_block, lambda s, b, *_, k=k: ((s - k) % group, b, 0, 0))
        for k in range(group)
    ]
    dq_slots = pl.pallas_call(
        functools.partial(memory_backward, group, pairs),
        grid_spec=pltpu.PrefetchScalarGridSpec(
            num_scalar_prefetch=2,
            grid=(group, blocks),
            in_specs=[ANY] * 4 + row_specs * 2 + stat_specs,
            out_specs=t_specs,
            scratch_shapes=buffers + spreads + [acc, pltpu.SemaphoreType.DMA((4,))],
        ),
        out_shape=[t_shape] * group,
        compiler_params=limit,
        name="memory_backward",
    )(counts, lists, *memory, *q_slots, *do_slots, *stat_slots)
    dq_home = [dq_slots[0]] + [shifted(dq_slots[k], -k) for k in range(1, group)]

    home_spec = pl.BlockSpec((1, width, QBLK), lambda b: (b, 0, 0))
    home_out = pl.BlockSpec((QBLK, width), lambda b: (b, 0))
    home_stats = [stat_slots[(group - k) % group] for k in range(group)]
    home_specs = [
        pl.BlockSpec(stat_block, lambda b, k=k: (k, b, 0, 0)) for k in range(group)
    ]
    attention = pl.pallas_call(
        functools.partial(attention_kernel, group, heads),
        grid=(blocks,),
        in_specs=[SMEM] + [home_spec] * (1 + group) + home_specs,
        out_specs=home_out,
        out_shape=head_shape,
        name="attention",
    )(gating, o_local, *o_home, *home_stats)
    dq = pl.pallas_call(
        functools.partial(query_grad_kernel, group, heads),
        grid=(blocks,),
        in_specs=[SMEM] + [home_spec] * (1 + group),
        out_specs=home_out,
        out_shape=head_shape,
        name="query_grad",
    )(gating, dq_local, *dq_home)

    token_attention = to_tokens(attention)
    parts = token_attention.shape[0]
    projected = jnp.einsum(
        "stc,scd->td",
        token_attention,
        full_weight.reshape(parts, width, -1),
        preferred_element_type=F32,
    ).astype(BF)
    partial = dot(attention, cot, TN).astype(BF)
    columns = partial.shape[1] // n
    partial = partial.reshape(width, n, columns).transpose(1, 0, 2)
    partial = lax.all_to_all(partial, "mem", split_axis=0, concat_axis=0, tiled=True)
    weight_grad = jnp.sum(partial.astype(F32), axis=0)
    return (
        projected,
        side_by_side(to_tokens(dq)),
        side_by_side(to_tokens(dk)),
        side_by_side(to_tokens(dv)),
        weight_grad,
    )


def solution(mesh):
    in_specs = (
        P(("mem", "fsdp"), None),
        P(("mem", "fsdp"), None),
        P(("mem", "fsdp"), None),
        P("mem", "fsdp"),
        P("mem", "fsdp"),
        P(),
        P(),
        P("fsdp", None),
        P(("mem", "fsdp"), None),
    )
    out_specs = (
        P(("mem", "fsdp"), None),
        P(("mem", "fsdp"), None),
        P(("mem", "fsdp"), None),
        P(("mem", "fsdp"), None),
        P("fsdp", "mem"),
    )
    return jax.shard_map(
        per_device, mesh=mesh, in_specs=in_specs, out_specs=out_specs, check_vma=False
    )
```

```python
import functools

import jax
import jax.numpy as jnp
from jax import lax
from jax.experimental import pallas as pl
from jax.experimental.pallas import tpu as pltpu
from jax.sharding import PartitionSpec as P

DH = 64
QBLK = 128
MBLK = 128
LOW = -1e30
UNROLL = 4
HALVES = 1
SCALE = DH ** (-0.5)
BF = jnp.bfloat16
F32 = jnp.float32
NT = (((1,), (1,)), ((), ()))
NN = (((1,), (0,)), ((), ()))
TN = (((0,), (0,)), ((), ()))


def dot(a, b, dims):
    return lax.dot_general(a, b, dims, preferred_element_type=F32)


def spread(x):
    zero = jnp.zeros((DH, QBLK), x.dtype)
    upper = jnp.concatenate([x[:DH], zero], axis=1)
    lower = jnp.concatenate([zero, x[DH:]], axis=1)
    return jnp.concatenate([upper, lower], axis=0)


def query_block(ref, b, t):
    per = ref.shape[2] // QBLK
    return ref[b // per, t * 128 : (t + 1) * 128, (b % per) * QBLK : (b % per + 1) * QBLK]


def folded(x, op):
    return op(x.reshape(x.shape[0] // 8, 8, x.shape[1]), axis=0)


def own_blocks(parts):
    rows = []
    for part in parts:
        rows.append(part[:DH, :QBLK])
        rows.append(part[DH:, QBLK:])
    return rows


def at_slot(slot, last, column=0):
    def index(s, b, *_):
        return (jnp.where(s == slot, b, jnp.where(s > slot, last, 0)), column, 0)

    return index


def start_step(group, pairs, half, slot, memory, buffers, sems, q_refs, do_refs, q_t, do_t):
    rows, width = buffers[0].shape
    rows = rows // 2
    blocks = q_t.shape[0] - 1

    @pl.when((slot == 0) & (pl.program_id(1) == 0))
    def _():
        own = pl.ds(half * width, width)
        sources = [memory[0].at[:, own], memory[1], memory[2].at[:, own], memory[3]]
        targets = [buffers[i].at[pl.ds(j * rows, rows)] for i in range(2) for j in range(2)]
        copies = [
            pltpu.make_async_copy(source, target, sems.at[i])
            for i, (source, target) in enumerate(zip(sources, targets))
        ]
        for copy in copies:
            copy.start()
        q_t[...] = jnp.zeros_like(q_t)
        do_t[...] = jnp.zeros_like(do_t)
        for copy in copies:
            copy.wait()

    for i in range(group):

        @pl.when(slot == i)
        def _():
            for b in range(blocks):
                for t in range(pairs):
                    for refs, out in ((q_refs, q_t), (do_refs, do_t)):
                        x = query_block(refs[i], b, t)
                        out[b, t, :DH, :QBLK] = x[:DH]
                        out[b, t, DH:, QBLK:] = x[DH:]


def memory_forward(
    group, pairs, half, counts, places, homes, k_own, k_par, v_own, v_par, *rest
):
    q_refs = rest[:group]
    do_refs = rest[group : 2 * group]
    o_refs = rest[2 * group : 3 * group]
    stat_ref = rest[3 * group]
    kbuf, vbuf, q_t, do_t, scores, tops, norms, means, acc, sems = rest[3 * group + 1 :]
    slot = pl.program_id(0)
    number = slot * pl.num_programs(1) + pl.program_id(1)
    cap = scores.shape[0]
    blocks = q_t.shape[0] - 1
    start_step(
        group, pairs, half, slot, (k_own, k_par, v_own, v_par), (kbuf, vbuf), sems,
        q_refs, do_refs, q_t, do_t,
    )
    tops[...] = jnp.full(tops.shape, LOW, F32)
    norms[...] = jnp.zeros_like(norms)
    means[...] = jnp.zeros_like(means)
    acc[...] = jnp.zeros_like(acc)
    turns = (counts[number] + UNROLL - 1) // UNROLL

    def first(turn, carry):
        found = []
        for u in range(UNROLL):
            j = turn * UNROLL + u
            row = pl.multiple_of(places[number * cap + j] * MBLK, MBLK)
            b = homes[number * cap + j]
            for t in range(pairs):
                cols = slice(t * 128, (t + 1) * 128)
                s = dot(kbuf[pl.ds(row, MBLK), cols], q_t[b, t], NN)
                scores[j, t] = s
                found.append((b, t, folded(s, jnp.max)))
        for b, t, top in found:
            tops[b, t] = jnp.maximum(tops[b, t], top)
        return carry

    lax.fori_loop(0, turns, first, 0)
    tops[...] = jnp.broadcast_to(jnp.max(tops[...], axis=2, keepdims=True), tops.shape)

    def second(turn, carry):
        found = []
        for u in range(UNROLL):
            j = turn * UNROLL + u
            row = pl.multiple_of(places[number * cap + j] * MBLK, MBLK)
            b = homes[number * cap + j]
            for t in range(pairs):
                cols = slice(t * 128, (t + 1) * 128)
                values = vbuf[pl.ds(row, MBLK), cols]
                slope = dot(values, do_t[b, t], NN)
                p = jnp.exp(scores[j, t] - tops[b, t, 0:1, :])
                found.append(
                    (b, t, folded(p, jnp.sum), folded(p * slope, jnp.sum),
                     dot(values, p.astype(BF), TN))
                )
        for b, t, norm, mean, o in found:
            norms[b, t] += norm
            means[b, t] += mean
            acc[b, t] += o
        return carry

    lax.fori_loop(0, turns, second, 0)
    results = []
    for b in range(blocks):
        parts = []
        for t in range(pairs):
            wide = slice(t * 256, (t + 1) * 256)
            norm = jnp.sum(norms[b, t], axis=0, keepdims=True)
            mean = jnp.sum(means[b, t], axis=0, keepdims=True)
            some = norm > 0.0
            safe = jnp.where(some, norm, 1.0)
            inverse = 1.0 / safe
            lse = jnp.where(some, tops[b, t, 0:1, :] + jnp.log(safe), LOW)
            stat_ref[0, b, 0:1, wide] = lse
            stat_ref[0, b, 1:2, wide] = mean * inverse
            parts.append(acc[b, t] * inverse)
        results.append(jnp.concatenate(own_blocks(parts), axis=0).astype(BF))
    for i in range(group):

        @pl.when(slot == i)
        def _():
            for b in range(blocks):
                o_refs[i][b] = results[b]


def merged(stat_refs, b):
    lses = [ref[0, b, 0:1, :] for ref in stat_refs]
    top = functools.reduce(jnp.maximum, lses)
    shares = [jnp.exp(x - top) for x in lses]
    norm = functools.reduce(jnp.add, shares)
    return top, shares, norm


def memory_backward(
    group, pairs, half, counts, places, homes, k_own, k_par, v_own, v_par, *rest
):
    q_refs = rest[:group]
    do_refs = rest[group : 2 * group]
    stat_refs = rest[2 * group : 3 * group]
    dq_refs = rest[3 * group : 4 * group]
    kbuf, vbuf, q_t, do_t, weights, lses, means, acc, sems = rest[4 * group :]
    slot = pl.program_id(0)
    number = slot * pl.num_programs(1) + pl.program_id(1)
    cap = places.shape[0] // counts.shape[0]
    blocks = q_t.shape[0] - 1
    start_step(
        group, pairs, half, slot, (k_own, k_par, v_own, v_par), (kbuf, vbuf), sems,
        q_refs, do_refs, q_t, do_t,
    )
    lses[...] = jnp.zeros_like(lses)
    means[...] = jnp.zeros_like(means)
    for b in range(blocks):
        top, shares, norm = merged(stat_refs, b)
        lse = top + jnp.log(norm)
        mean = functools.reduce(
            jnp.add, [x * ref[0, b, 1:2, :] for x, ref in zip(shares, stat_refs)]
        ) / norm
        for t in range(pairs):
            wide = slice(t * 256, (t + 1) * 256)
            lses[b, t] = lse[:, wide]
            means[b, t] = mean[:, wide]
    acc[...] = jnp.zeros_like(acc)

    turns = (counts[number] + UNROLL - 1) // UNROLL

    def first(turn, carry):
        for u in range(UNROLL):
            j = turn * UNROLL + u
            row = pl.multiple_of(places[number * cap + j] * MBLK, MBLK)
            b = homes[number * cap + j]
            for t in range(pairs):
                cols = slice(t * 128, (t + 1) * 128)
                s = dot(kbuf[pl.ds(row, MBLK), cols], q_t[b, t], NN)
                weights[j, t] = jnp.exp(s - lses[b, t])
        return carry

    lax.fori_loop(0, turns, first, 0)

    def second(turn, carry):
        found = []
        for u in range(UNROLL):
            j = turn * UNROLL + u
            row = pl.multiple_of(places[number * cap + j] * MBLK, MBLK)
            b = homes[number * cap + j]
            for t in range(pairs):
                cols = slice(t * 128, (t + 1) * 128)
                slope = dot(vbuf[pl.ds(row, MBLK), cols], do_t[b, t], NN)
                delta = weights[j, t] * (slope - means[b, t])
                found.append((b, t, dot(kbuf[pl.ds(row, MBLK), cols], delta.astype(BF), TN)))
        for b, t, dq in found:
            acc[b, t] += dq
        return carry

    lax.fori_loop(0, turns, second, 0)
    results = [
        jnp.concatenate(own_blocks([acc[b, t] for t in range(pairs)]), axis=0).astype(BF)
        for b in range(blocks)
    ]
    for i in range(group):

        @pl.when(slot == i)
        def _():
            for b in range(blocks):
                dq_refs[i][b] = results[b]


def local_kernel(pairs, blocks, halves, gate, q_ref, k_ref, v_ref, *rest):
    do_refs = rest[:halves]
    o_ref, dq_ref, dk_ref, dv_ref, dk_acc, dv_acc = rest[halves:]
    per_half = pairs // halves
    dk_acc[...] = jnp.zeros_like(dk_acc)
    dv_acc[...] = jnp.zeros_like(dv_acc)
    key_at = lax.broadcasted_iota(jnp.int32, (MBLK, 2 * QBLK), 0)
    query_at = lax.broadcasted_iota(jnp.int32, (MBLK, 2 * QBLK), 1) % QBLK
    causal = key_at <= query_at
    lane = lax.broadcasted_iota(jnp.int32, (1, 128), 1)
    shares = []
    for t in range(pairs):
        shares.append(jnp.where(lane < DH, 1.0 - gate[2 * t], 1.0 - gate[2 * t + 1]))
    for t in range(pairs):
        cols = slice(t * 128, (t + 1) * 128)
        for b in range(blocks):
            q = spread(query_block(q_ref, b, t))
            do = spread(query_block(do_refs[t // per_half], b, t % per_half))
            scores, slopes = [], []
            for n in range(b + 1):
                rows = slice(n * MBLK, (n + 1) * MBLK)
                s = dot(k_ref[rows, cols], q, NN)
                scores.append(jnp.where(causal, s, LOW) if n == b else s)
                slopes.append(dot(v_ref[rows, cols], do, NN))
            largest = functools.reduce(jnp.maximum, [folded(s, jnp.max) for s in scores])
            largest = jnp.max(largest, axis=0, keepdims=True)
            weights = [jnp.exp(s - largest) for s in scores]
            norm = functools.reduce(jnp.add, [folded(p, jnp.sum) for p in weights])
            inverse = 1.0 / jnp.sum(norm, axis=0, keepdims=True)
            weights = [p * inverse for p in weights]
            mean = functools.reduce(
                jnp.add, [folded(p * x, jnp.sum) for p, x in zip(weights, slopes)]
            )
            mean = jnp.sum(mean, axis=0, keepdims=True)
            o = jnp.zeros((128, 256), F32)
            dq = jnp.zeros((128, 256), F32)
            for n in range(b + 1):
                rows = slice(n * MBLK, (n + 1) * MBLK)
                w = weights[n].astype(BF)
                delta = (weights[n] * (slopes[n] - mean)).astype(BF)
                o += dot(v_ref[rows, cols], w, TN)
                dq += dot(k_ref[rows, cols], delta, TN)
                dv_acc[rows, cols] += dot(w, do, NT)
                dk_acc[rows, cols] += dot(delta, q, NT)
            o_pair, dq_pair = own_blocks([o]), own_blocks([dq])
            for i in range(2):
                share = 1.0 - gate[2 * t + i]
                at = slice((2 * t + i) * DH, (2 * t + i + 1) * DH)
                o_ref[b, at, :] = o_pair[i] * share
                dq_ref[b, at, :] = dq_pair[i] * (share * SCALE)
        dk_ref[:, cols] = (dk_acc[:, cols] * shares[t]).astype(BF)
        dv_ref[:, cols] = (dv_acc[:, cols] * shares[t]).astype(BF)


def attention_kernel(group, heads, first, gate, local_ref, *rest):
    o_refs = rest[:group]
    stat_refs = rest[group : 2 * group]
    out_ref, out_t_ref = rest[2 * group :]
    for b in range(local_ref.shape[0]):
        _, shares, norm = merged(stat_refs, b)
        rows = []
        for h in range(heads):
            at = slice(h * DH, (h + 1) * DH)
            wide = slice(h * QBLK, (h + 1) * QBLK)
            total = functools.reduce(
                jnp.add,
                [x[:, wide] * ref[b, at, :].astype(F32) for x, ref in zip(shares, o_refs)],
            )
            rows.append(total * (gate[first + h] / norm[:, wide]) + local_ref[b, at, :])
        result = jnp.concatenate(rows, axis=0).astype(BF)
        out_t_ref[:, b * QBLK : (b + 1) * QBLK] = result
        out_ref[b * QBLK : (b + 1) * QBLK, :] = result.T


def query_grad_kernel(group, heads, first, gate, local_ref, *rest):
    dq_refs = rest[:group]
    out_ref = rest[group]
    for b in range(local_ref.shape[0]):
        rows = []
        for h in range(heads):
            at = slice(h * DH, (h + 1) * DH)
            total = functools.reduce(jnp.add, [ref[b, at, :].astype(F32) for ref in dq_refs])
            rows.append(total * (gate[first + h] * SCALE) + local_ref[b, at, :])
        result = jnp.concatenate(rows, axis=0).astype(BF)
        out_ref[b * QBLK : (b + 1) * QBLK, :] = result.T


def attention_grad_kernel(order, weight_ref, *rest):
    part_refs, out_refs = rest[:4], rest[4:]
    for i in range(4):
        grad = dot(weight_ref[...], part_refs[i][...], NT).astype(BF)
        rows = grad.shape[0] // len(out_refs)
        for j, out_ref in enumerate(out_refs):
            out_ref[order[i]] = grad[j * rows : (j + 1) * rows]


def weight_grad_kernel(order, dests, attention_ref, *rest):
    part_refs, (send_ref, keep_ref) = rest[:4], rest[4:]
    tokens = part_refs[0].shape[0]
    total = None
    for i in range(4):
        at = pl.multiple_of(order[i] * tokens, tokens)
        term = dot(attention_ref[:, pl.ds(at, tokens)], part_refs[i][...], NN)
        total = term if total is None else total + term

    @pl.when(pl.program_id(0) == 0)
    def _():
        send_ref[0] = total.astype(BF)

    @pl.when(pl.program_id(0) == 1)
    def _():
        keep_ref[0] = total.astype(BF)


ANY = pl.BlockSpec(memory_space=pl.ANY)
SMEM = pl.BlockSpec(memory_space=pltpu.SMEM)


def block_lists(block_ids, me, group, seg_dev, per_dev, cap):
    segments, per_seg, retr = block_ids.shape
    asked = per_seg * retr
    z = me // 2
    ids = block_ids.reshape(segments // (2 * seg_dev), 2, seg_dev, asked)
    ids = lax.dynamic_index_in_dim(ids, me % 2, 1, keepdims=False)
    slots = (z - jnp.arange(group, dtype=jnp.int32)) % group
    ids = jnp.take(ids, slots, axis=0).reshape(group * seg_dev, asked)
    owners = ids // per_dev
    here = owners // 2 == z
    place = ids - owners * per_dev + jnp.where(owners == me, 0, per_dev)
    position = jnp.arange(asked, dtype=jnp.int32)
    before = (position[None, :] < position[:, None])[None]
    rank = jnp.sum(jnp.logical_and(before, here[:, None, :]), axis=-1)
    chosen = jnp.logical_and(
        here[:, :, None], rank[:, :, None] == jnp.arange(cap, dtype=jnp.int32)
    )
    places = jnp.sum(jnp.where(chosen, place[:, :, None], 0), axis=1)
    home = position // retr - per_seg
    homes = per_seg + jnp.sum(jnp.where(chosen, home[None, :, None], 0), axis=1)
    counts = jnp.sum(here, axis=-1)
    return (
        counts.astype(jnp.int32),
        places.astype(jnp.int32).reshape(-1),
        homes.astype(jnp.int32).reshape(-1),
    )


def side_by_side(x):
    parts, rows, width = x.shape
    return x.transpose(1, 0, 2).reshape(rows, parts * width)


def gather_tokens(x):
    far = lax.ppermute(x, "fsdp", [(i, i ^ 2) for i in range(4)])
    near = lax.ppermute(x, "fsdp", [(i, i ^ 1) for i in range(4)])
    both = lax.ppermute(far, "fsdp", [(i, i ^ 1) for i in range(4)])
    return [x, near, far, both]


def weight_grad_plain(attention, parts, order):
    n = lax.axis_size("mem")
    rows = parts[0].shape[0]
    total = 0.0
    for i, part in enumerate(parts):
        own = lax.dynamic_slice_in_dim(attention, order[i] * rows, rows, 0)
        total = total + dot(own, part, TN)
    pieces = total.astype(BF).reshape(total.shape[0], n, -1).transpose(1, 0, 2)
    pieces = lax.all_to_all(pieces, "mem", split_axis=0, concat_axis=0, tiled=True)
    return jnp.sum(pieces.astype(F32), axis=0)


def after(first, *rest):
    return lax.optimization_barrier((first,) + rest)[1:]


def per_device(
    queries, keys, values, mem_keys, mem_values, block_ids, gate_bias, out_weight, cotangent
):
    n = lax.axis_size("mem")
    me = lax.axis_index("mem")
    fs = lax.axis_index("fsdp")
    group = n // 2
    full = mem_keys.shape[1]
    all_heads = full // DH
    width = full // HALVES
    heads = width // DH
    pairs = heads // 2
    segments, per_seg, retr = block_ids.shape
    seg_dev = segments // n
    per_dev = mem_keys.shape[0] // MBLK
    blocks = seg_dev * per_seg
    tokens = blocks * QBLK
    seg_len = per_seg * QBLK
    rows = queries.shape[0]
    seg_rows = seg_len // rows
    gating = jax.nn.sigmoid(lax.dynamic_slice_in_dim(gate_bias, fs * all_heads, all_heads))
    halves = range(HALVES)

    def shifted(x, k):
        return lax.ppermute(x, "mem", [(i, (i + 2 * k) % n) for i in range(n)])

    def exchange(x):
        return lax.all_to_all(x, "fsdp", split_axis=0, concat_axis=0, tiled=True)

    swap = [(i, i ^ 1) for i in range(n)]
    cap = -(-4 * max(1, retr * per_seg // n) // UNROLL) * UNROLL
    lists = block_lists(block_ids, me, group, seg_dev, per_dev, cap)

    par_keys, par_values = [], []
    for i in halves:
        k_part = mem_keys[:, i * width : (i + 1) * width]
        v_part = mem_values[:, i * width : (i + 1) * width]
        if i:
            (k_part,) = after(par_keys[-1], k_part)
            (v_part,) = after(par_values[-1], v_part)
        par_keys.append(lax.ppermute(k_part, "mem", swap))
        par_values.append(lax.ppermute(v_part, "mem", swap))

    q = exchange((queries * BF(SCALE)).T.reshape(4, full, rows))
    q_slots = [q] + [shifted(q, k) for k in range(1, group)]
    (cotangent,) = after(q, cotangent)
    cot_parts = gather_tokens(cotangent)
    order = fs ^ jnp.arange(4, dtype=jnp.int32)
    whole = pl.BlockSpec(memory_space=pltpu.VMEM)
    do_parts = pl.pallas_call(
        attention_grad_kernel,
        in_specs=[SMEM] + [whole] * 5,
        out_specs=[whole] * HALVES,
        out_shape=[jax.ShapeDtypeStruct((4, width, rows), BF)] * HALVES,
        compiler_params=pltpu.CompilerParams(vmem_limit_bytes=24 * 2**20),
        name="attention_grad",
    )(order, out_weight, *cot_parts)
    do_slots = [[x] + [shifted(x, k) for k in range(1, group)] for x in do_parts]
    keys, values = after(do_parts[0], keys, values)
    k, v = (
        exchange(x.reshape(rows, 4, full).transpose(1, 0, 2)).reshape(tokens, full)
        for x in (keys, values)
    )
    (late_weight,) = after(v, out_weight)
    full_weight = lax.all_gather(late_weight, "fsdp", axis=0, tiled=True)

    seg_spec = pl.BlockSpec((seg_len, full), lambda s: (s, 0))
    q_spec = pl.BlockSpec((seg_rows, full, rows), lambda s: (s, 0, 0))
    do_spec = pl.BlockSpec((seg_rows, width, rows), lambda s: (s, 0, 0))
    part_spec = pl.BlockSpec((per_seg, full, QBLK), lambda s: (s, 0, 0))
    part_shape = jax.ShapeDtypeStruct((blocks, full, QBLK), F32)
    head_shape = jax.ShapeDtypeStruct((tokens, full), BF)
    o_local, dq_local, dk, dv = pl.pallas_call(
        functools.partial(local_kernel, all_heads // 2, per_seg, HALVES),
        grid=(seg_dev,),
        in_specs=[SMEM, q_spec, seg_spec, seg_spec] + [do_spec] * HALVES,
        out_specs=[part_spec, part_spec, seg_spec, seg_spec],
        out_shape=[part_shape, part_shape, head_shape, head_shape],
        scratch_shapes=[pltpu.VMEM((seg_len, full), F32)] * 2,
        compiler_params=pltpu.CompilerParams(vmem_limit_bytes=32 * 2**20),
        name="local",
    )(gating, q, k, v, *do_parts)

    t_specs = [
        pl.BlockSpec((per_seg, width, QBLK), at_slot(i, seg_dev - 1)) for i in range(group)
    ]
    t_shape = jax.ShapeDtypeStruct((blocks, width, QBLK), BF)
    stat_block = (1, per_seg, 2, heads * QBLK)
    memory_rows = 2 * mem_keys.shape[0]
    scratch = [pltpu.VMEM((memory_rows, width), BF)] * 2
    scratch += [pltpu.VMEM((per_seg + 1, pairs, 128, 256), BF)] * 2
    scratch += [pltpu.VMEM((cap, pairs, MBLK, 256), F32)]
    acc = pltpu.VMEM((per_seg + 1, pairs, 128, 256), F32)
    rows8 = pltpu.VMEM((per_seg + 1, pairs, 8, 256), F32)
    rows1 = pltpu.VMEM((per_seg + 1, pairs, 1, 256), F32)
    sems = pltpu.SemaphoreType.DMA((4,))
    limit = pltpu.CompilerParams(vmem_limit_bytes=40 * 2**20)
    stat_specs = [
        pl.BlockSpec(stat_block, lambda s, b, *_, k=k: ((s - k) % group, b, 0, 0))
        for k in range(group)
    ]

    def slot_specs(half):
        return [
            pl.BlockSpec((seg_rows, width, rows), at_slot(i, seg_dev - 1, half))
            for i in range(group)
        ]

    o_home, stat_slots = [], []
    for i in halves:
        outs = pl.pallas_call(
            functools.partial(memory_forward, group, pairs, i),
            grid_spec=pltpu.PrefetchScalarGridSpec(
                num_scalar_prefetch=3,
                grid=(group, seg_dev),
                in_specs=[ANY] * 4 + slot_specs(i) + slot_specs(0),
                out_specs=t_specs + [pl.BlockSpec(stat_block, lambda s, b, *_: (s, b, 0, 0))],
                scratch_shapes=scratch + [rows8, rows8, rows8, acc, sems],
            ),
            out_shape=[t_shape] * group
            + [jax.ShapeDtypeStruct((group, blocks, 2, heads * QBLK), F32)],
            compiler_params=limit,
            name="memory_forward",
        )(*lists, mem_keys, par_keys[i], mem_values, par_values[i], *q_slots, *do_slots[i])
        stats = outs[group]
        stat_slots.append([stats] + [shifted(stats, k) for k in range(1, group)])
        o_home.append([outs[0]] + [shifted(outs[k], -k) for k in range(1, group)])

    dq_home = []
    last = stat_slots[-1][0]
    for i in halves:
        first_stats = after(last, *stat_slots[i])
        dq_slots = pl.pallas_call(
            functools.partial(memory_backward, group, pairs, i),
            grid_spec=pltpu.PrefetchScalarGridSpec(
                num_scalar_prefetch=3,
                grid=(group, seg_dev),
                in_specs=[ANY] * 4 + slot_specs(i) + slot_specs(0) + stat_specs,
                out_specs=t_specs,
                scratch_shapes=scratch + [rows1, rows1, acc, sems],
            ),
            out_shape=[t_shape] * group,
            compiler_params=limit,
            name="memory_backward",
        )(
            *lists, mem_keys, par_keys[i], mem_values, par_values[i],
            *q_slots, *do_slots[i], *first_stats,
        )
        last = dq_slots[0]
        dq_home.append([dq_slots[0]] + [shifted(dq_slots[k], -k) for k in range(1, group)])

    home_spec = pl.BlockSpec((per_seg, width, QBLK), lambda b: (b, 0, 0))
    home_out = pl.BlockSpec((seg_len, width), lambda b: (b, 0))
    home_shape = jax.ShapeDtypeStruct((tokens, width), BF)
    home_specs = [
        pl.BlockSpec(stat_block, lambda b, k=k: (k, b, 0, 0)) for k in range(group)
    ]
    columns = out_weight.shape[1] // n
    steps = jnp.arange(group, dtype=jnp.int32)
    homes = (me // 2 - steps) % group * 2
    dests = jnp.concatenate([homes + (1 - me % 2), homes + me % 2])
    token_attention, weight_rows, token_dq = [], [], []
    for i in halves:
        local_spec = pl.BlockSpec((per_seg, width, QBLK), lambda b, i=i: (b, i, 0))
        home_stats = [stat_slots[i][(group - k) % group] for k in range(group)]
        o_parts = after(last, *o_home[i])
        attention, attention_t = pl.pallas_call(
            functools.partial(attention_kernel, group, heads, i * heads),
            grid=(seg_dev,),
            in_specs=[SMEM, local_spec] + [home_spec] * group + home_specs,
            out_specs=[home_out, pl.BlockSpec((width, seg_len), lambda b: (0, b))],
            out_shape=[home_shape, jax.ShapeDtypeStruct((width, tokens), BF)],
            name="attention",
        )(gating, o_local, *o_parts, *home_stats)
        token_attention.append(exchange(attention.reshape(4, rows, width)))
        if columns % 128:
            weight_rows.append(weight_grad_plain(attention, cot_parts, order))
            continue
        piece = (1, width, columns)
        send, keep = pl.pallas_call(
            weight_grad_kernel,
            grid_spec=pltpu.PrefetchScalarGridSpec(
                num_scalar_prefetch=2,
                grid=(2, group),
                in_specs=[pl.BlockSpec((width, tokens), lambda p, k, *_: (0, 0))]
                + [
                    pl.BlockSpec((rows, columns), lambda p, k, _, to: (0, to[p * group + k]))
                ]
                * 4,
                out_specs=[
                    pl.BlockSpec(piece, lambda p, k, *_: (jnp.where(p == 0, k, group - 1), 0, 0)),
                    pl.BlockSpec(piece, lambda p, k, *_: (jnp.where(p == 0, 0, k), 0, 0)),
                ],
            ),
            out_shape=[jax.ShapeDtypeStruct((group, width, columns), BF)] * 2,
            name="weight_grad",
        )(order, dests, attention_t, *cot_parts)
        got = lax.ppermute(send, "mem", swap)
        sums = [
            (keep[k].astype(F32) + got[k].astype(F32)).astype(BF) for k in range(group)
        ]
        sums = [sums[0]] + [shifted(sums[k], -k) for k in range(1, group)]
        weight_rows.append(functools.reduce(jnp.add, [x.astype(F32) for x in sums]))
    for i in halves:
        local_spec = pl.BlockSpec((per_seg, width, QBLK), lambda b, i=i: (b, i, 0))
        dq = pl.pallas_call(
            functools.partial(query_grad_kernel, group, heads, i * heads),
            grid=(seg_dev,),
            in_specs=[SMEM, local_spec] + [home_spec] * group,
            out_specs=home_out,
            out_shape=home_shape,
            name="query_grad",
        )(gating, dq_local, *dq_home[i])
        token_dq.append(exchange(dq.reshape(4, rows, width)))

    projected = jnp.einsum(
        "stc,scd->td",
        jnp.concatenate(token_attention, axis=2),
        full_weight.reshape(4, full, -1),
        preferred_element_type=F32,
    ).astype(BF)
    dk, dv = after(last, dk, dv)
    return (
        projected,
        side_by_side(jnp.concatenate(token_dq, axis=2)),
        side_by_side(exchange(dk.reshape(4, rows, full))),
        side_by_side(exchange(dv.reshape(4, rows, full))),
        jnp.concatenate(weight_rows, axis=0),
    )


def solution(mesh):
    in_specs = (
        P(("mem", "fsdp"), None),
        P(("mem", "fsdp"), None),
        P(("mem", "fsdp"), None),
        P("mem", "fsdp"),
        P("mem", "fsdp"),
        P(),
        P(),
        P("fsdp", None),
        P(("mem", "fsdp"), None),
    )
    out_specs = (
        P(("mem", "fsdp"), None),
        P(("mem", "fsdp"), None),
        P(("mem", "fsdp"), None),
        P(("mem", "fsdp"), None),
        P("fsdp", "mem"),
    )
    return jax.shard_map(
        per_device, mesh=mesh, in_specs=in_specs, out_specs=out_specs, check_vma=False
    )
```

```python
import functools

import jax
import jax.numpy as jnp
from jax import lax
from jax.experimental import pallas as pl
from jax.experimental.pallas import tpu as pltpu
from jax.sharding import PartitionSpec as P

DH = 64
QBLK = 128
MBLK = 128
LOW = -1e30
UNROLL = 4
HALVES = 1
ORDER = True
SCALE = DH ** (-0.5)
BF = jnp.bfloat16
F32 = jnp.float32
NT = (((1,), (1,)), ((), ()))
NN = (((1,), (0,)), ((), ()))
TN = (((0,), (0,)), ((), ()))


def dot(a, b, dims):
    return lax.dot_general(a, b, dims, preferred_element_type=F32)


def spread(x):
    zero = jnp.zeros((DH, QBLK), x.dtype)
    upper = jnp.concatenate([x[:DH], zero], axis=1)
    lower = jnp.concatenate([zero, x[DH:]], axis=1)
    return jnp.concatenate([upper, lower], axis=0)


def query_block(ref, b, t):
    per = ref.shape[2] // QBLK
    return ref[b // per, t * 128 : (t + 1) * 128, (b % per) * QBLK : (b % per + 1) * QBLK]


def folded(x, op):
    return op(x.reshape(x.shape[0] // 8, 8, x.shape[1]), axis=0)


def own_blocks(parts):
    rows = []
    for part in parts:
        rows.append(part[:DH, :QBLK])
        rows.append(part[DH:, QBLK:])
    return rows


def at_slot(slot, last, column=0):
    def index(s, b, *_):
        return (jnp.where(s == slot, b, jnp.where(s > slot, last, 0)), column, 0)

    return index


def start_step(group, half, slot, memory, buffers, sems, sides):
    rows, width = buffers[0].shape
    rows = rows // 2

    @pl.when((slot == 0) & (pl.program_id(1) == 0))
    def _():
        own = pl.ds(half * width, width)
        sources = [memory[0].at[:, own], memory[1], memory[2].at[:, own], memory[3]]
        targets = [buffers[i].at[pl.ds(j * rows, rows)] for i in range(2) for j in range(2)]
        copies = [
            pltpu.make_async_copy(source, target, sems.at[i])
            for i, (source, target) in enumerate(zip(sources, targets))
        ]
        for copy in copies:
            copy.start()
        for _, out in sides:
            out[...] = jnp.zeros_like(out)
        for copy in copies:
            copy.wait()

    for i in range(group):

        @pl.when(slot == i)
        def _():
            for refs, out in sides:
                for b in range(out.shape[0] - 1):
                    for t in range(out.shape[1]):
                        x = query_block(refs[i], b, t)
                        out[b, t, :DH, :QBLK] = x[:DH]
                        out[b, t, DH:, QBLK:] = x[DH:]


def memory_forward(
    group, pairs, half, counts, places, homes, k_own, k_par, v_own, v_par, *rest
):
    q_refs = rest[:group]
    o_refs = rest[group : 2 * group]
    exact_refs = rest[2 * group : 3 * group]
    lse_ref = rest[3 * group]
    kbuf, vbuf, q_t, scores, tops, norms, acc, sems = rest[3 * group + 1 :]
    slot = pl.program_id(0)
    number = slot * pl.num_programs(1) + pl.program_id(1)
    cap = scores.shape[0]
    blocks = q_t.shape[0] - 1
    start_step(
        group, half, slot, (k_own, k_par, v_own, v_par), (kbuf, vbuf), sems, [(q_refs, q_t)]
    )
    tops[...] = jnp.full(tops.shape, LOW, F32)
    norms[...] = jnp.zeros_like(norms)
    acc[...] = jnp.zeros_like(acc)
    turns = (counts[number] + UNROLL - 1) // UNROLL

    def first(turn, carry):
        found = []
        for u in range(UNROLL):
            j = turn * UNROLL + u
            row = pl.multiple_of(places[number * cap + j] * MBLK, MBLK)
            b = homes[number * cap + j]
            for t in range(pairs):
                cols = slice(t * 128, (t + 1) * 128)
                s = dot(kbuf[pl.ds(row, MBLK), cols], q_t[b, t], NN)
                scores[j, t] = s
                found.append((b, t, folded(s, jnp.max)))
        for b, t, top in found:
            tops[b, t] = jnp.maximum(tops[b, t], top)
        return carry

    lax.fori_loop(0, turns, first, 0)
    tops[...] = jnp.broadcast_to(jnp.max(tops[...], axis=2, keepdims=True), tops.shape)

    def second(turn, carry):
        found = []
        for u in range(UNROLL):
            j = turn * UNROLL + u
            row = pl.multiple_of(places[number * cap + j] * MBLK, MBLK)
            b = homes[number * cap + j]
            for t in range(pairs):
                cols = slice(t * 128, (t + 1) * 128)
                p = jnp.exp(scores[j, t] - tops[b, t, 0:1, :])
                o = dot(vbuf[pl.ds(row, MBLK), cols], p.astype(BF), TN)
                found.append((b, t, folded(p, jnp.sum), o))
        for b, t, norm, o in found:
            norms[b, t] += norm
            acc[b, t] += o
        return carry

    lax.fori_loop(0, turns, second, 0)
    results = []
    for b in range(blocks):
        parts = []
        for t in range(pairs):
            wide = slice(t * 256, (t + 1) * 256)
            norm = jnp.sum(norms[b, t], axis=0, keepdims=True)
            some = norm > 0.0
            safe = jnp.where(some, norm, 1.0)
            lse_ref[0, b, :, wide] = jnp.where(some, tops[b, t, 0:1, :] + jnp.log(safe), LOW)
            parts.append(acc[b, t] * (1.0 / safe))
        results.append(jnp.concatenate(own_blocks(parts), axis=0))
    for i in range(group):

        @pl.when(slot == i)
        def _():
            for b in range(blocks):
                exact_refs[i][b] = results[b]
                o_refs[i][b] = results[b].astype(BF)


def statistics_kernel(group, heads, lse_ref, *rest):
    do_refs, o_refs, stat_ref = rest[:group], rest[group : 2 * group], rest[2 * group]
    for i in range(group):

        @pl.when(pl.program_id(0) == i)
        def _():
            for b in range(lse_ref.shape[1]):
                stat_ref[0, b, 0:1, :] = lse_ref[0, b]
                for t in range(heads // 2):
                    do = query_block(do_refs[i], b, t).astype(F32)
                    product = do * o_refs[i][b, t * 128 : (t + 1) * 128, :]
                    for h in range(2):
                        at = slice((2 * t + h) * QBLK, (2 * t + h + 1) * QBLK)
                        stat_ref[0, b, 1:2, at] = jnp.sum(
                            product[h * DH : (h + 1) * DH], axis=0, keepdims=True
                        )


def merged(stat_refs, b):
    lses = [ref[0, b, 0:1, :] for ref in stat_refs]
    top = functools.reduce(jnp.maximum, lses)
    shares = [jnp.exp(x - top) for x in lses]
    norm = functools.reduce(jnp.add, shares)
    return top, shares, norm


def memory_backward(
    group, pairs, half, counts, places, homes, k_own, k_par, v_own, v_par, *rest
):
    q_refs = rest[:group]
    do_refs = rest[group : 2 * group]
    stat_refs = rest[2 * group : 3 * group]
    dq_refs = rest[3 * group : 4 * group]
    kbuf, vbuf, q_t, do_t, weights, lses, means, acc, sems = rest[4 * group :]
    slot = pl.program_id(0)
    number = slot * pl.num_programs(1) + pl.program_id(1)
    cap = places.shape[0] // counts.shape[0]
    blocks = q_t.shape[0] - 1
    start_step(
        group, half, slot, (k_own, k_par, v_own, v_par), (kbuf, vbuf), sems,
        [(q_refs, q_t), (do_refs, do_t)],
    )
    lses[...] = jnp.zeros_like(lses)
    means[...] = jnp.zeros_like(means)
    for b in range(blocks):
        top, shares, norm = merged(stat_refs, b)
        lse = top + jnp.log(norm)
        mean = functools.reduce(
            jnp.add, [x * ref[0, b, 1:2, :] for x, ref in zip(shares, stat_refs)]
        ) / norm
        for t in range(pairs):
            wide = slice(t * 256, (t + 1) * 256)
            lses[b, t] = lse[:, wide]
            means[b, t] = mean[:, wide]
    acc[...] = jnp.zeros_like(acc)

    turns = (counts[number] + UNROLL - 1) // UNROLL

    def first(turn, carry):
        for u in range(UNROLL):
            j = turn * UNROLL + u
            row = pl.multiple_of(places[number * cap + j] * MBLK, MBLK)
            b = homes[number * cap + j]
            for t in range(pairs):
                cols = slice(t * 128, (t + 1) * 128)
                s = dot(kbuf[pl.ds(row, MBLK), cols], q_t[b, t], NN)
                weights[j, t] = jnp.exp(s - lses[b, t])
        return carry

    lax.fori_loop(0, turns, first, 0)

    def second(turn, carry):
        found = []
        for u in range(UNROLL):
            j = turn * UNROLL + u
            row = pl.multiple_of(places[number * cap + j] * MBLK, MBLK)
            b = homes[number * cap + j]
            for t in range(pairs):
                cols = slice(t * 128, (t + 1) * 128)
                slope = dot(vbuf[pl.ds(row, MBLK), cols], do_t[b, t], NN)
                delta = weights[j, t] * (slope - means[b, t])
                found.append((b, t, dot(kbuf[pl.ds(row, MBLK), cols], delta.astype(BF), TN)))
        for b, t, dq in found:
            acc[b, t] += dq
        return carry

    lax.fori_loop(0, turns, second, 0)
    results = [
        jnp.concatenate(own_blocks([acc[b, t] for t in range(pairs)]), axis=0).astype(BF)
        for b in range(blocks)
    ]
    for i in range(group):

        @pl.when(slot == i)
        def _():
            for b in range(blocks):
                dq_refs[i][b] = results[b]


def local_kernel(pairs, blocks, halves, gate, q_ref, k_ref, v_ref, *rest):
    do_refs = rest[:halves]
    o_ref, dq_ref, dk_ref, dv_ref, dk_acc, dv_acc = rest[halves:]
    per_half = pairs // halves
    dk_acc[...] = jnp.zeros_like(dk_acc)
    dv_acc[...] = jnp.zeros_like(dv_acc)
    key_at = lax.broadcasted_iota(jnp.int32, (MBLK, 2 * QBLK), 0)
    query_at = lax.broadcasted_iota(jnp.int32, (MBLK, 2 * QBLK), 1) % QBLK
    causal = key_at <= query_at
    lane = lax.broadcasted_iota(jnp.int32, (1, 128), 1)
    shares = []
    for t in range(pairs):
        shares.append(jnp.where(lane < DH, 1.0 - gate[2 * t], 1.0 - gate[2 * t + 1]))
    for t in range(pairs):
        cols = slice(t * 128, (t + 1) * 128)
        for b in range(blocks):
            q = spread(query_block(q_ref, b, t))
            do = spread(query_block(do_refs[t // per_half], b, t % per_half))
            scores, slopes = [], []
            for n in range(b + 1):
                rows = slice(n * MBLK, (n + 1) * MBLK)
                s = dot(k_ref[rows, cols], q, NN)
                scores.append(jnp.where(causal, s, LOW) if n == b else s)
                slopes.append(dot(v_ref[rows, cols], do, NN))
            largest = functools.reduce(jnp.maximum, [folded(s, jnp.max) for s in scores])
            largest = jnp.max(largest, axis=0, keepdims=True)
            weights = [jnp.exp(s - largest) for s in scores]
            norm = functools.reduce(jnp.add, [folded(p, jnp.sum) for p in weights])
            inverse = 1.0 / jnp.sum(norm, axis=0, keepdims=True)
            weights = [p * inverse for p in weights]
            mean = functools.reduce(
                jnp.add, [folded(p * x, jnp.sum) for p, x in zip(weights, slopes)]
            )
            mean = jnp.sum(mean, axis=0, keepdims=True)
            o = jnp.zeros((128, 256), F32)
            dq = jnp.zeros((128, 256), F32)
            for n in range(b + 1):
                rows = slice(n * MBLK, (n + 1) * MBLK)
                w = weights[n].astype(BF)
                delta = (weights[n] * (slopes[n] - mean)).astype(BF)
                o += dot(v_ref[rows, cols], w, TN)
                dq += dot(k_ref[rows, cols], delta, TN)
                dv_acc[rows, cols] += dot(w, do, NT)
                dk_acc[rows, cols] += dot(delta, q, NT)
            o_pair, dq_pair = own_blocks([o]), own_blocks([dq])
            for i in range(2):
                share = 1.0 - gate[2 * t + i]
                at = slice((2 * t + i) * DH, (2 * t + i + 1) * DH)
                o_ref[b, at, :] = o_pair[i] * share
                dq_ref[b, at, :] = dq_pair[i] * (share * SCALE)
        dk_ref[:, cols] = (dk_acc[:, cols] * shares[t]).astype(BF)
        dv_ref[:, cols] = (dv_acc[:, cols] * shares[t]).astype(BF)


def attention_kernel(group, heads, first, gate, local_ref, *rest):
    o_refs = rest[:group]
    stat_refs = rest[group : 2 * group]
    out_ref, out_t_ref = rest[2 * group :]
    for b in range(local_ref.shape[0]):
        _, shares, norm = merged(stat_refs, b)
        rows = []
        for h in range(heads):
            at = slice(h * DH, (h + 1) * DH)
            wide = slice(h * QBLK, (h + 1) * QBLK)
            total = functools.reduce(
                jnp.add,
                [x[:, wide] * ref[b, at, :].astype(F32) for x, ref in zip(shares, o_refs)],
            )
            rows.append(total * (gate[first + h] / norm[:, wide]) + local_ref[b, at, :])
        result = jnp.concatenate(rows, axis=0).astype(BF)
        out_t_ref[:, b * QBLK : (b + 1) * QBLK] = result
        out_ref[b * QBLK : (b + 1) * QBLK, :] = result.T


def query_grad_kernel(group, heads, first, gate, local_ref, *rest):
    dq_refs = rest[:group]
    out_ref = rest[group]
    for b in range(local_ref.shape[0]):
        rows = []
        for h in range(heads):
            at = slice(h * DH, (h + 1) * DH)
            total = functools.reduce(jnp.add, [ref[b, at, :].astype(F32) for ref in dq_refs])
            rows.append(total * (gate[first + h] * SCALE) + local_ref[b, at, :])
        result = jnp.concatenate(rows, axis=0).astype(BF)
        out_ref[b * QBLK : (b + 1) * QBLK, :] = result.T


def attention_grad_kernel(order, weight_ref, *rest):
    part_refs, out_refs = rest[:4], rest[4:]
    for i in range(4):
        grad = dot(weight_ref[...], part_refs[i][...], NT).astype(BF)
        rows = grad.shape[0] // len(out_refs)
        for j, out_ref in enumerate(out_refs):
            out_ref[order[i]] = grad[j * rows : (j + 1) * rows]


def weight_grad_kernel(order, dests, attention_ref, *rest):
    part_refs, (send_ref, keep_ref) = rest[:4], rest[4:]
    tokens = part_refs[0].shape[0]
    columns = part_refs[0].shape[1] // 2
    total = None
    for i in range(4):
        at = pl.multiple_of(order[i] * tokens, tokens)
        term = dot(attention_ref[:, pl.ds(at, tokens)], part_refs[i][...], NN)
        total = term if total is None else total + term
    total = total.astype(BF)
    side = dests[dests.shape[0] - 1]

    @pl.when(side == 0)
    def _():
        keep_ref[0] = total[:, :columns]
        send_ref[0] = total[:, columns:]

    @pl.when(side == 1)
    def _():
        keep_ref[0] = total[:, columns:]
        send_ref[0] = total[:, :columns]


ANY = pl.BlockSpec(memory_space=pl.ANY)
SMEM = pl.BlockSpec(memory_space=pltpu.SMEM)


def block_lists(block_ids, me, group, seg_dev, per_dev, cap):
    segments, per_seg, retr = block_ids.shape
    asked = per_seg * retr
    z = me // 2
    ids = block_ids.reshape(segments // (2 * seg_dev), 2, seg_dev, asked)
    ids = lax.dynamic_index_in_dim(ids, me % 2, 1, keepdims=False)
    slots = (z - jnp.arange(group, dtype=jnp.int32)) % group
    ids = jnp.take(ids, slots, axis=0).reshape(group * seg_dev, asked)
    owners = ids // per_dev
    here = owners // 2 == z
    place = ids - owners * per_dev + jnp.where(owners == me, 0, per_dev)
    position = jnp.arange(asked, dtype=jnp.int32)
    before = (position[None, :] < position[:, None])[None]
    rank = jnp.sum(jnp.logical_and(before, here[:, None, :]), axis=-1)
    chosen = jnp.logical_and(
        here[:, :, None], rank[:, :, None] == jnp.arange(cap, dtype=jnp.int32)
    )
    places = jnp.sum(jnp.where(chosen, place[:, :, None], 0), axis=1)
    home = position // retr - per_seg
    homes = per_seg + jnp.sum(jnp.where(chosen, home[None, :, None], 0), axis=1)
    counts = jnp.sum(here, axis=-1)
    return (
        counts.astype(jnp.int32),
        places.astype(jnp.int32).reshape(-1),
        homes.astype(jnp.int32).reshape(-1),
    )


def side_by_side(x):
    parts, rows, width = x.shape
    return x.transpose(1, 0, 2).reshape(rows, parts * width)


def gather_tokens(x):
    far = lax.ppermute(x, "fsdp", [(i, i ^ 2) for i in range(4)])
    near = lax.ppermute(x, "fsdp", [(i, i ^ 1) for i in range(4)])
    both = lax.ppermute(far, "fsdp", [(i, i ^ 1) for i in range(4)])
    return [x, near, far, both]


def weight_grad_plain(attention, parts, order):
    n = lax.axis_size("mem")
    rows = parts[0].shape[0]
    total = 0.0
    for i, part in enumerate(parts):
        own = lax.dynamic_slice_in_dim(attention, order[i] * rows, rows, 0)
        total = total + dot(own, part, TN)
    pieces = total.astype(BF).reshape(total.shape[0], n, -1).transpose(1, 0, 2)
    pieces = lax.all_to_all(pieces, "mem", split_axis=0, concat_axis=0, tiled=True)
    return jnp.sum(pieces.astype(F32), axis=0)


def cost(us):
    return pl.CostEstimate(flops=us * 10**9, bytes_accessed=us * 10**6, transcendentals=0)


def after(first, *rest):
    return lax.optimization_barrier((first, *rest))[1:]


def per_device(
    queries, keys, values, mem_keys, mem_values, block_ids, gate_bias, out_weight, cotangent
):
    n = lax.axis_size("mem")
    me = lax.axis_index("mem")
    fs = lax.axis_index("fsdp")
    group = n // 2
    full = mem_keys.shape[1]
    all_heads = full // DH
    width = full // HALVES
    heads = width // DH
    pairs = heads // 2
    segments, per_seg, retr = block_ids.shape
    seg_dev = segments // n
    per_dev = mem_keys.shape[0] // MBLK
    blocks = seg_dev * per_seg
    tokens = blocks * QBLK
    seg_len = per_seg * QBLK
    rows = queries.shape[0]
    seg_rows = seg_len // rows
    gating = jax.nn.sigmoid(lax.dynamic_slice_in_dim(gate_bias, fs * all_heads, all_heads))
    halves = range(HALVES)

    def shifted(x, k):
        return lax.ppermute(x, "mem", [(i, (i + 2 * k) % n) for i in range(n)])

    def exchange(x):
        return lax.all_to_all(x, "fsdp", split_axis=0, concat_axis=0, tiled=True)

    swap = [(i, i ^ 1) for i in range(n)]
    cap = -(-4 * max(1, retr * per_seg // n) // UNROLL) * UNROLL
    lists = block_lists(block_ids, me, group, seg_dev, per_dev, cap)

    par_keys = [lax.ppermute(mem_keys, "mem", swap)]
    par_values = [lax.ppermute(mem_values, "mem", swap)]

    q = exchange((queries * BF(SCALE)).T.reshape(4, full, rows))
    q_slots = [q] + [shifted(q, k) for k in range(1, group)]
    (cotangent,) = after(q, cotangent)
    cot_parts = gather_tokens(cotangent)
    keys, values = after(q, keys, values)
    k, v = (
        exchange(x.reshape(rows, 4, full).transpose(1, 0, 2)).reshape(tokens, full)
        for x in (keys, values)
    )
    cot_parts = after((q_slots, k, v), *cot_parts)
    order = fs ^ jnp.arange(4, dtype=jnp.int32)
    whole = pl.BlockSpec(memory_space=pltpu.VMEM)
    do_parts = pl.pallas_call(
        attention_grad_kernel,
        in_specs=[SMEM] + [whole] * 5,
        out_specs=[whole] * HALVES,
        out_shape=[jax.ShapeDtypeStruct((4, width, rows), BF)] * HALVES,
        compiler_params=pltpu.CompilerParams(vmem_limit_bytes=24 * 2**20),
        cost_estimate=cost(1),
            name="attention_grad",
    )(order, out_weight, *cot_parts)
    do_slots = [[x] + [shifted(x, k) for k in range(1, group)] for x in do_parts]
    (late_weight,) = after(v, out_weight)
    full_weight = lax.all_gather(late_weight, "fsdp", axis=0, tiled=True)

    t_specs = [
        pl.BlockSpec((per_seg, width, QBLK), at_slot(i, seg_dev - 1)) for i in range(group)
    ]
    t_shape = jax.ShapeDtypeStruct((blocks, width, QBLK), BF)
    stat_block = (1, per_seg, 2, heads * QBLK)
    memory_rows = 2 * mem_keys.shape[0]
    scratch = [pltpu.VMEM((memory_rows, width), BF)] * 2
    scratch += [pltpu.VMEM((per_seg + 1, pairs, 128, 256), BF)] * 2
    scratch += [pltpu.VMEM((cap, pairs, MBLK, 256), F32)]
    acc = pltpu.VMEM((per_seg + 1, pairs, 128, 256), F32)
    rows8 = pltpu.VMEM((per_seg + 1, pairs, 8, 256), F32)
    rows1 = pltpu.VMEM((per_seg + 1, pairs, 1, 256), F32)
    sems = pltpu.SemaphoreType.DMA((4,))
    limit = pltpu.CompilerParams(vmem_limit_bytes=40 * 2**20)
    stat_specs = [
        pl.BlockSpec(stat_block, lambda s, b, *_, k=k: ((s - k) % group, b, 0, 0))
        for k in range(group)
    ]

    def slot_specs(half):
        return [
            pl.BlockSpec((seg_rows, width, rows), at_slot(i, seg_dev - 1, half))
            for i in range(group)
        ]

    o_home, stat_slots = [], []
    spreads = [pltpu.VMEM((per_seg + 1, pairs, 128, 256), BF)]
    for i in halves:
        outs = pl.pallas_call(
            functools.partial(memory_forward, group, pairs, i),
            grid_spec=pltpu.PrefetchScalarGridSpec(
                num_scalar_prefetch=3,
                grid=(group, seg_dev),
                in_specs=[ANY] * 4 + slot_specs(i),
                out_specs=t_specs
                + t_specs
                + [
                    pl.BlockSpec(
                        (1, per_seg, 1, heads * QBLK), lambda s, b, *_: (s, b, 0, 0)
                    )
                ],
                scratch_shapes=scratch[:2] + spreads + scratch[-1:] + [rows8, rows8, acc, sems],
            ),
            out_shape=[t_shape] * group
            + [jax.ShapeDtypeStruct(t_shape.shape, F32)] * group
            + [jax.ShapeDtypeStruct((group, blocks, 1, heads * QBLK), F32)],
            compiler_params=limit,
            cost_estimate=cost(30),
            name="memory_forward",
        )(*lists, mem_keys, par_keys[i], mem_values, par_values[i], *q_slots)
        o_slots, exact, lse = outs[:group], outs[group : 2 * group], outs[-1]
        stats = pl.pallas_call(
            functools.partial(statistics_kernel, group, heads),
            grid=(group, seg_dev),
            in_specs=[
                pl.BlockSpec((1, per_seg, 1, heads * QBLK), lambda s, b: (s, b, 0, 0))
            ]
            + slot_specs(0)
            + t_specs,
            out_specs=pl.BlockSpec(stat_block, lambda s, b: (s, b, 0, 0)),
            out_shape=jax.ShapeDtypeStruct((group, blocks, 2, heads * QBLK), F32),
            cost_estimate=cost(5),
            name="statistics",
        )(lse, *do_slots[i], *exact)
        stat_slots.append([stats] + [shifted(stats, k) for k in range(1, group)])
        if ORDER:
            o_slots = after(stat_slots[-1], *o_slots)
        o_home.append([o_slots[0]] + [shifted(o_slots[k], -k) for k in range(1, group)])

    last = stat_slots[-1][0]
    seg_spec = pl.BlockSpec((seg_len, full), lambda s: (s, 0))
    q_spec = pl.BlockSpec((seg_rows, full, rows), lambda s: (s, 0, 0))
    do_spec = pl.BlockSpec((seg_rows, width, rows), lambda s: (s, 0, 0))
    part_spec = pl.BlockSpec((per_seg, full, QBLK), lambda s: (s, 0, 0))
    part_shape = jax.ShapeDtypeStruct((blocks, full, QBLK), F32)
    head_shape = jax.ShapeDtypeStruct((tokens, full), BF)
    o_local, dq_local, dk, dv = pl.pallas_call(
        functools.partial(local_kernel, all_heads // 2, per_seg, HALVES),
        grid=(seg_dev,),
        in_specs=[SMEM, q_spec, seg_spec, seg_spec] + [do_spec] * HALVES,
        out_specs=[part_spec, part_spec, seg_spec, seg_spec],
        out_shape=[part_shape, part_shape, head_shape, head_shape],
        scratch_shapes=[pltpu.VMEM((seg_len, full), F32)] * 2,
        compiler_params=pltpu.CompilerParams(vmem_limit_bytes=32 * 2**20),
        cost_estimate=cost(1),
            name="local",
    )(gating, q, *after(last, k, v), *do_parts)

    dq_home = []
    last = after((last, o_local), last)[0]
    for i in halves:
        first_stats = after(last, *stat_slots[i])
        dq_slots = pl.pallas_call(
            functools.partial(memory_backward, group, pairs, i),
            grid_spec=pltpu.PrefetchScalarGridSpec(
                num_scalar_prefetch=3,
                grid=(group, seg_dev),
                in_specs=[ANY] * 4 + slot_specs(i) + slot_specs(0) + stat_specs,
                out_specs=t_specs,
                scratch_shapes=scratch + [rows1, rows1, acc, sems],
            ),
            out_shape=[t_shape] * group,
            compiler_params=limit,
            cost_estimate=cost(30),
            name="memory_backward",
        )(
            *lists, mem_keys, par_keys[i], mem_values, par_values[i],
            *q_slots, *do_slots[i], *first_stats,
        )
        last = dq_slots[0]
        dq_home.append([dq_slots[0]] + [shifted(dq_slots[k], -k) for k in range(1, group)])

    dk, dv = after(last, dk, dv)
    key_grad, value_grad = [side_by_side(exchange(x.reshape(4, rows, full))) for x in (dk, dv)]
    home_spec = pl.BlockSpec((per_seg, width, QBLK), lambda b: (b, 0, 0))
    home_out = pl.BlockSpec((seg_len, width), lambda b: (b, 0))
    home_shape = jax.ShapeDtypeStruct((tokens, width), BF)
    home_specs = [
        pl.BlockSpec(stat_block, lambda b, k=k: (k, b, 0, 0)) for k in range(group)
    ]
    columns = out_weight.shape[1] // n
    steps = jnp.arange(group, dtype=jnp.int32)
    dests = jnp.concatenate([(me // 2 - steps) % group, (me % 2)[None]]).astype(jnp.int32)
    token_attention, weight_rows, token_dq = [], [], []
    for i in halves:
        local_spec = pl.BlockSpec((per_seg, width, QBLK), lambda b, i=i: (b, i, 0))
        home_stats = [stat_slots[i][(group - k) % group] for k in range(group)]
        o_parts = after(last, *o_home[i])
        attention, attention_t = pl.pallas_call(
            functools.partial(attention_kernel, group, heads, i * heads),
            grid=(seg_dev,),
            in_specs=[SMEM, local_spec] + [home_spec] * group + home_specs,
            out_specs=[home_out, pl.BlockSpec((width, seg_len), lambda b: (0, b))],
            out_shape=[home_shape, jax.ShapeDtypeStruct((width, tokens), BF)],
            cost_estimate=cost(3),
            name="attention",
        )(gating, o_local, *o_parts, *home_stats)
        token_attention.append(exchange(attention.reshape(4, rows, width)))
        if columns % 128:
            weight_rows.append(weight_grad_plain(attention, cot_parts, order))
            continue
        piece = (1, width, columns)
        send, keep = pl.pallas_call(
            weight_grad_kernel,
            grid_spec=pltpu.PrefetchScalarGridSpec(
                num_scalar_prefetch=2,
                grid=(group,),
                in_specs=[pl.BlockSpec((width, tokens), lambda k, *_: (0, 0))]
                + [pl.BlockSpec((rows, 2 * columns), lambda k, _, to: (0, to[k]))] * 4,
                out_specs=[pl.BlockSpec(piece, lambda k, *_: (k, 0, 0))] * 2,
            ),
            out_shape=[jax.ShapeDtypeStruct((group, width, columns), BF)] * 2,
            cost_estimate=cost(5),
            name="weight_grad",
        )(order, dests, attention_t, *cot_parts)
        got = lax.ppermute(send, "mem", swap)
        sums = [
            (keep[k].astype(F32) + got[k].astype(F32)).astype(BF) for k in range(group)
        ]
        sums = [sums[0]] + [shifted(sums[k], -k) for k in range(1, group)]
        weight_rows.append(functools.reduce(jnp.add, [x.astype(F32) for x in sums]))
    projected = jnp.einsum(
        "stc,scd->td",
        jnp.concatenate(token_attention, axis=2),
        full_weight.reshape(4, full, -1),
        preferred_element_type=F32,
    ).astype(BF)
    for i in halves:
        dq_parts = after(projected, *dq_home[i])
        local_spec = pl.BlockSpec((per_seg, width, QBLK), lambda b, i=i: (b, i, 0))
        dq = pl.pallas_call(
            functools.partial(query_grad_kernel, group, heads, i * heads),
            grid=(seg_dev,),
            in_specs=[SMEM, local_spec] + [home_spec] * group,
            out_specs=home_out,
            out_shape=home_shape,
            cost_estimate=cost(3),
            name="query_grad",
        )(gating, dq_local, *dq_parts)
        token_dq.append(exchange(dq.reshape(4, rows, width)))

    return (
        projected,
        side_by_side(jnp.concatenate(token_dq, axis=2)),
        key_grad,
        value_grad,
        jnp.concatenate(weight_rows, axis=0),
    )


def solution(mesh):
    in_specs = (
        P(("mem", "fsdp"), None),
        P(("mem", "fsdp"), None),
        P(("mem", "fsdp"), None),
        P("mem", "fsdp"),
        P("mem", "fsdp"),
        P(),
        P(),
        P("fsdp", None),
        P(("mem", "fsdp"), None),
    )
    out_specs = (
        P(("mem", "fsdp"), None),
        P(("mem", "fsdp"), None),
        P(("mem", "fsdp"), None),
        P(("mem", "fsdp"), None),
        P("fsdp", "mem"),
    )
    return jax.shard_map(
        per_device, mesh=mesh, in_specs=in_specs, out_specs=out_specs, check_vma=False
    )
```

```python
import functools

import jax
import jax.numpy as jnp
from jax import lax
from jax.experimental import pallas as pl
from jax.experimental.pallas import tpu as pltpu
from jax.sharding import PartitionSpec as P

DH = 64
QBLK = 128
MBLK = 128
LOW = -1e30
UNROLL = 4
HALVES = 1
ORDER = True
VMEM = 58 * 2**20
SCALE = DH ** (-0.5)
BF = jnp.bfloat16
F32 = jnp.float32
NT = (((1,), (1,)), ((), ()))
NN = (((1,), (0,)), ((), ()))
TN = (((0,), (0,)), ((), ()))


def dot(a, b, dims):
    return lax.dot_general(a, b, dims, preferred_element_type=F32)


def spread(x):
    zero = jnp.zeros((DH, QBLK), x.dtype)
    upper = jnp.concatenate([x[:DH], zero], axis=1)
    lower = jnp.concatenate([zero, x[DH:]], axis=1)
    return jnp.concatenate([upper, lower], axis=0)


def query_block(ref, b, t):
    per = ref.shape[2] // QBLK
    return ref[b // per, t * 128 : (t + 1) * 128, (b % per) * QBLK : (b % per + 1) * QBLK]


def folded(x, op):
    return op(x.reshape(x.shape[0] // 8, 8, x.shape[1]), axis=0)


def own_blocks(parts):
    rows = []
    for part in parts:
        rows.append(part[:DH, :QBLK])
        rows.append(part[DH:, QBLK:])
    return rows


def at_slot(slot, last, column=0):
    def index(s, b, *_):
        return (jnp.where(s == slot, b, jnp.where(s > slot, last, 0)), column, 0)

    return index


def start_step(group, half, slot, memory, buffers, sems, sides):
    rows, width = buffers[0].shape
    rows = rows // 2

    @pl.when((slot == 0) & (pl.program_id(1) == 0))
    def _():
        own = pl.ds(half * width, width)
        sources = [memory[0].at[:, own], memory[1], memory[2].at[:, own], memory[3]]
        targets = [buffers[i].at[pl.ds(j * rows, rows)] for i in range(2) for j in range(2)]
        copies = [
            pltpu.make_async_copy(source, target, sems.at[i])
            for i, (source, target) in enumerate(zip(sources, targets))
        ]
        for copy in copies:
            copy.start()
        for _, out in sides:
            out[...] = jnp.zeros_like(out)
        for copy in copies:
            copy.wait()

    for i in range(group):

        @pl.when(slot == i)
        def _():
            for refs, out in sides:
                for b in range(out.shape[0] - 1):
                    for t in range(out.shape[1]):
                        x = query_block(refs[i], b, t)
                        out[b, t, :DH, :QBLK] = x[:DH]
                        out[b, t, DH:, QBLK:] = x[DH:]


def memory_forward(
    group, pairs, half, counts, places, homes, k_own, k_par, v_own, v_par, *rest
):
    q_refs = rest[:group]
    o_refs = rest[group : 2 * group]
    exact_refs = rest[2 * group : 3 * group]
    lse_ref = rest[3 * group]
    kbuf, vbuf, q_t, scores, tops, norms, acc, sems = rest[3 * group + 1 :]
    slot = pl.program_id(0)
    number = slot * pl.num_programs(1) + pl.program_id(1)
    cap = scores.shape[0]
    blocks = q_t.shape[0] - 1
    start_step(
        group, half, slot, (k_own, k_par, v_own, v_par), (kbuf, vbuf), sems, [(q_refs, q_t)]
    )
    tops[...] = jnp.full(tops.shape, LOW, F32)
    norms[...] = jnp.zeros_like(norms)
    acc[...] = jnp.zeros_like(acc)
    turns = (counts[number] + UNROLL - 1) // UNROLL

    def first(turn, carry):
        found = []
        for u in range(UNROLL):
            j = turn * UNROLL + u
            row = pl.multiple_of(places[number * cap + j] * MBLK, MBLK)
            b = homes[number * cap + j]
            for t in range(pairs):
                cols = slice(t * 128, (t + 1) * 128)
                s = dot(kbuf[pl.ds(row, MBLK), cols], q_t[b, t], NN)
                scores[j, t] = s
                found.append((b, t, folded(s, jnp.max)))
        for b, t, top in found:
            tops[b, t] = jnp.maximum(tops[b, t], top)
        return carry

    lax.fori_loop(0, turns, first, 0)
    tops[...] = jnp.broadcast_to(jnp.max(tops[...], axis=2, keepdims=True), tops.shape)

    def second(turn, carry):
        found = []
        for u in range(UNROLL):
            j = turn * UNROLL + u
            row = pl.multiple_of(places[number * cap + j] * MBLK, MBLK)
            b = homes[number * cap + j]
            for t in range(pairs):
                cols = slice(t * 128, (t + 1) * 128)
                p = jnp.exp(scores[j, t] - tops[b, t, 0:1, :])
                o = dot(vbuf[pl.ds(row, MBLK), cols], p.astype(BF), TN)
                found.append((b, t, folded(p, jnp.sum), o))
        for b, t, norm, o in found:
            norms[b, t] += norm
            acc[b, t] += o
        return carry

    lax.fori_loop(0, turns, second, 0)
    results = []
    for b in range(blocks):
        parts = []
        for t in range(pairs):
            wide = slice(t * 256, (t + 1) * 256)
            norm = jnp.sum(norms[b, t], axis=0, keepdims=True)
            some = norm > 0.0
            safe = jnp.where(some, norm, 1.0)
            lse_ref[0, b, :, wide] = jnp.where(some, tops[b, t, 0:1, :] + jnp.log(safe), LOW)
            parts.append(acc[b, t] * (1.0 / safe))
        results.append(jnp.concatenate(own_blocks(parts), axis=0))
    for i in range(group):

        @pl.when(slot == i)
        def _():
            for b in range(blocks):
                exact_refs[i][b] = results[b]
                o_refs[i][b] = results[b].astype(BF)


def statistics_kernel(group, heads, lse_ref, *rest):
    do_refs, o_refs, stat_ref = rest[:group], rest[group : 2 * group], rest[2 * group]
    for i in range(group):
        for b in range(lse_ref.shape[1]):
            stat_ref[i, b, 0:1, :] = lse_ref[i, b]
            for t in range(heads // 2):
                do = query_block(do_refs[i], b, t).astype(F32)
                product = do * o_refs[i][b, t * 128 : (t + 1) * 128, :]
                for h in range(2):
                    at = slice((2 * t + h) * QBLK, (2 * t + h + 1) * QBLK)
                    stat_ref[i, b, 1:2, at] = jnp.sum(
                        product[h * DH : (h + 1) * DH], axis=0, keepdims=True
                    )


def merged(stat_refs, b):
    lses = [ref[0, b, 0:1, :] for ref in stat_refs]
    top = functools.reduce(jnp.maximum, lses)
    shares = [jnp.exp(x - top) for x in lses]
    norm = functools.reduce(jnp.add, shares)
    return top, shares, norm


def memory_backward(
    group, pairs, half, counts, places, homes, k_own, k_par, v_own, v_par, *rest
):
    q_refs = rest[:group]
    do_refs = rest[group : 2 * group]
    stat_refs = rest[2 * group : 3 * group]
    dq_refs = rest[3 * group : 4 * group]
    kbuf, vbuf, q_t, do_t, weights, lses, means, acc, sems = rest[4 * group :]
    slot = pl.program_id(0)
    number = slot * pl.num_programs(1) + pl.program_id(1)
    cap = places.shape[0] // counts.shape[0]
    blocks = q_t.shape[0] - 1
    start_step(
        group, half, slot, (k_own, k_par, v_own, v_par), (kbuf, vbuf), sems,
        [(q_refs, q_t), (do_refs, do_t)],
    )
    lses[...] = jnp.zeros_like(lses)
    means[...] = jnp.zeros_like(means)
    for b in range(blocks):
        top, shares, norm = merged(stat_refs, b)
        lse = top + jnp.log(norm)
        mean = functools.reduce(
            jnp.add, [x * ref[0, b, 1:2, :] for x, ref in zip(shares, stat_refs)]
        ) / norm
        for t in range(pairs):
            wide = slice(t * 256, (t + 1) * 256)
            lses[b, t] = lse[:, wide]
            means[b, t] = mean[:, wide]
    acc[...] = jnp.zeros_like(acc)

    turns = (counts[number] + UNROLL - 1) // UNROLL

    def first(turn, carry):
        for u in range(UNROLL):
            j = turn * UNROLL + u
            row = pl.multiple_of(places[number * cap + j] * MBLK, MBLK)
            b = homes[number * cap + j]
            for t in range(pairs):
                cols = slice(t * 128, (t + 1) * 128)
                s = dot(kbuf[pl.ds(row, MBLK), cols], q_t[b, t], NN)
                weights[j, t] = jnp.exp(s - lses[b, t])
        return carry

    lax.fori_loop(0, turns, first, 0)

    def second(turn, carry):
        found = []
        for u in range(UNROLL):
            j = turn * UNROLL + u
            row = pl.multiple_of(places[number * cap + j] * MBLK, MBLK)
            b = homes[number * cap + j]
            for t in range(pairs):
                cols = slice(t * 128, (t + 1) * 128)
                slope = dot(vbuf[pl.ds(row, MBLK), cols], do_t[b, t], NN)
                delta = weights[j, t] * (slope - means[b, t])
                found.append((b, t, dot(kbuf[pl.ds(row, MBLK), cols], delta.astype(BF), TN)))
        for b, t, dq in found:
            acc[b, t] += dq
        return carry

    lax.fori_loop(0, turns, second, 0)
    results = [
        jnp.concatenate(own_blocks([acc[b, t] for t in range(pairs)]), axis=0).astype(BF)
        for b in range(blocks)
    ]
    for i in range(group):

        @pl.when(slot == i)
        def _():
            for b in range(blocks):
                dq_refs[i][b] = results[b]


def local_kernel(pairs, blocks, halves, gate, q_ref, k_ref, v_ref, *rest):
    do_refs = rest[:halves]
    o_ref, dq_ref, dk_ref, dv_ref, dk_acc, dv_acc = rest[halves:]
    per_half = pairs // halves
    dk_acc[...] = jnp.zeros_like(dk_acc)
    dv_acc[...] = jnp.zeros_like(dv_acc)
    key_at = lax.broadcasted_iota(jnp.int32, (MBLK, 2 * QBLK), 0)
    query_at = lax.broadcasted_iota(jnp.int32, (MBLK, 2 * QBLK), 1) % QBLK
    causal = key_at <= query_at
    lane = lax.broadcasted_iota(jnp.int32, (1, 128), 1)
    shares = []
    for t in range(pairs):
        shares.append(jnp.where(lane < DH, 1.0 - gate[2 * t], 1.0 - gate[2 * t + 1]))
    for t in range(pairs):
        cols = slice(t * 128, (t + 1) * 128)
        for b in range(blocks):
            q = spread(query_block(q_ref, b, t))
            do = spread(query_block(do_refs[t // per_half], b, t % per_half))
            scores, slopes = [], []
            for n in range(b + 1):
                rows = slice(n * MBLK, (n + 1) * MBLK)
                s = dot(k_ref[rows, cols], q, NN)
                scores.append(jnp.where(causal, s, LOW) if n == b else s)
                slopes.append(dot(v_ref[rows, cols], do, NN))
            largest = functools.reduce(jnp.maximum, [folded(s, jnp.max) for s in scores])
            largest = jnp.max(largest, axis=0, keepdims=True)
            weights = [jnp.exp(s - largest) for s in scores]
            norm = functools.reduce(jnp.add, [folded(p, jnp.sum) for p in weights])
            inverse = 1.0 / jnp.sum(norm, axis=0, keepdims=True)
            weights = [p * inverse for p in weights]
            mean = functools.reduce(
                jnp.add, [folded(p * x, jnp.sum) for p, x in zip(weights, slopes)]
            )
            mean = jnp.sum(mean, axis=0, keepdims=True)
            o = jnp.zeros((128, 256), F32)
            dq = jnp.zeros((128, 256), F32)
            for n in range(b + 1):
                rows = slice(n * MBLK, (n + 1) * MBLK)
                w = weights[n].astype(BF)
                delta = (weights[n] * (slopes[n] - mean)).astype(BF)
                o += dot(v_ref[rows, cols], w, TN)
                dq += dot(k_ref[rows, cols], delta, TN)
                dv_acc[rows, cols] += dot(w, do, NT)
                dk_acc[rows, cols] += dot(delta, q, NT)
            o_pair, dq_pair = own_blocks([o]), own_blocks([dq])
            for i in range(2):
                share = 1.0 - gate[2 * t + i]
                at = slice((2 * t + i) * DH, (2 * t + i + 1) * DH)
                o_ref[b, at, :] = o_pair[i] * share
                dq_ref[b, at, :] = dq_pair[i] * (share * SCALE)
        dk_ref[:, cols] = (dk_acc[:, cols] * shares[t]).astype(BF)
        dv_ref[:, cols] = (dv_acc[:, cols] * shares[t]).astype(BF)


def attention_kernel(group, heads, first, gate, local_ref, *rest):
    o_refs = rest[:group]
    stat_refs = rest[group : 2 * group]
    out_ref, out_t_ref = rest[2 * group :]
    for b in range(local_ref.shape[0]):
        _, shares, norm = merged(stat_refs, b)
        rows = []
        for h in range(heads):
            at = slice(h * DH, (h + 1) * DH)
            wide = slice(h * QBLK, (h + 1) * QBLK)
            total = functools.reduce(
                jnp.add,
                [x[:, wide] * ref[b, at, :].astype(F32) for x, ref in zip(shares, o_refs)],
            )
            rows.append(total * (gate[first + h] / norm[:, wide]) + local_ref[b, at, :])
        result = jnp.concatenate(rows, axis=0).astype(BF)
        out_t_ref[:, b * QBLK : (b + 1) * QBLK] = result
        out_ref[b * QBLK : (b + 1) * QBLK, :] = result.T


def query_grad_kernel(group, heads, first, gate, local_ref, *rest):
    dq_refs = rest[:group]
    out_ref = rest[group]
    for b in range(local_ref.shape[0]):
        rows = []
        for h in range(heads):
            at = slice(h * DH, (h + 1) * DH)
            total = functools.reduce(jnp.add, [ref[b, at, :].astype(F32) for ref in dq_refs])
            rows.append(total * (gate[first + h] * SCALE) + local_ref[b, at, :])
        result = jnp.concatenate(rows, axis=0).astype(BF)
        out_ref[b * QBLK : (b + 1) * QBLK, :] = result.T


def attention_grad_kernel(order, weight_ref, *rest):
    part_refs, out_refs = rest[:4], rest[4:]
    for i in range(4):
        grad = dot(weight_ref[...], part_refs[i][...], NT).astype(BF)
        rows = grad.shape[0] // len(out_refs)
        for j, out_ref in enumerate(out_refs):
            out_ref[order[i]] = grad[j * rows : (j + 1) * rows]


def weight_grad_kernel(order, dests, attention_ref, *rest):
    part_refs, (send_ref, keep_ref) = rest[:4], rest[4:]
    tokens = part_refs[0].shape[0]
    columns = part_refs[0].shape[1] // 2
    total = None
    for i in range(4):
        at = pl.multiple_of(order[i] * tokens, tokens)
        term = dot(attention_ref[:, pl.ds(at, tokens)], part_refs[i][...], NN)
        total = term if total is None else total + term
    total = total.astype(BF)
    side = dests[dests.shape[0] - 1]

    @pl.when(side == 0)
    def _():
        keep_ref[0] = total[:, :columns]
        send_ref[0] = total[:, columns:]

    @pl.when(side == 1)
    def _():
        keep_ref[0] = total[:, columns:]
        send_ref[0] = total[:, :columns]


ANY = pl.BlockSpec(memory_space=pl.ANY)
SMEM = pl.BlockSpec(memory_space=pltpu.SMEM)


def block_lists(block_ids, me, group, seg_dev, per_dev, cap):
    segments, per_seg, retr = block_ids.shape
    asked = per_seg * retr
    z = me // 2
    ids = block_ids.reshape(segments // (2 * seg_dev), 2, seg_dev, asked)
    ids = lax.dynamic_index_in_dim(ids, me % 2, 1, keepdims=False)
    slots = (z - jnp.arange(group, dtype=jnp.int32)) % group
    ids = jnp.take(ids, slots, axis=0).reshape(group * seg_dev, asked)
    owners = ids // per_dev
    here = owners // 2 == z
    place = ids - owners * per_dev + jnp.where(owners == me, 0, per_dev)
    position = jnp.arange(asked, dtype=jnp.int32)
    before = (position[None, :] < position[:, None])[None]
    rank = jnp.sum(jnp.logical_and(before, here[:, None, :]), axis=-1)
    chosen = jnp.logical_and(
        here[:, :, None], rank[:, :, None] == jnp.arange(cap, dtype=jnp.int32)
    )
    places = jnp.sum(jnp.where(chosen, place[:, :, None], 0), axis=1)
    home = position // retr - per_seg
    homes = per_seg + jnp.sum(jnp.where(chosen, home[None, :, None], 0), axis=1)
    counts = jnp.sum(here, axis=-1)
    return (
        counts.astype(jnp.int32),
        places.astype(jnp.int32).reshape(-1),
        homes.astype(jnp.int32).reshape(-1),
    )


def side_by_side(x):
    parts, rows, width = x.shape
    return x.transpose(1, 0, 2).reshape(rows, parts * width)


def gather_tokens(x):
    far = lax.ppermute(x, "fsdp", [(i, i ^ 2) for i in range(4)])
    near = lax.ppermute(x, "fsdp", [(i, i ^ 1) for i in range(4)])
    both = lax.ppermute(far, "fsdp", [(i, i ^ 1) for i in range(4)])
    return [x, near, far, both]


def weight_grad_plain(attention, parts, order):
    n = lax.axis_size("mem")
    rows = parts[0].shape[0]
    total = 0.0
    for i, part in enumerate(parts):
        own = lax.dynamic_slice_in_dim(attention, order[i] * rows, rows, 0)
        total = total + dot(own, part, TN)
    pieces = total.astype(BF).reshape(total.shape[0], n, -1).transpose(1, 0, 2)
    pieces = lax.all_to_all(pieces, "mem", split_axis=0, concat_axis=0, tiled=True)
    return jnp.sum(pieces.astype(F32), axis=0)


def cost(us):
    return pl.CostEstimate(flops=us * 10**9, bytes_accessed=us * 10**6, transcendentals=0)


def after(first, *rest):
    return lax.optimization_barrier((first, *rest))[1:]


def per_device(
    queries, keys, values, mem_keys, mem_values, block_ids, gate_bias, out_weight, cotangent
):
    n = lax.axis_size("mem")
    me = lax.axis_index("mem")
    fs = lax.axis_index("fsdp")
    group = n // 2
    full = mem_keys.shape[1]
    all_heads = full // DH
    width = full // HALVES
    heads = width // DH
    pairs = heads // 2
    segments, per_seg, retr = block_ids.shape
    seg_dev = segments // n
    per_dev = mem_keys.shape[0] // MBLK
    blocks = seg_dev * per_seg
    tokens = blocks * QBLK
    seg_len = per_seg * QBLK
    rows = queries.shape[0]
    seg_rows = seg_len // rows
    gating = jax.nn.sigmoid(lax.dynamic_slice_in_dim(gate_bias, fs * all_heads, all_heads))
    halves = range(HALVES)

    def shifted(x, k):
        return lax.ppermute(x, "mem", [(i, (i + 2 * k) % n) for i in range(n)])

    def exchange(x):
        return lax.all_to_all(x, "fsdp", split_axis=0, concat_axis=0, tiled=True)

    swap = [(i, i ^ 1) for i in range(n)]
    cap = -(-4 * max(1, retr * per_seg // n) // UNROLL) * UNROLL
    lists = block_lists(block_ids, me, group, seg_dev, per_dev, cap)

    par_keys = [lax.ppermute(mem_keys, "mem", swap)]
    par_values = [lax.ppermute(mem_values, "mem", swap)]

    q = exchange((queries * BF(SCALE)).T.reshape(4, full, rows))
    q_slots = [q] + [shifted(q, k) for k in range(1, group)]
    (cotangent,) = after(q, cotangent)
    cot_parts = gather_tokens(cotangent)
    keys, values = after(q, keys, values)
    k, v = (
        exchange(x.reshape(rows, 4, full).transpose(1, 0, 2)).reshape(tokens, full)
        for x in (keys, values)
    )
    cot_parts = after((q_slots, k, v), *cot_parts)
    order = fs ^ jnp.arange(4, dtype=jnp.int32)
    whole = pl.BlockSpec(memory_space=pltpu.VMEM)
    do_parts = pl.pallas_call(
        attention_grad_kernel,
        in_specs=[SMEM] + [whole] * 5,
        out_specs=[whole] * HALVES,
        out_shape=[jax.ShapeDtypeStruct((4, width, rows), BF)] * HALVES,
        compiler_params=pltpu.CompilerParams(vmem_limit_bytes=VMEM),
        cost_estimate=cost(1),
            name="attention_grad",
    )(order, out_weight, *cot_parts)
    do_slots = [[x] + [shifted(x, k) for k in range(1, group)] for x in do_parts]
    (late_weight,) = after(v, out_weight)
    full_weight = lax.all_gather(late_weight, "fsdp", axis=0, tiled=True)

    seg_spec = pl.BlockSpec((seg_len, full), lambda s: (s, 0))
    q_spec = pl.BlockSpec((seg_rows, full, rows), lambda s: (s, 0, 0))
    do_spec = pl.BlockSpec((seg_rows, width, rows), lambda s: (s, 0, 0))
    part_spec = pl.BlockSpec((per_seg, full, QBLK), lambda s: (s, 0, 0))
    part_shape = jax.ShapeDtypeStruct((blocks, full, QBLK), F32)
    head_shape = jax.ShapeDtypeStruct((tokens, full), BF)
    o_local, dq_local, dk, dv = pl.pallas_call(
        functools.partial(local_kernel, all_heads // 2, per_seg, HALVES),
        grid=(seg_dev,),
        in_specs=[SMEM, q_spec, seg_spec, seg_spec] + [do_spec] * HALVES,
        out_specs=[part_spec, part_spec, seg_spec, seg_spec],
        out_shape=[part_shape, part_shape, head_shape, head_shape],
        scratch_shapes=[pltpu.VMEM((seg_len, full), F32)] * 2,
        compiler_params=pltpu.CompilerParams(vmem_limit_bytes=VMEM),
        cost_estimate=cost(1),
            name="local",
    )(gating, q, k, v, *do_parts)

    lists = after((o_local, dk), *lists)
    t_specs = [
        pl.BlockSpec((per_seg, width, QBLK), at_slot(i, seg_dev - 1)) for i in range(group)
    ]
    t_shape = jax.ShapeDtypeStruct((blocks, width, QBLK), BF)
    stat_block = (1, per_seg, 2, heads * QBLK)
    memory_rows = 2 * mem_keys.shape[0]
    scratch = [pltpu.VMEM((memory_rows, width), BF)] * 2
    scratch += [pltpu.VMEM((per_seg + 1, pairs, 128, 256), BF)] * 2
    scratch += [pltpu.VMEM((cap, pairs, MBLK, 256), F32)]
    acc = pltpu.VMEM((per_seg + 1, pairs, 128, 256), F32)
    rows8 = pltpu.VMEM((per_seg + 1, pairs, 8, 256), F32)
    rows1 = pltpu.VMEM((per_seg + 1, pairs, 1, 256), F32)
    sems = pltpu.SemaphoreType.DMA((4,))
    limit = pltpu.CompilerParams(vmem_limit_bytes=VMEM)
    stat_specs = [
        pl.BlockSpec(stat_block, lambda s, b, *_, k=k: ((s - k) % group, b, 0, 0))
        for k in range(group)
    ]

    def slot_specs(half):
        return [
            pl.BlockSpec((seg_rows, width, rows), at_slot(i, seg_dev - 1, half))
            for i in range(group)
        ]

    o_home, stat_slots = [], []
    spreads = [pltpu.VMEM((per_seg + 1, pairs, 128, 256), BF)]
    for i in halves:
        outs = pl.pallas_call(
            functools.partial(memory_forward, group, pairs, i),
            grid_spec=pltpu.PrefetchScalarGridSpec(
                num_scalar_prefetch=3,
                grid=(group, seg_dev),
                in_specs=[ANY] * 4 + slot_specs(i),
                out_specs=t_specs
                + t_specs
                + [
                    pl.BlockSpec(
                        (1, per_seg, 1, heads * QBLK), lambda s, b, *_: (s, b, 0, 0)
                    )
                ],
                scratch_shapes=scratch[:2] + spreads + scratch[-1:] + [rows8, rows8, acc, sems],
            ),
            out_shape=[t_shape] * group
            + [jax.ShapeDtypeStruct(t_shape.shape, F32)] * group
            + [jax.ShapeDtypeStruct((group, blocks, 1, heads * QBLK), F32)],
            compiler_params=limit,
            cost_estimate=cost(30),
            name="memory_forward",
        )(*lists, mem_keys, par_keys[i], mem_values, par_values[i], *q_slots)
        o_slots, exact, lse = list(outs[:group]), outs[group : 2 * group], outs[-1]
        stats = pl.pallas_call(
            functools.partial(statistics_kernel, group, heads),
            grid=(seg_dev,),
            in_specs=[
                pl.BlockSpec((group, per_seg, 1, heads * QBLK), lambda s: (0, s, 0, 0))
            ]
            + [pl.BlockSpec((seg_rows, width, rows), lambda s: (s, 0, 0))] * group
            + [pl.BlockSpec((per_seg, width, QBLK), lambda s: (s, 0, 0))] * group,
            out_specs=pl.BlockSpec(
                (group, per_seg, 2, heads * QBLK), lambda s: (0, s, 0, 0)
            ),
            out_shape=jax.ShapeDtypeStruct((group, blocks, 2, heads * QBLK), F32),
            compiler_params=limit,
            cost_estimate=cost(5),
            name="statistics",
        )(lse, *do_slots[i], *exact)
        stat_slots.append([stats] + [shifted(stats, k) for k in range(1, group)])
        if ORDER:
            middle = range(2, group - 1)
            held = after(stat_slots[-1], *[o_slots[j] for j in middle])
            for j, x in zip(middle, held):
                o_slots[j] = x
        o_home.append([o_slots[0]] + [shifted(o_slots[k], -k) for k in range(1, group)])

    last = stat_slots[-1][0]
    dq_home = []
    for i in halves:
        first_stats = after(last, *stat_slots[i])
        dq_slots = pl.pallas_call(
            functools.partial(memory_backward, group, pairs, i),
            grid_spec=pltpu.PrefetchScalarGridSpec(
                num_scalar_prefetch=3,
                grid=(group, seg_dev),
                in_specs=[ANY] * 4 + slot_specs(i) + slot_specs(0) + stat_specs,
                out_specs=t_specs,
                scratch_shapes=scratch + [rows1, rows1, acc, sems],
            ),
            out_shape=[t_shape] * group,
            compiler_params=limit,
            cost_estimate=cost(30),
            name="memory_backward",
        )(
            *lists, mem_keys, par_keys[i], mem_values, par_values[i],
            *q_slots, *do_slots[i], *first_stats,
        )
        last = dq_slots[0]
        dq_home.append([dq_slots[0]] + [shifted(dq_slots[k], -k) for k in range(1, group)])

    dk, dv = after(last, dk, dv)
    key_grad, value_grad = [side_by_side(exchange(x.reshape(4, rows, full))) for x in (dk, dv)]
    home_spec = pl.BlockSpec((per_seg, width, QBLK), lambda b: (b, 0, 0))
    home_out = pl.BlockSpec((seg_len, width), lambda b: (b, 0))
    home_shape = jax.ShapeDtypeStruct((tokens, width), BF)
    home_specs = [
        pl.BlockSpec(stat_block, lambda b, k=k: (k, b, 0, 0)) for k in range(group)
    ]
    columns = out_weight.shape[1] // n
    steps = jnp.arange(group, dtype=jnp.int32)
    dests = jnp.concatenate([(me // 2 - steps) % group, (me % 2)[None]]).astype(jnp.int32)
    token_attention, weight_rows, token_dq = [], [], []
    for i in halves:
        local_spec = pl.BlockSpec((per_seg, width, QBLK), lambda b, i=i: (b, i, 0))
        home_stats = [stat_slots[i][(group - k) % group] for k in range(group)]
        o_parts = after(last, *o_home[i])
        attention, attention_t = pl.pallas_call(
            functools.partial(attention_kernel, group, heads, i * heads),
            grid=(seg_dev,),
            in_specs=[SMEM, local_spec] + [home_spec] * group + home_specs,
            out_specs=[home_out, pl.BlockSpec((width, seg_len), lambda b: (0, b))],
            out_shape=[home_shape, jax.ShapeDtypeStruct((width, tokens), BF)],
            compiler_params=limit,
            cost_estimate=cost(3),
            name="attention",
        )(gating, o_local, *o_parts, *home_stats)
        token_attention.append(exchange(attention.reshape(4, rows, width)))
        if columns % 128:
            weight_rows.append(weight_grad_plain(attention, cot_parts, order))
            continue
        piece = (1, width, columns)
        send, keep = pl.pallas_call(
            weight_grad_kernel,
            grid_spec=pltpu.PrefetchScalarGridSpec(
                num_scalar_prefetch=2,
                grid=(group,),
                in_specs=[pl.BlockSpec((width, tokens), lambda k, *_: (0, 0))]
                + [pl.BlockSpec((rows, 2 * columns), lambda k, _, to: (0, to[k]))] * 4,
                out_specs=[pl.BlockSpec(piece, lambda k, *_: (k, 0, 0))] * 2,
            ),
            out_shape=[jax.ShapeDtypeStruct((group, width, columns), BF)] * 2,
            compiler_params=limit,
            cost_estimate=cost(5),
            name="weight_grad",
        )(order, dests, attention_t, *cot_parts)
        got = lax.ppermute(send, "mem", swap)
        sums = [
            (keep[k].astype(F32) + got[k].astype(F32)).astype(BF) for k in range(group)
        ]
        sums = [sums[0]] + [shifted(sums[k], -k) for k in range(1, group)]
        weight_rows.append(functools.reduce(jnp.add, [x.astype(F32) for x in sums]))
    projected = jnp.einsum(
        "stc,scd->td",
        jnp.concatenate(token_attention, axis=2),
        full_weight.reshape(4, full, -1),
        preferred_element_type=F32,
    ).astype(BF)
    for i in halves:
        dq_parts = after(projected, *dq_home[i])
        local_spec = pl.BlockSpec((per_seg, width, QBLK), lambda b, i=i: (b, i, 0))
        dq = pl.pallas_call(
            functools.partial(query_grad_kernel, group, heads, i * heads),
            grid=(seg_dev,),
            in_specs=[SMEM, local_spec] + [home_spec] * group,
            out_specs=home_out,
            out_shape=home_shape,
            compiler_params=limit,
            cost_estimate=cost(3),
            name="query_grad",
        )(gating, dq_local, *dq_parts)
        token_dq.append(exchange(dq.reshape(4, rows, width)))

    return (
        projected,
        side_by_side(jnp.concatenate(token_dq, axis=2)),
        key_grad,
        value_grad,
        jnp.concatenate(weight_rows, axis=0),
    )


def solution(mesh):
    in_specs = (
        P(("mem", "fsdp"), None),
        P(("mem", "fsdp"), None),
        P(("mem", "fsdp"), None),
        P("mem", "fsdp"),
        P("mem", "fsdp"),
        P(),
        P(),
        P("fsdp", None),
        P(("mem", "fsdp"), None),
    )
    out_specs = (
        P(("mem", "fsdp"), None),
        P(("mem", "fsdp"), None),
        P(("mem", "fsdp"), None),
        P(("mem", "fsdp"), None),
        P("fsdp", "mem"),
    )
    return jax.shard_map(
        per_device, mesh=mesh, in_specs=in_specs, out_specs=out_specs, check_vma=False
    )
```

```python
import functools

import jax
import jax.numpy as jnp
from jax import lax
from jax.experimental import pallas as pl
from jax.experimental.pallas import tpu as pltpu
from jax.sharding import PartitionSpec as P

DH = 64
QBLK = 128
MBLK = 128
LOW = -1e30
UNROLL = 4
HALVES = 1
ORDER = False
VMEM = 58 * 2**20
SCALE = DH ** (-0.5)
BF = jnp.bfloat16
F32 = jnp.float32
NT = (((1,), (1,)), ((), ()))
NN = (((1,), (0,)), ((), ()))
TN = (((0,), (0,)), ((), ()))


def dot(a, b, dims):
    return lax.dot_general(a, b, dims, preferred_element_type=F32)


def spread(x):
    zero = jnp.zeros((DH, QBLK), x.dtype)
    upper = jnp.concatenate([x[:DH], zero], axis=1)
    lower = jnp.concatenate([zero, x[DH:]], axis=1)
    return jnp.concatenate([upper, lower], axis=0)


def query_block(ref, b, t):
    per = ref.shape[2] // QBLK
    return ref[b // per, t * 128 : (t + 1) * 128, (b % per) * QBLK : (b % per + 1) * QBLK]


def folded(x, op):
    return op(x.reshape(x.shape[0] // 8, 8, x.shape[1]), axis=0)


def own_blocks(parts):
    rows = []
    for part in parts:
        rows.append(part[:DH, :QBLK])
        rows.append(part[DH:, QBLK:])
    return rows


def at_slot(slot, last, column=0):
    def index(s, b, *_):
        return (jnp.where(s == slot, b, jnp.where(s > slot, last, 0)), column, 0)

    return index


def start_step(group, half, slot, memory, buffers, sems, sides):
    rows, width = buffers[0].shape
    rows = rows // 2
    own = pl.ds(half * width, width)
    sources = [memory[0].at[:, own], memory[1], memory[2].at[:, own], memory[3]]
    targets = [buffers[i].at[pl.ds(j * rows, rows)] for i in range(2) for j in range(2)]
    copies = [
        pltpu.make_async_copy(source, target, sems.at[i])
        for i, (source, target) in enumerate(zip(sources, targets))
    ]
    begins = (slot == 0) & (pl.program_id(1) == 0)

    @pl.when(begins)
    def _():
        for copy in copies:
            copy.start()
        for _, out in sides:
            out[...] = jnp.zeros_like(out)
        for copy in copies[:2]:
            copy.wait()

    def wait_values():
        @pl.when(begins)
        def _():
            for copy in copies[2:]:
                copy.wait()

    for i in range(group):

        @pl.when(slot == i)
        def _():
            for refs, out in sides:
                for b in range(out.shape[0] - 1):
                    for t in range(out.shape[1]):
                        x = query_block(refs[i], b, t)
                        out[b, t, :DH, :QBLK] = x[:DH]
                        out[b, t, DH:, QBLK:] = x[DH:]
    return wait_values


def memory_forward(
    group, pairs, half, counts, places, homes, k_own, k_par, v_own, v_par, *rest
):
    q_refs = rest[:group]
    o_refs = rest[group : 2 * group]
    exact_ref, lse_ref = rest[2 * group : 2 * group + 2]
    kbuf, vbuf, q_t, scores, tops, norms, acc, sems = rest[2 * group + 2 :]
    slot = pl.program_id(0)
    number = slot * pl.num_programs(1) + pl.program_id(1)
    cap = scores.shape[0]
    blocks = q_t.shape[0] - 1
    wait_values = start_step(
        group, half, slot, (k_own, k_par, v_own, v_par), (kbuf, vbuf), sems, [(q_refs, q_t)]
    )
    tops[...] = jnp.full(tops.shape, LOW, F32)
    norms[...] = jnp.zeros_like(norms)
    acc[...] = jnp.zeros_like(acc)
    turns = (counts[number] + UNROLL - 1) // UNROLL

    def first(turn, carry):
        found = []
        for u in range(UNROLL):
            j = turn * UNROLL + u
            row = pl.multiple_of(places[number * cap + j] * MBLK, MBLK)
            b = homes[number * cap + j]
            for t in range(pairs):
                cols = slice(t * 128, (t + 1) * 128)
                s = dot(kbuf[pl.ds(row, MBLK), cols], q_t[b, t], NN)
                scores[j, t] = s
                found.append((b, t, folded(s, jnp.max)))
        for b, t, top in found:
            tops[b, t] = jnp.maximum(tops[b, t], top)
        return carry

    lax.fori_loop(0, turns, first, 0)
    wait_values()
    tops[...] = jnp.broadcast_to(jnp.max(tops[...], axis=2, keepdims=True), tops.shape)

    def second(turn, carry):
        found = []
        for u in range(UNROLL):
            j = turn * UNROLL + u
            row = pl.multiple_of(places[number * cap + j] * MBLK, MBLK)
            b = homes[number * cap + j]
            for t in range(pairs):
                cols = slice(t * 128, (t + 1) * 128)
                p = jnp.exp(scores[j, t] - tops[b, t, 0:1, :])
                o = dot(vbuf[pl.ds(row, MBLK), cols], p.astype(BF), TN)
                found.append((b, t, folded(p, jnp.sum), o))
        for b, t, norm, o in found:
            norms[b, t] += norm
            acc[b, t] += o
        return carry

    lax.fori_loop(0, turns, second, 0)
    results = []
    for b in range(blocks):
        parts = []
        for t in range(pairs):
            wide = slice(t * 256, (t + 1) * 256)
            norm = jnp.sum(norms[b, t], axis=0, keepdims=True)
            some = norm > 0.0
            safe = jnp.where(some, norm, 1.0)
            lse_ref[0, b, :, wide] = jnp.where(some, tops[b, t, 0:1, :] + jnp.log(safe), LOW)
            parts.append(acc[b, t] * (1.0 / safe))
        results.append(jnp.concatenate(own_blocks(parts), axis=0))
        exact_ref[0, b] = results[b]
    for i in range(group):

        @pl.when(slot == i)
        def _():
            for b in range(blocks):
                o_refs[i][b] = results[b].astype(BF)


def statistics_kernel(group, heads, lse_ref, *rest):
    do_refs, (o_ref, stat_ref) = rest[:group], rest[group:]
    for i in range(group):
        for b in range(lse_ref.shape[1]):
            stat_ref[i, b, 0:1, :] = lse_ref[i, b]
            for t in range(heads // 2):
                do = query_block(do_refs[i], b, t).astype(F32)
                product = do * o_ref[i, b, t * 128 : (t + 1) * 128, :]
                for h in range(2):
                    at = slice((2 * t + h) * QBLK, (2 * t + h + 1) * QBLK)
                    stat_ref[i, b, 1:2, at] = jnp.sum(
                        product[h * DH : (h + 1) * DH], axis=0, keepdims=True
                    )


def merged(stat_refs, b):
    lses = [ref[0, b, 0:1, :] for ref in stat_refs]
    top = functools.reduce(jnp.maximum, lses)
    shares = [jnp.exp(x - top) for x in lses]
    norm = functools.reduce(jnp.add, shares)
    return top, shares, norm


def memory_backward(
    group, pairs, half, counts, places, homes, k_own, k_par, v_own, v_par, *rest
):
    q_refs = rest[:group]
    do_refs = rest[group : 2 * group]
    stat_ref = rest[2 * group]
    delta_ref, key_ref = rest[2 * group + 1 : 2 * group + 3]
    kbuf, vbuf, q_t, do_t, weights, lses, means, acc, acc_keys, sems = rest[2 * group + 3 :]
    slot = pl.program_id(0)
    number = slot * pl.num_programs(1) + pl.program_id(1)
    cap = places.shape[0] // counts.shape[0]
    blocks = q_t.shape[0] - 1
    wait_values = start_step(
        group, half, slot, (k_own, k_par, v_own, v_par), (kbuf, vbuf), sems,
        [(q_refs, q_t), (do_refs, do_t)],
    )
    lses[...] = jnp.zeros_like(lses)
    means[...] = jnp.zeros_like(means)
    for b in range(blocks):
        for t in range(pairs):
            wide = slice(t * 256, (t + 1) * 256)
            lses[b, t] = stat_ref[0, b, 0:1, wide]
            means[b, t] = stat_ref[0, b, 1:2, wide]
    acc[...] = jnp.zeros_like(acc)
    acc_keys[...] = jnp.zeros_like(acc_keys)
    turns = (counts[number] + UNROLL - 1) // UNROLL

    def first(turn, carry):
        found = []
        for u in range(UNROLL):
            j = turn * UNROLL + u
            row = pl.multiple_of(places[number * cap + j] * MBLK, MBLK)
            b = homes[number * cap + j]
            for t in range(pairs):
                cols = slice(t * 128, (t + 1) * 128)
                keys = kbuf[pl.ds(row, MBLK), cols]
                p = jnp.exp(dot(keys, q_t[b, t], NN) - lses[b, t])
                weights[j, t] = p
                found.append((b, t, dot(keys, p.astype(BF), TN)))
        for b, t, sums in found:
            acc_keys[b, t] += sums
        return carry

    lax.fori_loop(0, turns, first, 0)
    wait_values()

    def second(turn, carry):
        found = []
        for u in range(UNROLL):
            j = turn * UNROLL + u
            row = pl.multiple_of(places[number * cap + j] * MBLK, MBLK)
            b = homes[number * cap + j]
            for t in range(pairs):
                cols = slice(t * 128, (t + 1) * 128)
                slope = dot(vbuf[pl.ds(row, MBLK), cols], do_t[b, t], NN)
                delta = weights[j, t] * (slope - means[b, t])
                found.append((b, t, dot(kbuf[pl.ds(row, MBLK), cols], delta.astype(BF), TN)))
        for b, t, sums in found:
            acc[b, t] += sums
        return carry

    lax.fori_loop(0, turns, second, 0)
    for b in range(blocks):
        for out_ref, total in ((delta_ref, acc), (key_ref, acc_keys)):
            parts = own_blocks([total[b, t] for t in range(pairs)])
            out_ref[0, b] = jnp.concatenate(parts, axis=0)


def combine_kernel(group, heads, *rest):
    stat_refs = rest[:group]
    delta_ref, key_ref = rest[group : group + 2]
    dq_refs = rest[group + 2 :]
    for i in range(group):
        for b in range(dq_refs[i].shape[0]):
            rows = [ref[(i - j) % group, b] for j, ref in enumerate(stat_refs)]
            top = functools.reduce(jnp.maximum, [x[0:1] for x in rows])
            shares = [jnp.exp(x[0:1] - top) for x in rows]
            norm = functools.reduce(jnp.add, shares)
            mean = functools.reduce(jnp.add, [p * x[1:2] for p, x in zip(shares, rows)]) / norm
            share = shares[0] / norm
            moved = share * (rows[0][1:2] - mean)
            for h in range(heads):
                at = slice(h * DH, (h + 1) * DH)
                wide = slice(h * QBLK, (h + 1) * QBLK)
                dq_refs[i][b, at, :] = (
                    delta_ref[i, b, at, :] * share[:, wide]
                    + key_ref[i, b, at, :] * moved[:, wide]
                ).astype(BF)


def local_kernel(pairs, blocks, halves, gate, q_ref, k_ref, v_ref, *rest):
    do_refs = rest[:halves]
    o_ref, dq_ref, dk_ref, dv_ref, dk_acc, dv_acc = rest[halves:]
    per_half = pairs // halves
    dk_acc[...] = jnp.zeros_like(dk_acc)
    dv_acc[...] = jnp.zeros_like(dv_acc)
    key_at = lax.broadcasted_iota(jnp.int32, (MBLK, 2 * QBLK), 0)
    query_at = lax.broadcasted_iota(jnp.int32, (MBLK, 2 * QBLK), 1) % QBLK
    causal = key_at <= query_at
    lane = lax.broadcasted_iota(jnp.int32, (1, 128), 1)
    shares = []
    for t in range(pairs):
        shares.append(jnp.where(lane < DH, 1.0 - gate[2 * t], 1.0 - gate[2 * t + 1]))
    for t in range(pairs):
        cols = slice(t * 128, (t + 1) * 128)
        for b in range(blocks):
            q = spread(query_block(q_ref, b, t))
            do = spread(query_block(do_refs[t // per_half], b, t % per_half))
            scores, slopes = [], []
            for n in range(b + 1):
                rows = slice(n * MBLK, (n + 1) * MBLK)
                s = dot(k_ref[rows, cols], q, NN)
                scores.append(jnp.where(causal, s, LOW) if n == b else s)
                slopes.append(dot(v_ref[rows, cols], do, NN))
            largest = functools.reduce(jnp.maximum, [folded(s, jnp.max) for s in scores])
            largest = jnp.max(largest, axis=0, keepdims=True)
            weights = [jnp.exp(s - largest) for s in scores]
            norm = functools.reduce(jnp.add, [folded(p, jnp.sum) for p in weights])
            inverse = 1.0 / jnp.sum(norm, axis=0, keepdims=True)
            weights = [p * inverse for p in weights]
            mean = functools.reduce(
                jnp.add, [folded(p * x, jnp.sum) for p, x in zip(weights, slopes)]
            )
            mean = jnp.sum(mean, axis=0, keepdims=True)
            o = jnp.zeros((128, 256), F32)
            dq = jnp.zeros((128, 256), F32)
            for n in range(b + 1):
                rows = slice(n * MBLK, (n + 1) * MBLK)
                w = weights[n].astype(BF)
                delta = (weights[n] * (slopes[n] - mean)).astype(BF)
                o += dot(v_ref[rows, cols], w, TN)
                dq += dot(k_ref[rows, cols], delta, TN)
                dv_acc[rows, cols] += dot(w, do, NT)
                dk_acc[rows, cols] += dot(delta, q, NT)
            o_pair, dq_pair = own_blocks([o]), own_blocks([dq])
            for i in range(2):
                share = 1.0 - gate[2 * t + i]
                at = slice((2 * t + i) * DH, (2 * t + i + 1) * DH)
                o_ref[b, at, :] = o_pair[i] * share
                dq_ref[b, at, :] = dq_pair[i] * (share * SCALE)
        dk_ref[:, cols] = (dk_acc[:, cols] * shares[t]).astype(BF)
        dv_ref[:, cols] = (dv_acc[:, cols] * shares[t]).astype(BF)


def attention_kernel(group, heads, first, gate, local_ref, *rest):
    o_refs = rest[:group]
    stat_refs = rest[group : 2 * group]
    out_ref, out_t_ref = rest[2 * group :]
    for b in range(local_ref.shape[0]):
        _, shares, norm = merged(stat_refs, b)
        rows = []
        for h in range(heads):
            at = slice(h * DH, (h + 1) * DH)
            wide = slice(h * QBLK, (h + 1) * QBLK)
            total = functools.reduce(
                jnp.add,
                [x[:, wide] * ref[b, at, :].astype(F32) for x, ref in zip(shares, o_refs)],
            )
            rows.append(total * (gate[first + h] / norm[:, wide]) + local_ref[b, at, :])
        result = jnp.concatenate(rows, axis=0).astype(BF)
        out_t_ref[:, b * QBLK : (b + 1) * QBLK] = result
        out_ref[b * QBLK : (b + 1) * QBLK, :] = result.T


def query_grad_kernel(group, heads, first, gate, local_ref, *rest):
    dq_refs = rest[:group]
    out_ref = rest[group]
    for b in range(local_ref.shape[0]):
        rows = []
        for h in range(heads):
            at = slice(h * DH, (h + 1) * DH)
            total = functools.reduce(jnp.add, [ref[b, at, :].astype(F32) for ref in dq_refs])
            rows.append(total * (gate[first + h] * SCALE) + local_ref[b, at, :])
        result = jnp.concatenate(rows, axis=0).astype(BF)
        out_ref[b * QBLK : (b + 1) * QBLK, :] = result.T


def attention_grad_kernel(order, weight_ref, *rest):
    part_refs, out_refs = rest[:4], rest[4:]
    for i in range(4):
        grad = dot(weight_ref[...], part_refs[i][...], NT).astype(BF)
        rows = grad.shape[0] // len(out_refs)
        for j, out_ref in enumerate(out_refs):
            out_ref[order[i]] = grad[j * rows : (j + 1) * rows]


def weight_grad_kernel(order, dests, attention_ref, *rest):
    part_refs, (send_ref, keep_ref) = rest[:4], rest[4:]
    tokens = part_refs[0].shape[0]
    columns = part_refs[0].shape[1] // 2
    total = None
    for i in range(4):
        at = pl.multiple_of(order[i] * tokens, tokens)
        term = dot(attention_ref[:, pl.ds(at, tokens)], part_refs[i][...], NN)
        total = term if total is None else total + term
    total = total.astype(BF)
    side = dests[dests.shape[0] - 1]

    @pl.when(side == 0)
    def _():
        keep_ref[0] = total[:, :columns]
        send_ref[0] = total[:, columns:]

    @pl.when(side == 1)
    def _():
        keep_ref[0] = total[:, columns:]
        send_ref[0] = total[:, :columns]


ANY = pl.BlockSpec(memory_space=pl.ANY)
SMEM = pl.BlockSpec(memory_space=pltpu.SMEM)


def block_lists(block_ids, me, group, seg_dev, per_dev, cap):
    segments, per_seg, retr = block_ids.shape
    asked = per_seg * retr
    z = me // 2
    ids = block_ids.reshape(segments // (2 * seg_dev), 2, seg_dev, asked)
    ids = lax.dynamic_index_in_dim(ids, me % 2, 1, keepdims=False)
    slots = (z - jnp.arange(group, dtype=jnp.int32)) % group
    ids = jnp.take(ids, slots, axis=0).reshape(group * seg_dev, asked)
    owners = ids // per_dev
    here = owners // 2 == z
    place = ids - owners * per_dev + jnp.where(owners == me, 0, per_dev)
    position = jnp.arange(asked, dtype=jnp.int32)
    before = (position[None, :] < position[:, None])[None]
    rank = jnp.sum(jnp.logical_and(before, here[:, None, :]), axis=-1)
    chosen = jnp.logical_and(
        here[:, :, None], rank[:, :, None] == jnp.arange(cap, dtype=jnp.int32)
    )
    places = jnp.sum(jnp.where(chosen, place[:, :, None], 0), axis=1)
    home = position // retr - per_seg
    homes = per_seg + jnp.sum(jnp.where(chosen, home[None, :, None], 0), axis=1)
    counts = jnp.sum(here, axis=-1)
    return (
        counts.astype(jnp.int32),
        places.astype(jnp.int32).reshape(-1),
        homes.astype(jnp.int32).reshape(-1),
    )


def side_by_side(x):
    parts, rows, width = x.shape
    return x.transpose(1, 0, 2).reshape(rows, parts * width)


def gather_tokens(x):
    far = lax.ppermute(x, "fsdp", [(i, i ^ 2) for i in range(4)])
    near = lax.ppermute(x, "fsdp", [(i, i ^ 1) for i in range(4)])
    both = lax.ppermute(far, "fsdp", [(i, i ^ 1) for i in range(4)])
    return [x, near, far, both]


def weight_grad_plain(attention, parts, order):
    n = lax.axis_size("mem")
    rows = parts[0].shape[0]
    total = 0.0
    for i, part in enumerate(parts):
        own = lax.dynamic_slice_in_dim(attention, order[i] * rows, rows, 0)
        total = total + dot(own, part, TN)
    pieces = total.astype(BF).reshape(total.shape[0], n, -1).transpose(1, 0, 2)
    pieces = lax.all_to_all(pieces, "mem", split_axis=0, concat_axis=0, tiled=True)
    return jnp.sum(pieces.astype(F32), axis=0)


def cost(us):
    return pl.CostEstimate(flops=us * 10**9, bytes_accessed=us * 10**6, transcendentals=0)


def after(first, *rest):
    return lax.optimization_barrier((first, *rest))[1:]


def per_device(
    queries, keys, values, mem_keys, mem_values, block_ids, gate_bias, out_weight, cotangent
):
    n = lax.axis_size("mem")
    me = lax.axis_index("mem")
    fs = lax.axis_index("fsdp")
    group = n // 2
    full = mem_keys.shape[1]
    all_heads = full // DH
    width = full // HALVES
    heads = width // DH
    pairs = heads // 2
    segments, per_seg, retr = block_ids.shape
    seg_dev = segments // n
    per_dev = mem_keys.shape[0] // MBLK
    blocks = seg_dev * per_seg
    tokens = blocks * QBLK
    seg_len = per_seg * QBLK
    rows = queries.shape[0]
    seg_rows = seg_len // rows
    gating = jax.nn.sigmoid(lax.dynamic_slice_in_dim(gate_bias, fs * all_heads, all_heads))
    halves = range(HALVES)

    def shifted(x, k):
        return lax.ppermute(x, "mem", [(i, (i + 2 * k) % n) for i in range(n)])

    def exchange(x):
        return lax.all_to_all(x, "fsdp", split_axis=0, concat_axis=0, tiled=True)

    swap = [(i, i ^ 1) for i in range(n)]
    cap = -(-4 * max(1, retr * per_seg // n) // UNROLL) * UNROLL
    lists = block_lists(block_ids, me, group, seg_dev, per_dev, cap)

    par_keys = [lax.ppermute(mem_keys, "mem", swap)]
    par_values = [lax.ppermute(mem_values, "mem", swap)]

    q = exchange((queries * BF(SCALE)).T.reshape(4, full, rows))
    q_slots = [q] + [shifted(q, k) for k in range(1, group)]
    (cotangent,) = after(q, cotangent)
    cot_parts = gather_tokens(cotangent)
    keys, values = after(q, keys, values)
    k, v = (
        exchange(x.reshape(rows, 4, full).transpose(1, 0, 2)).reshape(tokens, full)
        for x in (keys, values)
    )
    cot_parts = after((q_slots, k, v), *cot_parts)
    order = fs ^ jnp.arange(4, dtype=jnp.int32)
    whole = pl.BlockSpec(memory_space=pltpu.VMEM)
    do_parts = pl.pallas_call(
        attention_grad_kernel,
        in_specs=[SMEM] + [whole] * 5,
        out_specs=[whole] * HALVES,
        out_shape=[jax.ShapeDtypeStruct((4, width, rows), BF)] * HALVES,
        compiler_params=pltpu.CompilerParams(vmem_limit_bytes=VMEM),
        cost_estimate=cost(1),
            name="attention_grad",
    )(order, out_weight, *cot_parts)
    do_slots = [[x] + [shifted(x, k) for k in range(1, group)] for x in do_parts]
    (late_weight,) = after(v, out_weight)
    full_weight = lax.all_gather(late_weight, "fsdp", axis=0, tiled=True)

    seg_spec = pl.BlockSpec((seg_len, full), lambda s: (s, 0))
    q_spec = pl.BlockSpec((seg_rows, full, rows), lambda s: (s, 0, 0))
    do_spec = pl.BlockSpec((seg_rows, width, rows), lambda s: (s, 0, 0))
    part_spec = pl.BlockSpec((per_seg, full, QBLK), lambda s: (s, 0, 0))
    part_shape = jax.ShapeDtypeStruct((blocks, full, QBLK), F32)
    head_shape = jax.ShapeDtypeStruct((tokens, full), BF)
    o_local, dq_local, dk, dv = pl.pallas_call(
        functools.partial(local_kernel, all_heads // 2, per_seg, HALVES),
        grid=(seg_dev,),
        in_specs=[SMEM, q_spec, seg_spec, seg_spec] + [do_spec] * HALVES,
        out_specs=[part_spec, part_spec, seg_spec, seg_spec],
        out_shape=[part_shape, part_shape, head_shape, head_shape],
        scratch_shapes=[pltpu.VMEM((seg_len, full), F32)] * 2,
        compiler_params=pltpu.CompilerParams(vmem_limit_bytes=VMEM),
        cost_estimate=cost(1),
            name="local",
    )(gating, q, k, v, *do_parts)

    lists = after((o_local, dk), *lists)
    t_specs = [
        pl.BlockSpec((per_seg, width, QBLK), at_slot(i, seg_dev - 1)) for i in range(group)
    ]
    t_shape = jax.ShapeDtypeStruct((blocks, width, QBLK), BF)
    slot_shape = jax.ShapeDtypeStruct((group, blocks, width, QBLK), F32)
    slot_spec = pl.BlockSpec((1, per_seg, width, QBLK), lambda s, b, *_: (s, b, 0, 0))
    all_spec = pl.BlockSpec((group, per_seg, width, QBLK), lambda s: (0, s, 0, 0))
    stat_block = (1, per_seg, 2, heads * QBLK)
    memory_rows = 2 * mem_keys.shape[0]
    scratch = [pltpu.VMEM((memory_rows, width), BF)] * 2
    scratch += [pltpu.VMEM((per_seg + 1, pairs, 128, 256), BF)] * 2
    scratch += [pltpu.VMEM((cap, pairs, MBLK, 256), F32)]
    acc = pltpu.VMEM((per_seg + 1, pairs, 128, 256), F32)
    rows8 = pltpu.VMEM((per_seg + 1, pairs, 8, 256), F32)
    rows1 = pltpu.VMEM((per_seg + 1, pairs, 1, 256), F32)
    sems = pltpu.SemaphoreType.DMA((4,))
    limit = pltpu.CompilerParams(vmem_limit_bytes=VMEM)
    def slot_specs(half):
        return [
            pl.BlockSpec((seg_rows, width, rows), at_slot(i, seg_dev - 1, half))
            for i in range(group)
        ]

    o_home, stat_slots = [], []
    spreads = [pltpu.VMEM((per_seg + 1, pairs, 128, 256), BF)]
    for i in halves:
        outs = pl.pallas_call(
            functools.partial(memory_forward, group, pairs, i),
            grid_spec=pltpu.PrefetchScalarGridSpec(
                num_scalar_prefetch=3,
                grid=(group, seg_dev),
                in_specs=[ANY] * 4 + slot_specs(i),
                out_specs=t_specs
                + [
                    slot_spec,
                    pl.BlockSpec(
                        (1, per_seg, 1, heads * QBLK), lambda s, b, *_: (s, b, 0, 0)
                    )
                ],
                scratch_shapes=scratch[:2] + spreads + scratch[-1:] + [rows8, rows8, acc, sems],
            ),
            out_shape=[t_shape] * group
            + [slot_shape]
            + [jax.ShapeDtypeStruct((group, blocks, 1, heads * QBLK), F32)],
            compiler_params=limit,
            cost_estimate=cost(30),
            name="memory_forward",
        )(*lists, mem_keys, par_keys[i], mem_values, par_values[i], *q_slots)
        o_slots, exact, lse = list(outs[:group]), outs[-2], outs[-1]
        stats = pl.pallas_call(
            functools.partial(statistics_kernel, group, heads),
            grid=(seg_dev,),
            in_specs=[
                pl.BlockSpec((group, per_seg, 1, heads * QBLK), lambda s: (0, s, 0, 0))
            ]
            + [pl.BlockSpec((seg_rows, width, rows), lambda s: (s, 0, 0))] * group
            + [all_spec],
            out_specs=pl.BlockSpec(
                (group, per_seg, 2, heads * QBLK), lambda s: (0, s, 0, 0)
            ),
            out_shape=jax.ShapeDtypeStruct((group, blocks, 2, heads * QBLK), F32),
            compiler_params=limit,
            cost_estimate=cost(5),
            name="statistics",
        )(lse, *do_slots[i], exact)
        stat_slots.append([stats] + [shifted(stats, k) for k in range(1, group)])
        if ORDER:
            middle = range(2, group - 1)
            held = after(stat_slots[-1], *[o_slots[j] for j in middle])
            for j, x in zip(middle, held):
                o_slots[j] = x
        o_home.append([o_slots[0]] + [shifted(o_slots[k], -k) for k in range(1, group)])

    last = stat_slots[-1][0]
    dq_home = []
    for i in halves:
        (own_stats,) = after(last, stat_slots[i][0])
        sums = pl.pallas_call(
            functools.partial(memory_backward, group, pairs, i),
            grid_spec=pltpu.PrefetchScalarGridSpec(
                num_scalar_prefetch=3,
                grid=(group, seg_dev),
                in_specs=[ANY] * 4
                + slot_specs(i)
                + slot_specs(0)
                + [pl.BlockSpec(stat_block, lambda s, b, *_: (s, b, 0, 0))],
                out_specs=[slot_spec] * 2,
                scratch_shapes=scratch + [rows1, rows1, acc, acc, sems],
            ),
            out_shape=[slot_shape] * 2,
            compiler_params=limit,
            cost_estimate=cost(30),
            name="memory_backward",
        )(
            *lists, mem_keys, par_keys[i], mem_values, par_values[i],
            *q_slots, *do_slots[i], own_stats,
        )
        wide_spec = pl.BlockSpec((per_seg, width, QBLK), lambda s: (s, 0, 0))
        dq_slots = pl.pallas_call(
            functools.partial(combine_kernel, group, heads),
            grid=(seg_dev,),
            in_specs=[
                pl.BlockSpec((group, per_seg, 2, heads * QBLK), lambda s: (0, s, 0, 0))
            ]
            * group
            + [all_spec] * 2,
            out_specs=[wide_spec] * group,
            out_shape=[t_shape] * group,
            compiler_params=limit,
            cost_estimate=cost(5),
            name="combine",
        )(*stat_slots[i], *sums)
        last = dq_slots[0]
        dq_home.append([dq_slots[0]] + [shifted(dq_slots[k], -k) for k in range(1, group)])

    dk, dv = after(last, dk, dv)
    key_grad, value_grad = [side_by_side(exchange(x.reshape(4, rows, full))) for x in (dk, dv)]
    home_spec = pl.BlockSpec((per_seg, width, QBLK), lambda b: (b, 0, 0))
    home_out = pl.BlockSpec((seg_len, width), lambda b: (b, 0))
    home_shape = jax.ShapeDtypeStruct((tokens, width), BF)
    home_specs = [
        pl.BlockSpec(stat_block, lambda b, k=k: (k, b, 0, 0)) for k in range(group)
    ]
    columns = out_weight.shape[1] // n
    steps = jnp.arange(group, dtype=jnp.int32)
    dests = jnp.concatenate([(me // 2 - steps) % group, (me % 2)[None]]).astype(jnp.int32)
    token_attention, weight_rows, token_dq = [], [], []
    for i in halves:
        local_spec = pl.BlockSpec((per_seg, width, QBLK), lambda b, i=i: (b, i, 0))
        home_stats = [stat_slots[i][(group - k) % group] for k in range(group)]
        o_parts = after(last, *o_home[i])
        attention, attention_t = pl.pallas_call(
            functools.partial(attention_kernel, group, heads, i * heads),
            grid=(seg_dev,),
            in_specs=[SMEM, local_spec] + [home_spec] * group + home_specs,
            out_specs=[home_out, pl.BlockSpec((width, seg_len), lambda b: (0, b))],
            out_shape=[home_shape, jax.ShapeDtypeStruct((width, tokens), BF)],
            compiler_params=limit,
            cost_estimate=cost(3),
            name="attention",
        )(gating, o_local, *o_parts, *home_stats)
        token_attention.append(exchange(attention.reshape(4, rows, width)))
        if columns % 128:
            weight_rows.append(weight_grad_plain(attention, cot_parts, order))
            continue
        piece = (1, width, columns)
        send, keep = pl.pallas_call(
            weight_grad_kernel,
            grid_spec=pltpu.PrefetchScalarGridSpec(
                num_scalar_prefetch=2,
                grid=(group,),
                in_specs=[pl.BlockSpec((width, tokens), lambda k, *_: (0, 0))]
                + [pl.BlockSpec((rows, 2 * columns), lambda k, _, to: (0, to[k]))] * 4,
                out_specs=[pl.BlockSpec(piece, lambda k, *_: (k, 0, 0))] * 2,
            ),
            out_shape=[jax.ShapeDtypeStruct((group, width, columns), BF)] * 2,
            compiler_params=limit,
            cost_estimate=cost(5),
            name="weight_grad",
        )(order, dests, attention_t, *cot_parts)
        got = lax.ppermute(send, "mem", swap)
        sums = [
            (keep[k].astype(F32) + got[k].astype(F32)).astype(BF) for k in range(group)
        ]
        sums = [sums[0]] + [shifted(sums[k], -k) for k in range(1, group)]
        weight_rows.append(functools.reduce(jnp.add, [x.astype(F32) for x in sums]))
    projected = jnp.einsum(
        "stc,scd->td",
        jnp.concatenate(token_attention, axis=2),
        full_weight.reshape(4, full, -1),
        preferred_element_type=F32,
    ).astype(BF)
    for i in halves:
        dq_parts = after(projected, *dq_home[i])
        local_spec = pl.BlockSpec((per_seg, width, QBLK), lambda b, i=i: (b, i, 0))
        dq = pl.pallas_call(
            functools.partial(query_grad_kernel, group, heads, i * heads),
            grid=(seg_dev,),
            in_specs=[SMEM, local_spec] + [home_spec] * group,
            out_specs=home_out,
            out_shape=home_shape,
            compiler_params=limit,
            cost_estimate=cost(3),
            name="query_grad",
        )(gating, dq_local, *dq_parts)
        token_dq.append(exchange(dq.reshape(4, rows, width)))

    return (
        projected,
        side_by_side(jnp.concatenate(token_dq, axis=2)),
        key_grad,
        value_grad,
        jnp.concatenate(weight_rows, axis=0),
    )


def solution(mesh):
    in_specs = (
        P(("mem", "fsdp"), None),
        P(("mem", "fsdp"), None),
        P(("mem", "fsdp"), None),
        P("mem", "fsdp"),
        P("mem", "fsdp"),
        P(),
        P(),
        P("fsdp", None),
        P(("mem", "fsdp"), None),
    )
    out_specs = (
        P(("mem", "fsdp"), None),
        P(("mem", "fsdp"), None),
        P(("mem", "fsdp"), None),
        P(("mem", "fsdp"), None),
        P("fsdp", "mem"),
    )
    return jax.shard_map(
        per_device, mesh=mesh, in_specs=in_specs, out_specs=out_specs, check_vma=False
    )
```

```python
import functools

import jax
import jax.numpy as jnp
from jax import lax
from jax.experimental import pallas as pl
from jax.experimental.pallas import tpu as pltpu
from jax.sharding import PartitionSpec as P

DH = 64
QBLK = 128
MBLK = 128
LOW = -1e30
UNROLL = 8
HALVES = 1
ORDER = False
VMEM = 58 * 2**20
SCALE = DH ** (-0.5)
BF = jnp.bfloat16
F32 = jnp.float32
NT = (((1,), (1,)), ((), ()))
NN = (((1,), (0,)), ((), ()))
TN = (((0,), (0,)), ((), ()))


def dot(a, b, dims):
    return lax.dot_general(a, b, dims, preferred_element_type=F32)


def spread(x):
    zero = jnp.zeros((DH, QBLK), x.dtype)
    upper = jnp.concatenate([x[:DH], zero], axis=1)
    lower = jnp.concatenate([zero, x[DH:]], axis=1)
    return jnp.concatenate([upper, lower], axis=0)


def query_block(ref, b, t):
    per = ref.shape[2] // QBLK
    return ref[b // per, t * 128 : (t + 1) * 128, (b % per) * QBLK : (b % per + 1) * QBLK]


def folded(x, op):
    return op(x.reshape(x.shape[0] // 8, 8, x.shape[1]), axis=0)


def own_blocks(parts):
    rows = []
    for part in parts:
        rows.append(part[:DH, :QBLK])
        rows.append(part[DH:, QBLK:])
    return rows


def at_slot(slot, last, column=0):
    def index(s, b, *_):
        return (jnp.where(s == slot, b, jnp.where(s > slot, last, 0)), column, 0)

    return index


def start_step(group, half, slot, memory, buffers, sems, sides):
    rows, width = buffers[0].shape
    rows = rows // 2
    own = pl.ds(half * width, width)
    sources = [memory[0].at[:, own], memory[1], memory[2].at[:, own], memory[3]]
    targets = [buffers[i].at[pl.ds(j * rows, rows)] for i in range(2) for j in range(2)]
    copies = [
        pltpu.make_async_copy(source, target, sems.at[i])
        for i, (source, target) in enumerate(zip(sources, targets))
    ]
    begins = (slot == 0) & (pl.program_id(1) == 0)

    @pl.when(begins)
    def _():
        for copy in copies:
            copy.start()
        for _, out in sides:
            out[...] = jnp.zeros_like(out)
        for copy in copies[:2]:
            copy.wait()

    def wait_values():
        @pl.when(begins)
        def _():
            for copy in copies[2:]:
                copy.wait()

    for i in range(group):

        @pl.when(slot == i)
        def _():
            for refs, out in sides:
                for b in range(out.shape[0] - 1):
                    for t in range(out.shape[1]):
                        x = query_block(refs[i], b, t)
                        out[b, t, :DH, :QBLK] = x[:DH]
                        out[b, t, DH:, QBLK:] = x[DH:]
    return wait_values


def memory_forward(
    group, pairs, half, counts, places, homes, k_own, k_par, v_own, v_par, *rest
):
    q_refs = rest[:group]
    o_refs = rest[group : 2 * group]
    exact_ref, lse_ref = rest[2 * group : 2 * group + 2]
    kbuf, vbuf, q_t, scores, tops, norms, acc, sems = rest[2 * group + 2 :]
    slot = pl.program_id(0)
    number = slot * pl.num_programs(1) + pl.program_id(1)
    cap = scores.shape[0]
    blocks = q_t.shape[0] - 1
    wait_values = start_step(
        group, half, slot, (k_own, k_par, v_own, v_par), (kbuf, vbuf), sems, [(q_refs, q_t)]
    )
    tops[...] = jnp.full(tops.shape, LOW, F32)
    norms[...] = jnp.zeros_like(norms)
    acc[...] = jnp.zeros_like(acc)
    turns = (counts[number] + UNROLL - 1) // UNROLL

    def first(turn, carry):
        found = []
        for u in range(UNROLL):
            j = turn * UNROLL + u
            row = pl.multiple_of(places[number * cap + j] * MBLK, MBLK)
            b = homes[number * cap + j]
            for t in range(pairs):
                cols = slice(t * 128, (t + 1) * 128)
                s = dot(kbuf[pl.ds(row, MBLK), cols], q_t[b, t], NN)
                scores[j, t] = s
                found.append((b, t, folded(s, jnp.max)))
        for b, t, top in found:
            tops[b, t] = jnp.maximum(tops[b, t], top)
        return carry

    lax.fori_loop(0, turns, first, 0)
    wait_values()
    tops[...] = jnp.broadcast_to(jnp.max(tops[...], axis=2, keepdims=True), tops.shape)

    def second(turn, carry):
        found = []
        for u in range(UNROLL):
            j = turn * UNROLL + u
            row = pl.multiple_of(places[number * cap + j] * MBLK, MBLK)
            b = homes[number * cap + j]
            for t in range(pairs):
                cols = slice(t * 128, (t + 1) * 128)
                p = jnp.exp(scores[j, t] - tops[b, t, 0:1, :])
                o = dot(vbuf[pl.ds(row, MBLK), cols], p.astype(BF), TN)
                found.append((b, t, folded(p, jnp.sum), o))
        for b, t, norm, o in found:
            norms[b, t] += norm
            acc[b, t] += o
        return carry

    lax.fori_loop(0, turns, second, 0)
    results = []
    for b in range(blocks):
        parts = []
        for t in range(pairs):
            wide = slice(t * 256, (t + 1) * 256)
            norm = jnp.sum(norms[b, t], axis=0, keepdims=True)
            some = norm > 0.0
            safe = jnp.where(some, norm, 1.0)
            lse_ref[0, b, :, wide] = jnp.where(some, tops[b, t, 0:1, :] + jnp.log(safe), LOW)
            parts.append(acc[b, t] * (1.0 / safe))
        results.append(jnp.concatenate(own_blocks(parts), axis=0))
        exact_ref[0, b] = results[b]
    for i in range(group):

        @pl.when(slot == i)
        def _():
            for b in range(blocks):
                o_refs[i][b] = results[b].astype(BF)


def statistics_kernel(group, heads, lse_ref, *rest):
    do_refs, (o_ref, stat_ref) = rest[:group], rest[group:]
    for i in range(group):
        for b in range(lse_ref.shape[1]):
            stat_ref[i, b, 0:1, :] = lse_ref[i, b]
            for t in range(heads // 2):
                do = query_block(do_refs[i], b, t).astype(F32)
                product = do * o_ref[i, b, t * 128 : (t + 1) * 128, :]
                for h in range(2):
                    at = slice((2 * t + h) * QBLK, (2 * t + h + 1) * QBLK)
                    stat_ref[i, b, 1:2, at] = jnp.sum(
                        product[h * DH : (h + 1) * DH], axis=0, keepdims=True
                    )


def merged(stat_refs, b):
    lses = [ref[0, b, 0:1, :] for ref in stat_refs]
    top = functools.reduce(jnp.maximum, lses)
    shares = [jnp.exp(x - top) for x in lses]
    norm = functools.reduce(jnp.add, shares)
    return top, shares, norm


def memory_backward(
    group, pairs, half, counts, places, homes, k_own, k_par, v_own, v_par, *rest
):
    q_refs = rest[:group]
    do_refs = rest[group : 2 * group]
    stat_ref = rest[2 * group]
    delta_ref, key_ref = rest[2 * group + 1 : 2 * group + 3]
    kbuf, vbuf, q_t, do_t, weights, lses, means, acc, acc_keys, sems = rest[2 * group + 3 :]
    slot = pl.program_id(0)
    number = slot * pl.num_programs(1) + pl.program_id(1)
    cap = places.shape[0] // counts.shape[0]
    blocks = q_t.shape[0] - 1
    wait_values = start_step(
        group, half, slot, (k_own, k_par, v_own, v_par), (kbuf, vbuf), sems,
        [(q_refs, q_t), (do_refs, do_t)],
    )
    lses[...] = jnp.zeros_like(lses)
    means[...] = jnp.zeros_like(means)
    for b in range(blocks):
        for t in range(pairs):
            wide = slice(t * 256, (t + 1) * 256)
            lses[b, t] = stat_ref[0, b, 0:1, wide]
            means[b, t] = stat_ref[0, b, 1:2, wide]
    acc[...] = jnp.zeros_like(acc)
    acc_keys[...] = jnp.zeros_like(acc_keys)
    turns = (counts[number] + UNROLL - 1) // UNROLL

    def first(turn, carry):
        found = []
        for u in range(UNROLL):
            j = turn * UNROLL + u
            row = pl.multiple_of(places[number * cap + j] * MBLK, MBLK)
            b = homes[number * cap + j]
            for t in range(pairs):
                cols = slice(t * 128, (t + 1) * 128)
                keys = kbuf[pl.ds(row, MBLK), cols]
                p = jnp.exp(dot(keys, q_t[b, t], NN) - lses[b, t])
                weights[j, t] = p
                found.append((b, t, dot(keys, p.astype(BF), TN)))
        for b, t, sums in found:
            acc_keys[b, t] += sums
        return carry

    lax.fori_loop(0, turns, first, 0)
    wait_values()

    def second(turn, carry):
        found = []
        for u in range(UNROLL):
            j = turn * UNROLL + u
            row = pl.multiple_of(places[number * cap + j] * MBLK, MBLK)
            b = homes[number * cap + j]
            for t in range(pairs):
                cols = slice(t * 128, (t + 1) * 128)
                slope = dot(vbuf[pl.ds(row, MBLK), cols], do_t[b, t], NN)
                delta = weights[j, t] * (slope - means[b, t])
                found.append((b, t, dot(kbuf[pl.ds(row, MBLK), cols], delta.astype(BF), TN)))
        for b, t, sums in found:
            acc[b, t] += sums
        return carry

    lax.fori_loop(0, turns, second, 0)
    for b in range(blocks):
        for out_ref, total in ((delta_ref, acc), (key_ref, acc_keys)):
            parts = own_blocks([total[b, t] for t in range(pairs)])
            out_ref[0, b] = jnp.concatenate(parts, axis=0)


def combine_kernel(group, heads, *rest):
    stat_refs = rest[:group]
    delta_ref, key_ref = rest[group : group + 2]
    dq_refs = rest[group + 2 :]
    for i in range(group):
        for b in range(dq_refs[i].shape[0]):
            rows = [ref[(i - j) % group, b] for j, ref in enumerate(stat_refs)]
            top = functools.reduce(jnp.maximum, [x[0:1] for x in rows])
            shares = [jnp.exp(x[0:1] - top) for x in rows]
            norm = functools.reduce(jnp.add, shares)
            mean = functools.reduce(jnp.add, [p * x[1:2] for p, x in zip(shares, rows)]) / norm
            share = shares[0] / norm
            moved = share * (rows[0][1:2] - mean)
            for h in range(heads):
                at = slice(h * DH, (h + 1) * DH)
                wide = slice(h * QBLK, (h + 1) * QBLK)
                dq_refs[i][b, at, :] = (
                    delta_ref[i, b, at, :] * share[:, wide]
                    + key_ref[i, b, at, :] * moved[:, wide]
                ).astype(BF)


def local_kernel(pairs, blocks, halves, gate, q_ref, k_ref, v_ref, *rest):
    do_refs = rest[:halves]
    o_ref, dq_ref, dk_ref, dv_ref, dk_acc, dv_acc = rest[halves:]
    per_half = pairs // halves
    dk_acc[...] = jnp.zeros_like(dk_acc)
    dv_acc[...] = jnp.zeros_like(dv_acc)
    key_at = lax.broadcasted_iota(jnp.int32, (MBLK, 2 * QBLK), 0)
    query_at = lax.broadcasted_iota(jnp.int32, (MBLK, 2 * QBLK), 1) % QBLK
    causal = key_at <= query_at
    lane = lax.broadcasted_iota(jnp.int32, (1, 128), 1)
    shares = []
    for t in range(pairs):
        shares.append(jnp.where(lane < DH, 1.0 - gate[2 * t], 1.0 - gate[2 * t + 1]))
    for t in range(pairs):
        cols = slice(t * 128, (t + 1) * 128)
        for b in range(blocks):
            q = spread(query_block(q_ref, b, t))
            do = spread(query_block(do_refs[t // per_half], b, t % per_half))
            scores, slopes = [], []
            for n in range(b + 1):
                rows = slice(n * MBLK, (n + 1) * MBLK)
                s = dot(k_ref[rows, cols], q, NN)
                scores.append(jnp.where(causal, s, LOW) if n == b else s)
                slopes.append(dot(v_ref[rows, cols], do, NN))
            largest = functools.reduce(jnp.maximum, [folded(s, jnp.max) for s in scores])
            largest = jnp.max(largest, axis=0, keepdims=True)
            weights = [jnp.exp(s - largest) for s in scores]
            norm = functools.reduce(jnp.add, [folded(p, jnp.sum) for p in weights])
            inverse = 1.0 / jnp.sum(norm, axis=0, keepdims=True)
            weights = [p * inverse for p in weights]
            mean = functools.reduce(
                jnp.add, [folded(p * x, jnp.sum) for p, x in zip(weights, slopes)]
            )
            mean = jnp.sum(mean, axis=0, keepdims=True)
            o = jnp.zeros((128, 256), F32)
            dq = jnp.zeros((128, 256), F32)
            for n in range(b + 1):
                rows = slice(n * MBLK, (n + 1) * MBLK)
                w = weights[n].astype(BF)
                delta = (weights[n] * (slopes[n] - mean)).astype(BF)
                o += dot(v_ref[rows, cols], w, TN)
                dq += dot(k_ref[rows, cols], delta, TN)
                dv_acc[rows, cols] += dot(w, do, NT)
                dk_acc[rows, cols] += dot(delta, q, NT)
            o_pair, dq_pair = own_blocks([o]), own_blocks([dq])
            for i in range(2):
                share = 1.0 - gate[2 * t + i]
                at = slice((2 * t + i) * DH, (2 * t + i + 1) * DH)
                o_ref[b, at, :] = o_pair[i] * share
                dq_ref[b, at, :] = dq_pair[i] * (share * SCALE)
        dk_ref[:, cols] = (dk_acc[:, cols] * shares[t]).astype(BF)
        dv_ref[:, cols] = (dv_acc[:, cols] * shares[t]).astype(BF)


def attention_kernel(group, heads, first, gate, local_ref, *rest):
    o_refs = rest[:group]
    stat_refs = rest[group : 2 * group]
    out_ref, out_t_ref = rest[2 * group :]
    for b in range(local_ref.shape[0]):
        _, shares, norm = merged(stat_refs, b)
        rows = []
        for h in range(heads):
            at = slice(h * DH, (h + 1) * DH)
            wide = slice(h * QBLK, (h + 1) * QBLK)
            total = functools.reduce(
                jnp.add,
                [x[:, wide] * ref[b, at, :].astype(F32) for x, ref in zip(shares, o_refs)],
            )
            rows.append(total * (gate[first + h] / norm[:, wide]) + local_ref[b, at, :])
        result = jnp.concatenate(rows, axis=0).astype(BF)
        out_t_ref[:, b * QBLK : (b + 1) * QBLK] = result
        out_ref[b * QBLK : (b + 1) * QBLK, :] = result.T


def query_grad_kernel(group, heads, first, gate, local_ref, *rest):
    dq_refs = rest[:group]
    out_ref = rest[group]
    for b in range(local_ref.shape[0]):
        rows = []
        for h in range(heads):
            at = slice(h * DH, (h + 1) * DH)
            total = functools.reduce(jnp.add, [ref[b, at, :].astype(F32) for ref in dq_refs])
            rows.append(total * (gate[first + h] * SCALE) + local_ref[b, at, :])
        result = jnp.concatenate(rows, axis=0).astype(BF)
        out_ref[b * QBLK : (b + 1) * QBLK, :] = result.T


def attention_grad_kernel(order, weight_ref, *rest):
    part_refs, out_refs = rest[:4], rest[4:]
    for i in range(4):
        grad = dot(weight_ref[...], part_refs[i][...], NT).astype(BF)
        rows = grad.shape[0] // len(out_refs)
        for j, out_ref in enumerate(out_refs):
            out_ref[order[i]] = grad[j * rows : (j + 1) * rows]


def weight_grad_kernel(order, dests, attention_ref, *rest):
    part_refs, (send_ref, keep_ref) = rest[:4], rest[4:]
    tokens = part_refs[0].shape[0]
    columns = part_refs[0].shape[1] // 2
    total = None
    for i in range(4):
        at = pl.multiple_of(order[i] * tokens, tokens)
        term = dot(attention_ref[:, pl.ds(at, tokens)], part_refs[i][...], NN)
        total = term if total is None else total + term
    total = total.astype(BF)
    side = dests[dests.shape[0] - 1]

    @pl.when(side == 0)
    def _():
        keep_ref[0] = total[:, :columns]
        send_ref[0] = total[:, columns:]

    @pl.when(side == 1)
    def _():
        keep_ref[0] = total[:, columns:]
        send_ref[0] = total[:, :columns]


ANY = pl.BlockSpec(memory_space=pl.ANY)
SMEM = pl.BlockSpec(memory_space=pltpu.SMEM)


def block_lists(block_ids, me, group, seg_dev, per_dev, cap):
    segments, per_seg, retr = block_ids.shape
    asked = per_seg * retr
    z = me // 2
    ids = block_ids.reshape(segments // (2 * seg_dev), 2, seg_dev, asked)
    ids = lax.dynamic_index_in_dim(ids, me % 2, 1, keepdims=False)
    slots = (z - jnp.arange(group, dtype=jnp.int32)) % group
    ids = jnp.take(ids, slots, axis=0).reshape(group * seg_dev, asked)
    owners = ids // per_dev
    here = owners // 2 == z
    place = ids - owners * per_dev + jnp.where(owners == me, 0, per_dev)
    position = jnp.arange(asked, dtype=jnp.int32)
    before = (position[None, :] < position[:, None])[None]
    rank = jnp.sum(jnp.logical_and(before, here[:, None, :]), axis=-1)
    chosen = jnp.logical_and(
        here[:, :, None], rank[:, :, None] == jnp.arange(cap, dtype=jnp.int32)
    )
    places = jnp.sum(jnp.where(chosen, place[:, :, None], 0), axis=1)
    home = position // retr - per_seg
    homes = per_seg + jnp.sum(jnp.where(chosen, home[None, :, None], 0), axis=1)
    counts = jnp.sum(here, axis=-1)
    return (
        counts.astype(jnp.int32),
        places.astype(jnp.int32).reshape(-1),
        homes.astype(jnp.int32).reshape(-1),
    )


def side_by_side(x):
    parts, rows, width = x.shape
    return x.transpose(1, 0, 2).reshape(rows, parts * width)


def gather_tokens(x):
    far = lax.ppermute(x, "fsdp", [(i, i ^ 2) for i in range(4)])
    near = lax.ppermute(x, "fsdp", [(i, i ^ 1) for i in range(4)])
    both = lax.ppermute(far, "fsdp", [(i, i ^ 1) for i in range(4)])
    return [x, near, far, both]


def weight_grad_plain(attention, parts, order):
    n = lax.axis_size("mem")
    rows = parts[0].shape[0]
    total = 0.0
    for i, part in enumerate(parts):
        own = lax.dynamic_slice_in_dim(attention, order[i] * rows, rows, 0)
        total = total + dot(own, part, TN)
    pieces = total.astype(BF).reshape(total.shape[0], n, -1).transpose(1, 0, 2)
    pieces = lax.all_to_all(pieces, "mem", split_axis=0, concat_axis=0, tiled=True)
    return jnp.sum(pieces.astype(F32), axis=0)


def cost(us):
    return pl.CostEstimate(flops=us * 10**9, bytes_accessed=us * 10**6, transcendentals=0)


def after(first, *rest):
    return lax.optimization_barrier((first, *rest))[1:]


def per_device(
    queries, keys, values, mem_keys, mem_values, block_ids, gate_bias, out_weight, cotangent
):
    n = lax.axis_size("mem")
    me = lax.axis_index("mem")
    fs = lax.axis_index("fsdp")
    group = n // 2
    full = mem_keys.shape[1]
    all_heads = full // DH
    width = full // HALVES
    heads = width // DH
    pairs = heads // 2
    segments, per_seg, retr = block_ids.shape
    seg_dev = segments // n
    per_dev = mem_keys.shape[0] // MBLK
    blocks = seg_dev * per_seg
    tokens = blocks * QBLK
    seg_len = per_seg * QBLK
    rows = queries.shape[0]
    seg_rows = seg_len // rows
    gating = jax.nn.sigmoid(lax.dynamic_slice_in_dim(gate_bias, fs * all_heads, all_heads))
    halves = range(HALVES)

    def shifted(x, k):
        return lax.ppermute(x, "mem", [(i, (i + 2 * k) % n) for i in range(n)])

    def exchange(x):
        return lax.all_to_all(x, "fsdp", split_axis=0, concat_axis=0, tiled=True)

    swap = [(i, i ^ 1) for i in range(n)]
    cap = -(-4 * max(1, retr * per_seg // n) // UNROLL) * UNROLL
    lists = block_lists(block_ids, me, group, seg_dev, per_dev, cap)

    par_keys = [lax.ppermute(mem_keys, "mem", swap)]
    par_values = [lax.ppermute(mem_values, "mem", swap)]

    q = exchange((queries * BF(SCALE)).T.reshape(4, full, rows))
    q_slots = [q] + [shifted(q, k) for k in range(1, group)]
    (cotangent,) = after(q, cotangent)
    cot_parts = gather_tokens(cotangent)
    keys, values = after(q, keys, values)
    k, v = (
        exchange(x.reshape(rows, 4, full).transpose(1, 0, 2)).reshape(tokens, full)
        for x in (keys, values)
    )
    cot_parts = after((q_slots, k, v), *cot_parts)
    order = fs ^ jnp.arange(4, dtype=jnp.int32)
    whole = pl.BlockSpec(memory_space=pltpu.VMEM)
    do_parts = pl.pallas_call(
        attention_grad_kernel,
        in_specs=[SMEM] + [whole] * 5,
        out_specs=[whole] * HALVES,
        out_shape=[jax.ShapeDtypeStruct((4, width, rows), BF)] * HALVES,
        compiler_params=pltpu.CompilerParams(vmem_limit_bytes=VMEM),
        cost_estimate=cost(1),
            name="attention_grad",
    )(order, out_weight, *cot_parts)
    do_slots = [[x] + [shifted(x, k) for k in range(1, group)] for x in do_parts]
    (late_weight,) = after(v, out_weight)
    full_weight = lax.all_gather(late_weight, "fsdp", axis=0, tiled=True)

    seg_spec = pl.BlockSpec((seg_len, full), lambda s: (s, 0))
    q_spec = pl.BlockSpec((seg_rows, full, rows), lambda s: (s, 0, 0))
    do_spec = pl.BlockSpec((seg_rows, width, rows), lambda s: (s, 0, 0))
    part_spec = pl.BlockSpec((per_seg, full, QBLK), lambda s: (s, 0, 0))
    part_shape = jax.ShapeDtypeStruct((blocks, full, QBLK), F32)
    head_shape = jax.ShapeDtypeStruct((tokens, full), BF)
    o_local, dq_local, dk, dv = pl.pallas_call(
        functools.partial(local_kernel, all_heads // 2, per_seg, HALVES),
        grid=(seg_dev,),
        in_specs=[SMEM, q_spec, seg_spec, seg_spec] + [do_spec] * HALVES,
        out_specs=[part_spec, part_spec, seg_spec, seg_spec],
        out_shape=[part_shape, part_shape, head_shape, head_shape],
        scratch_shapes=[pltpu.VMEM((seg_len, full), F32)] * 2,
        compiler_params=pltpu.CompilerParams(vmem_limit_bytes=VMEM),
        cost_estimate=cost(1),
            name="local",
    )(gating, q, k, v, *do_parts)

    lists = after((o_local, dk), *lists)
    t_specs = [
        pl.BlockSpec((per_seg, width, QBLK), at_slot(i, seg_dev - 1)) for i in range(group)
    ]
    t_shape = jax.ShapeDtypeStruct((blocks, width, QBLK), BF)
    slot_shape = jax.ShapeDtypeStruct((group, blocks, width, QBLK), F32)
    slot_spec = pl.BlockSpec((1, per_seg, width, QBLK), lambda s, b, *_: (s, b, 0, 0))
    all_spec = pl.BlockSpec((group, per_seg, width, QBLK), lambda s: (0, s, 0, 0))
    stat_block = (1, per_seg, 2, heads * QBLK)
    memory_rows = 2 * mem_keys.shape[0]
    scratch = [pltpu.VMEM((memory_rows, width), BF)] * 2
    scratch += [pltpu.VMEM((per_seg + 1, pairs, 128, 256), BF)] * 2
    scratch += [pltpu.VMEM((cap, pairs, MBLK, 256), F32)]
    acc = pltpu.VMEM((per_seg + 1, pairs, 128, 256), F32)
    rows8 = pltpu.VMEM((per_seg + 1, pairs, 8, 256), F32)
    rows1 = pltpu.VMEM((per_seg + 1, pairs, 1, 256), F32)
    sems = pltpu.SemaphoreType.DMA((4,))
    limit = pltpu.CompilerParams(vmem_limit_bytes=VMEM)
    def slot_specs(half):
        return [
            pl.BlockSpec((seg_rows, width, rows), at_slot(i, seg_dev - 1, half))
            for i in range(group)
        ]

    o_home, stat_slots = [], []
    spreads = [pltpu.VMEM((per_seg + 1, pairs, 128, 256), BF)]
    for i in halves:
        outs = pl.pallas_call(
            functools.partial(memory_forward, group, pairs, i),
            grid_spec=pltpu.PrefetchScalarGridSpec(
                num_scalar_prefetch=3,
                grid=(group, seg_dev),
                in_specs=[ANY] * 4 + slot_specs(i),
                out_specs=t_specs
                + [
                    slot_spec,
                    pl.BlockSpec(
                        (1, per_seg, 1, heads * QBLK), lambda s, b, *_: (s, b, 0, 0)
                    )
                ],
                scratch_shapes=scratch[:2] + spreads + scratch[-1:] + [rows8, rows8, acc, sems],
            ),
            out_shape=[t_shape] * group
            + [slot_shape]
            + [jax.ShapeDtypeStruct((group, blocks, 1, heads * QBLK), F32)],
            compiler_params=limit,
            cost_estimate=cost(30),
            name="memory_forward",
        )(*lists, mem_keys, par_keys[i], mem_values, par_values[i], *q_slots)
        o_slots, exact, lse = list(outs[:group]), outs[-2], outs[-1]
        stats = pl.pallas_call(
            functools.partial(statistics_kernel, group, heads),
            grid=(seg_dev,),
            in_specs=[
                pl.BlockSpec((group, per_seg, 1, heads * QBLK), lambda s: (0, s, 0, 0))
            ]
            + [pl.BlockSpec((seg_rows, width, rows), lambda s: (s, 0, 0))] * group
            + [all_spec],
            out_specs=pl.BlockSpec(
                (group, per_seg, 2, heads * QBLK), lambda s: (0, s, 0, 0)
            ),
            out_shape=jax.ShapeDtypeStruct((group, blocks, 2, heads * QBLK), F32),
            compiler_params=limit,
            cost_estimate=cost(5),
            name="statistics",
        )(lse, *do_slots[i], exact)
        stat_slots.append([stats] + [shifted(stats, k) for k in range(1, group)])
        if ORDER:
            middle = range(2, group - 1)
            held = after(stat_slots[-1], *[o_slots[j] for j in middle])
            for j, x in zip(middle, held):
                o_slots[j] = x
        o_home.append([o_slots[0]] + [shifted(o_slots[k], -k) for k in range(1, group)])

    last = stat_slots[-1][0]
    dq_home = []
    for i in halves:
        (own_stats,) = after(last, stat_slots[i][0])
        sums = pl.pallas_call(
            functools.partial(memory_backward, group, pairs, i),
            grid_spec=pltpu.PrefetchScalarGridSpec(
                num_scalar_prefetch=3,
                grid=(group, seg_dev),
                in_specs=[ANY] * 4
                + slot_specs(i)
                + slot_specs(0)
                + [pl.BlockSpec(stat_block, lambda s, b, *_: (s, b, 0, 0))],
                out_specs=[slot_spec] * 2,
                scratch_shapes=scratch + [rows1, rows1, acc, acc, sems],
            ),
            out_shape=[slot_shape] * 2,
            compiler_params=limit,
            cost_estimate=cost(30),
            name="memory_backward",
        )(
            *lists, mem_keys, par_keys[i], mem_values, par_values[i],
            *q_slots, *do_slots[i], own_stats,
        )
        wide_spec = pl.BlockSpec((per_seg, width, QBLK), lambda s: (s, 0, 0))
        dq_slots = pl.pallas_call(
            functools.partial(combine_kernel, group, heads),
            grid=(seg_dev,),
            in_specs=[
                pl.BlockSpec((group, per_seg, 2, heads * QBLK), lambda s: (0, s, 0, 0))
            ]
            * group
            + [all_spec] * 2,
            out_specs=[wide_spec] * group,
            out_shape=[t_shape] * group,
            compiler_params=limit,
            cost_estimate=cost(5),
            name="combine",
        )(*stat_slots[i], *sums)
        last = dq_slots[0]
        dq_home.append([dq_slots[0]] + [shifted(dq_slots[k], -k) for k in range(1, group)])

    dk, dv = after(last, dk, dv)
    key_grad, value_grad = [side_by_side(exchange(x.reshape(4, rows, full))) for x in (dk, dv)]
    home_spec = pl.BlockSpec((per_seg, width, QBLK), lambda b: (b, 0, 0))
    home_out = pl.BlockSpec((seg_len, width), lambda b: (b, 0))
    home_shape = jax.ShapeDtypeStruct((tokens, width), BF)
    home_specs = [
        pl.BlockSpec(stat_block, lambda b, k=k: (k, b, 0, 0)) for k in range(group)
    ]
    columns = out_weight.shape[1] // n
    steps = jnp.arange(group, dtype=jnp.int32)
    dests = jnp.concatenate([(me // 2 - steps) % group, (me % 2)[None]]).astype(jnp.int32)
    token_attention, weight_rows, token_dq = [], [], []
    for i in halves:
        local_spec = pl.BlockSpec((per_seg, width, QBLK), lambda b, i=i: (b, i, 0))
        home_stats = [stat_slots[i][(group - k) % group] for k in range(group)]
        o_parts = after(last, *o_home[i])
        attention, attention_t = pl.pallas_call(
            functools.partial(attention_kernel, group, heads, i * heads),
            grid=(seg_dev,),
            in_specs=[SMEM, local_spec] + [home_spec] * group + home_specs,
            out_specs=[home_out, pl.BlockSpec((width, seg_len), lambda b: (0, b))],
            out_shape=[home_shape, jax.ShapeDtypeStruct((width, tokens), BF)],
            compiler_params=limit,
            cost_estimate=cost(3),
            name="attention",
        )(gating, o_local, *o_parts, *home_stats)
        token_attention.append(exchange(attention.reshape(4, rows, width)))
        if columns % 128:
            weight_rows.append(weight_grad_plain(attention, cot_parts, order))
            continue
        piece = (1, width, columns)
        send, keep = pl.pallas_call(
            weight_grad_kernel,
            grid_spec=pltpu.PrefetchScalarGridSpec(
                num_scalar_prefetch=2,
                grid=(group,),
                in_specs=[pl.BlockSpec((width, tokens), lambda k, *_: (0, 0))]
                + [pl.BlockSpec((rows, 2 * columns), lambda k, _, to: (0, to[k]))] * 4,
                out_specs=[pl.BlockSpec(piece, lambda k, *_: (k, 0, 0))] * 2,
            ),
            out_shape=[jax.ShapeDtypeStruct((group, width, columns), BF)] * 2,
            compiler_params=limit,
            cost_estimate=cost(5),
            name="weight_grad",
        )(order, dests, attention_t, *cot_parts)
        got = lax.ppermute(send, "mem", swap)
        sums = [
            (keep[k].astype(F32) + got[k].astype(F32)).astype(BF) for k in range(group)
        ]
        sums = after(dq_home, *sums)
        sums = [sums[0]] + [shifted(sums[k], -k) for k in range(1, group)]
        weight_rows.append(functools.reduce(jnp.add, [x.astype(F32) for x in sums]))
    projected = jnp.einsum(
        "stc,scd->td",
        jnp.concatenate(token_attention, axis=2),
        full_weight.reshape(4, full, -1),
        preferred_element_type=F32,
    ).astype(BF)
    for i in halves:
        dq_parts = after(projected, *dq_home[i])
        local_spec = pl.BlockSpec((per_seg, width, QBLK), lambda b, i=i: (b, i, 0))
        dq = pl.pallas_call(
            functools.partial(query_grad_kernel, group, heads, i * heads),
            grid=(seg_dev,),
            in_specs=[SMEM, local_spec] + [home_spec] * group,
            out_specs=home_out,
            out_shape=home_shape,
            compiler_params=limit,
            cost_estimate=cost(3),
            name="query_grad",
        )(gating, dq_local, *dq_parts)
        token_dq.append(exchange(dq.reshape(4, rows, width)))

    return (
        projected,
        side_by_side(jnp.concatenate(token_dq, axis=2)),
        key_grad,
        value_grad,
        jnp.concatenate(weight_rows, axis=0),
    )


def solution(mesh):
    in_specs = (
        P(("mem", "fsdp"), None),
        P(("mem", "fsdp"), None),
        P(("mem", "fsdp"), None),
        P("mem", "fsdp"),
        P("mem", "fsdp"),
        P(),
        P(),
        P("fsdp", None),
        P(("mem", "fsdp"), None),
    )
    out_specs = (
        P(("mem", "fsdp"), None),
        P(("mem", "fsdp"), None),
        P(("mem", "fsdp"), None),
        P(("mem", "fsdp"), None),
        P("fsdp", "mem"),
    )
    return jax.shard_map(
        per_device, mesh=mesh, in_specs=in_specs, out_specs=out_specs, check_vma=False
    )
```

```python
import functools

import jax
import jax.numpy as jnp
from jax import lax
from jax.experimental import pallas as pl
from jax.experimental.pallas import tpu as pltpu
from jax.sharding import PartitionSpec as P

DH = 64
QBLK = 128
MBLK = 128
LOW = -1e30
UNROLL = 8
HALVES = 1
ORDER = False
VMEM = 58 * 2**20
SCALE = DH ** (-0.5)
BF = jnp.bfloat16
F32 = jnp.float32
NT = (((1,), (1,)), ((), ()))
NN = (((1,), (0,)), ((), ()))
TN = (((0,), (0,)), ((), ()))


def dot(a, b, dims):
    return lax.dot_general(a, b, dims, preferred_element_type=F32)


def spread(x):
    zero = jnp.zeros((DH, QBLK), x.dtype)
    upper = jnp.concatenate([x[:DH], zero], axis=1)
    lower = jnp.concatenate([zero, x[DH:]], axis=1)
    return jnp.concatenate([upper, lower], axis=0)


def query_block(ref, b, t):
    per = ref.shape[2] // QBLK
    return ref[b // per, t * 128 : (t + 1) * 128, (b % per) * QBLK : (b % per + 1) * QBLK]


def folded(x, op):
    return op(x.reshape(x.shape[0] // 8, 8, x.shape[1]), axis=0)


def own_blocks(parts):
    rows = []
    for part in parts:
        rows.append(part[:DH, :QBLK])
        rows.append(part[DH:, QBLK:])
    return rows


def own_columns(total):
    return jnp.concatenate([total[:DH, :QBLK], total[DH:, QBLK:]], axis=1)


def stacked(parts):
    rows = []
    for part in parts:
        rows += [part[:, :QBLK], part[:, QBLK:]]
    return jnp.concatenate(rows, axis=0)


def at_slot(slot, last, column=0):
    def index(s, b, *_):
        return (jnp.where(s == slot, b, jnp.where(s > slot, last, 0)), column, 0)

    return index


def start_step(group, half, slot, memory, buffers, sems, sides):
    rows, width = buffers[0].shape
    rows = rows // 2
    own = pl.ds(half * width, width)
    sources = [memory[0].at[:, own], memory[1], memory[2].at[:, own], memory[3]]
    targets = [buffers[i].at[pl.ds(j * rows, rows)] for i in range(2) for j in range(2)]
    copies = [
        pltpu.make_async_copy(source, target, sems.at[i])
        for i, (source, target) in enumerate(zip(sources, targets))
    ]
    begins = (slot == 0) & (pl.program_id(1) == 0)

    @pl.when(begins)
    def _():
        for copy in copies:
            copy.start()
        for _, out in sides:
            out[...] = jnp.zeros_like(out)
        for copy in copies[:2]:
            copy.wait()

    def wait_values():
        @pl.when(begins)
        def _():
            for copy in copies[2:]:
                copy.wait()

    for i in range(group):

        @pl.when(slot == i)
        def _():
            for refs, out in sides:
                for b in range(out.shape[0] - 1):
                    for t in range(out.shape[1]):
                        x = query_block(refs[i], b, t)
                        out[b, t, :DH, :QBLK] = x[:DH]
                        out[b, t, DH:, QBLK:] = x[DH:]
    return wait_values


def memory_forward(
    group, pairs, half, counts, places, homes, k_own, k_par, v_own, v_par, *rest
):
    q_refs = rest[:group]
    o_refs = rest[group : 2 * group]
    exact_ref, lse_ref = rest[2 * group : 2 * group + 2]
    kbuf, vbuf, q_t, scores, tops, norms, acc, sems = rest[2 * group + 2 :]
    slot = pl.program_id(0)
    number = slot * pl.num_programs(1) + pl.program_id(1)
    cap = scores.shape[0]
    blocks = q_t.shape[0] - 1
    wait_values = start_step(
        group, half, slot, (k_own, k_par, v_own, v_par), (kbuf, vbuf), sems, [(q_refs, q_t)]
    )
    tops[...] = jnp.full(tops.shape, LOW, F32)
    norms[...] = jnp.zeros_like(norms)
    acc[...] = jnp.zeros_like(acc)
    turns = (counts[number] + UNROLL - 1) // UNROLL

    def first(turn, carry):
        found = []
        for u in range(UNROLL):
            j = turn * UNROLL + u
            row = pl.multiple_of(places[number * cap + j] * MBLK, MBLK)
            b = homes[number * cap + j]
            for t in range(pairs):
                cols = slice(t * 128, (t + 1) * 128)
                s = dot(kbuf[pl.ds(row, MBLK), cols], q_t[b, t], NN)
                scores[j, t] = s
                found.append((b, t, folded(s, jnp.max)))
        for b, t, top in found:
            tops[b, t] = jnp.maximum(tops[b, t], top)
        return carry

    lax.fori_loop(0, turns, first, 0)
    wait_values()
    tops[...] = jnp.broadcast_to(jnp.max(tops[...], axis=2, keepdims=True), tops.shape)

    def second(turn, carry):
        found = []
        for u in range(UNROLL):
            j = turn * UNROLL + u
            row = pl.multiple_of(places[number * cap + j] * MBLK, MBLK)
            b = homes[number * cap + j]
            for t in range(pairs):
                cols = slice(t * 128, (t + 1) * 128)
                p = jnp.exp(scores[j, t] - tops[b, t, 0:1, :])
                o = dot(vbuf[pl.ds(row, MBLK), cols], p.astype(BF), TN)
                found.append((b, t, folded(p, jnp.sum), o))
        for b, t, norm, o in found:
            norms[b, t] += norm
            acc[b, t] += own_columns(o)
        return carry

    lax.fori_loop(0, turns, second, 0)
    results = []
    for b in range(blocks):
        parts = []
        for t in range(pairs):
            wide = slice(t * 256, (t + 1) * 256)
            norm = jnp.sum(norms[b, t], axis=0, keepdims=True)
            some = norm > 0.0
            safe = jnp.where(some, norm, 1.0)
            lse_ref[0, b, :, wide] = jnp.where(some, tops[b, t, 0:1, :] + jnp.log(safe), LOW)
            parts.append(acc[b, t] * (1.0 / safe))
        results.append(stacked(parts))
        exact_ref[0, b] = results[b]
    for i in range(group):

        @pl.when(slot == i)
        def _():
            for b in range(blocks):
                o_refs[i][b] = results[b].astype(BF)


def statistics_kernel(group, heads, lse_ref, *rest):
    do_refs, (o_ref, stat_ref) = rest[:group], rest[group:]
    for i in range(group):
        for b in range(lse_ref.shape[1]):
            stat_ref[i, b, 0:1, :] = lse_ref[i, b]
            for t in range(heads // 2):
                do = query_block(do_refs[i], b, t).astype(F32)
                product = do * o_ref[i, b, t * 128 : (t + 1) * 128, :]
                for h in range(2):
                    at = slice((2 * t + h) * QBLK, (2 * t + h + 1) * QBLK)
                    stat_ref[i, b, 1:2, at] = jnp.sum(
                        product[h * DH : (h + 1) * DH], axis=0, keepdims=True
                    )


def merged(stat_refs, b):
    lses = [ref[0, b, 0:1, :] for ref in stat_refs]
    top = functools.reduce(jnp.maximum, lses)
    shares = [jnp.exp(x - top) for x in lses]
    norm = functools.reduce(jnp.add, shares)
    return top, shares, norm


def memory_backward(
    group, pairs, half, counts, places, homes, k_own, k_par, v_own, v_par, *rest
):
    q_refs = rest[:group]
    do_refs = rest[group : 2 * group]
    stat_ref = rest[2 * group]
    delta_ref, key_ref = rest[2 * group + 1 : 2 * group + 3]
    kbuf, vbuf, q_t, do_t, weights, lses, means, acc, acc_keys, sems = rest[2 * group + 3 :]
    slot = pl.program_id(0)
    number = slot * pl.num_programs(1) + pl.program_id(1)
    cap = places.shape[0] // counts.shape[0]
    blocks = q_t.shape[0] - 1
    wait_values = start_step(
        group, half, slot, (k_own, k_par, v_own, v_par), (kbuf, vbuf), sems,
        [(q_refs, q_t), (do_refs, do_t)],
    )
    lses[...] = jnp.zeros_like(lses)
    means[...] = jnp.zeros_like(means)
    for b in range(blocks):
        for t in range(pairs):
            wide = slice(t * 256, (t + 1) * 256)
            lses[b, t] = stat_ref[0, b, 0:1, wide]
            means[b, t] = stat_ref[0, b, 1:2, wide]
    acc[...] = jnp.zeros_like(acc)
    acc_keys[...] = jnp.zeros_like(acc_keys)
    turns = (counts[number] + UNROLL - 1) // UNROLL

    def first(turn, carry):
        found = []
        for u in range(UNROLL):
            j = turn * UNROLL + u
            row = pl.multiple_of(places[number * cap + j] * MBLK, MBLK)
            b = homes[number * cap + j]
            for t in range(pairs):
                cols = slice(t * 128, (t + 1) * 128)
                keys = kbuf[pl.ds(row, MBLK), cols]
                p = jnp.exp(dot(keys, q_t[b, t], NN) - lses[b, t])
                weights[j, t] = p
                found.append((b, t, dot(keys, p.astype(BF), TN)))
        for b, t, sums in found:
            acc_keys[b, t] += own_columns(sums)
        return carry

    lax.fori_loop(0, turns, first, 0)
    wait_values()

    def second(turn, carry):
        found = []
        for u in range(UNROLL):
            j = turn * UNROLL + u
            row = pl.multiple_of(places[number * cap + j] * MBLK, MBLK)
            b = homes[number * cap + j]
            for t in range(pairs):
                cols = slice(t * 128, (t + 1) * 128)
                slope = dot(vbuf[pl.ds(row, MBLK), cols], do_t[b, t], NN)
                delta = weights[j, t] * (slope - means[b, t])
                found.append((b, t, dot(kbuf[pl.ds(row, MBLK), cols], delta.astype(BF), TN)))
        for b, t, sums in found:
            acc[b, t] += own_columns(sums)
        return carry

    lax.fori_loop(0, turns, second, 0)
    for b in range(blocks):
        for out_ref, total in ((delta_ref, acc), (key_ref, acc_keys)):
            out_ref[0, b] = stacked([total[b, t] for t in range(pairs)])


def combine_kernel(group, heads, *rest):
    stat_refs = rest[:group]
    delta_ref, key_ref = rest[group : group + 2]
    dq_refs = rest[group + 2 :]
    for i in range(group):
        for b in range(dq_refs[i].shape[0]):
            rows = [ref[(i - j) % group, b] for j, ref in enumerate(stat_refs)]
            top = functools.reduce(jnp.maximum, [x[0:1] for x in rows])
            shares = [jnp.exp(x[0:1] - top) for x in rows]
            norm = functools.reduce(jnp.add, shares)
            mean = functools.reduce(jnp.add, [p * x[1:2] for p, x in zip(shares, rows)]) / norm
            share = shares[0] / norm
            moved = share * (rows[0][1:2] - mean)
            for h in range(heads):
                at = slice(h * DH, (h + 1) * DH)
                wide = slice(h * QBLK, (h + 1) * QBLK)
                dq_refs[i][b, at, :] = (
                    delta_ref[i, b, at, :] * share[:, wide]
                    + key_ref[i, b, at, :] * moved[:, wide]
                ).astype(BF)


def local_kernel(pairs, blocks, halves, gate, q_ref, k_ref, v_ref, *rest):
    do_refs = rest[:halves]
    o_ref, dq_ref, dk_ref, dv_ref, dk_acc, dv_acc = rest[halves:]
    per_half = pairs // halves
    dk_acc[...] = jnp.zeros_like(dk_acc)
    dv_acc[...] = jnp.zeros_like(dv_acc)
    key_at = lax.broadcasted_iota(jnp.int32, (MBLK, 2 * QBLK), 0)
    query_at = lax.broadcasted_iota(jnp.int32, (MBLK, 2 * QBLK), 1) % QBLK
    causal = key_at <= query_at
    lane = lax.broadcasted_iota(jnp.int32, (1, 128), 1)
    shares = []
    for t in range(pairs):
        shares.append(jnp.where(lane < DH, 1.0 - gate[2 * t], 1.0 - gate[2 * t + 1]))
    for t in range(pairs):
        cols = slice(t * 128, (t + 1) * 128)
        for b in range(blocks):
            q = spread(query_block(q_ref, b, t))
            do = spread(query_block(do_refs[t // per_half], b, t % per_half))
            scores, slopes = [], []
            for n in range(b + 1):
                rows = slice(n * MBLK, (n + 1) * MBLK)
                s = dot(k_ref[rows, cols], q, NN)
                scores.append(jnp.where(causal, s, LOW) if n == b else s)
                slopes.append(dot(v_ref[rows, cols], do, NN))
            largest = functools.reduce(jnp.maximum, [folded(s, jnp.max) for s in scores])
            largest = jnp.max(largest, axis=0, keepdims=True)
            weights = [jnp.exp(s - largest) for s in scores]
            norm = functools.reduce(jnp.add, [folded(p, jnp.sum) for p in weights])
            inverse = 1.0 / jnp.sum(norm, axis=0, keepdims=True)
            weights = [p * inverse for p in weights]
            mean = functools.reduce(
                jnp.add, [folded(p * x, jnp.sum) for p, x in zip(weights, slopes)]
            )
            mean = jnp.sum(mean, axis=0, keepdims=True)
            o = jnp.zeros((128, 256), F32)
            dq = jnp.zeros((128, 256), F32)
            for n in range(b + 1):
                rows = slice(n * MBLK, (n + 1) * MBLK)
                w = weights[n].astype(BF)
                delta = (weights[n] * (slopes[n] - mean)).astype(BF)
                o += dot(v_ref[rows, cols], w, TN)
                dq += dot(k_ref[rows, cols], delta, TN)
                dv_acc[rows, cols] += dot(w, do, NT)
                dk_acc[rows, cols] += dot(delta, q, NT)
            o_pair, dq_pair = own_blocks([o]), own_blocks([dq])
            for i in range(2):
                share = 1.0 - gate[2 * t + i]
                at = slice((2 * t + i) * DH, (2 * t + i + 1) * DH)
                o_ref[b, at, :] = o_pair[i] * share
                dq_ref[b, at, :] = dq_pair[i] * (share * SCALE)
        dk_ref[:, cols] = (dk_acc[:, cols] * shares[t]).astype(BF)
        dv_ref[:, cols] = (dv_acc[:, cols] * shares[t]).astype(BF)


def attention_kernel(group, heads, first, gate, local_ref, *rest):
    o_refs = rest[:group]
    stat_refs = rest[group : 2 * group]
    out_ref, out_t_ref = rest[2 * group :]
    for b in range(local_ref.shape[0]):
        _, shares, norm = merged(stat_refs, b)
        rows = []
        for h in range(heads):
            at = slice(h * DH, (h + 1) * DH)
            wide = slice(h * QBLK, (h + 1) * QBLK)
            total = functools.reduce(
                jnp.add,
                [x[:, wide] * ref[b, at, :].astype(F32) for x, ref in zip(shares, o_refs)],
            )
            rows.append(total * (gate[first + h] / norm[:, wide]) + local_ref[b, at, :])
        result = jnp.concatenate(rows, axis=0).astype(BF)
        out_t_ref[:, b * QBLK : (b + 1) * QBLK] = result
        out_ref[b * QBLK : (b + 1) * QBLK, :] = result.T


def query_grad_kernel(group, heads, first, gate, local_ref, *rest):
    dq_refs = rest[:group]
    out_ref = rest[group]
    for b in range(local_ref.shape[0]):
        rows = []
        for h in range(heads):
            at = slice(h * DH, (h + 1) * DH)
            total = functools.reduce(jnp.add, [ref[b, at, :].astype(F32) for ref in dq_refs])
            rows.append(total * (gate[first + h] * SCALE) + local_ref[b, at, :])
        result = jnp.concatenate(rows, axis=0).astype(BF)
        out_ref[b * QBLK : (b + 1) * QBLK, :] = result.T


def attention_grad_kernel(order, weight_ref, *rest):
    part_refs, out_refs = rest[:4], rest[4:]
    for i in range(4):
        grad = dot(weight_ref[...], part_refs[i][...], NT).astype(BF)
        rows = grad.shape[0] // len(out_refs)
        for j, out_ref in enumerate(out_refs):
            out_ref[order[i]] = grad[j * rows : (j + 1) * rows]


def weight_grad_kernel(order, dests, attention_ref, *rest):
    part_refs, (send_ref, keep_ref) = rest[:4], rest[4:]
    tokens = part_refs[0].shape[0]
    columns = part_refs[0].shape[1] // 2
    total = None
    for i in range(4):
        at = pl.multiple_of(order[i] * tokens, tokens)
        term = dot(attention_ref[:, pl.ds(at, tokens)], part_refs[i][...], NN)
        total = term if total is None else total + term
    total = total.astype(BF)
    side = dests[dests.shape[0] - 1]

    @pl.when(side == 0)
    def _():
        keep_ref[0] = total[:, :columns]
        send_ref[0] = total[:, columns:]

    @pl.when(side == 1)
    def _():
        keep_ref[0] = total[:, columns:]
        send_ref[0] = total[:, :columns]


ANY = pl.BlockSpec(memory_space=pl.ANY)
SMEM = pl.BlockSpec(memory_space=pltpu.SMEM)


def block_lists(block_ids, me, group, seg_dev, per_dev, cap):
    segments, per_seg, retr = block_ids.shape
    asked = per_seg * retr
    z = me // 2
    ids = block_ids.reshape(segments // (2 * seg_dev), 2, seg_dev, asked)
    ids = lax.dynamic_index_in_dim(ids, me % 2, 1, keepdims=False)
    slots = (z - jnp.arange(group, dtype=jnp.int32)) % group
    ids = jnp.take(ids, slots, axis=0).reshape(group * seg_dev, asked)
    owners = ids // per_dev
    here = owners // 2 == z
    place = ids - owners * per_dev + jnp.where(owners == me, 0, per_dev)
    position = jnp.arange(asked, dtype=jnp.int32)
    before = (position[None, :] < position[:, None])[None]
    rank = jnp.sum(jnp.logical_and(before, here[:, None, :]), axis=-1)
    chosen = jnp.logical_and(
        here[:, :, None], rank[:, :, None] == jnp.arange(cap, dtype=jnp.int32)
    )
    places = jnp.sum(jnp.where(chosen, place[:, :, None], 0), axis=1)
    home = position // retr - per_seg
    homes = per_seg + jnp.sum(jnp.where(chosen, home[None, :, None], 0), axis=1)
    counts = jnp.sum(here, axis=-1)
    return (
        counts.astype(jnp.int32),
        places.astype(jnp.int32).reshape(-1),
        homes.astype(jnp.int32).reshape(-1),
    )


def side_by_side(x):
    parts, rows, width = x.shape
    return x.transpose(1, 0, 2).reshape(rows, parts * width)


def gather_tokens(x):
    far = lax.ppermute(x, "fsdp", [(i, i ^ 2) for i in range(4)])
    near = lax.ppermute(x, "fsdp", [(i, i ^ 1) for i in range(4)])
    both = lax.ppermute(far, "fsdp", [(i, i ^ 1) for i in range(4)])
    return [x, near, far, both]


def weight_grad_plain(attention, parts, order):
    n = lax.axis_size("mem")
    rows = parts[0].shape[0]
    total = 0.0
    for i, part in enumerate(parts):
        own = lax.dynamic_slice_in_dim(attention, order[i] * rows, rows, 0)
        total = total + dot(own, part, TN)
    pieces = total.astype(BF).reshape(total.shape[0], n, -1).transpose(1, 0, 2)
    pieces = lax.all_to_all(pieces, "mem", split_axis=0, concat_axis=0, tiled=True)
    return jnp.sum(pieces.astype(F32), axis=0)


def cost(us):
    return pl.CostEstimate(flops=us * 10**9, bytes_accessed=us * 10**6, transcendentals=0)


def after(first, *rest):
    return lax.optimization_barrier((first, *rest))[1:]


def per_device(
    queries, keys, values, mem_keys, mem_values, block_ids, gate_bias, out_weight, cotangent
):
    n = lax.axis_size("mem")
    me = lax.axis_index("mem")
    fs = lax.axis_index("fsdp")
    group = n // 2
    full = mem_keys.shape[1]
    all_heads = full // DH
    width = full // HALVES
    heads = width // DH
    pairs = heads // 2
    segments, per_seg, retr = block_ids.shape
    seg_dev = segments // n
    per_dev = mem_keys.shape[0] // MBLK
    blocks = seg_dev * per_seg
    tokens = blocks * QBLK
    seg_len = per_seg * QBLK
    rows = queries.shape[0]
    seg_rows = seg_len // rows
    gating = jax.nn.sigmoid(lax.dynamic_slice_in_dim(gate_bias, fs * all_heads, all_heads))
    halves = range(HALVES)

    def shifted(x, k):
        return lax.ppermute(x, "mem", [(i, (i + 2 * k) % n) for i in range(n)])

    def exchange(x):
        return lax.all_to_all(x, "fsdp", split_axis=0, concat_axis=0, tiled=True)

    swap = [(i, i ^ 1) for i in range(n)]
    cap = -(-4 * max(1, retr * per_seg // n) // UNROLL) * UNROLL
    lists = block_lists(block_ids, me, group, seg_dev, per_dev, cap)

    par_keys = [lax.ppermute(mem_keys, "mem", swap)]
    par_values = [lax.ppermute(mem_values, "mem", swap)]

    q = exchange((queries * BF(SCALE)).T.reshape(4, full, rows))
    q_slots = [q] + [shifted(q, k) for k in range(1, group)]
    (cotangent,) = after(q, cotangent)
    cot_parts = gather_tokens(cotangent)
    keys, values = after(q, keys, values)
    k, v = (
        exchange(x.reshape(rows, 4, full).transpose(1, 0, 2)).reshape(tokens, full)
        for x in (keys, values)
    )
    cot_parts = after((q_slots, k, v), *cot_parts)
    order = fs ^ jnp.arange(4, dtype=jnp.int32)
    whole = pl.BlockSpec(memory_space=pltpu.VMEM)
    do_parts = pl.pallas_call(
        attention_grad_kernel,
        in_specs=[SMEM] + [whole] * 5,
        out_specs=[whole] * HALVES,
        out_shape=[jax.ShapeDtypeStruct((4, width, rows), BF)] * HALVES,
        compiler_params=pltpu.CompilerParams(vmem_limit_bytes=VMEM),
        cost_estimate=cost(1),
            name="attention_grad",
    )(order, out_weight, *cot_parts)
    do_slots = [[x] + [shifted(x, k) for k in range(1, group)] for x in do_parts]
    (late_weight,) = after(v, out_weight)
    full_weight = lax.all_gather(late_weight, "fsdp", axis=0, tiled=True)

    seg_spec = pl.BlockSpec((seg_len, full), lambda s: (s, 0))
    q_spec = pl.BlockSpec((seg_rows, full, rows), lambda s: (s, 0, 0))
    do_spec = pl.BlockSpec((seg_rows, width, rows), lambda s: (s, 0, 0))
    part_spec = pl.BlockSpec((per_seg, full, QBLK), lambda s: (s, 0, 0))
    part_shape = jax.ShapeDtypeStruct((blocks, full, QBLK), F32)
    head_shape = jax.ShapeDtypeStruct((tokens, full), BF)
    o_local, dq_local, dk, dv = pl.pallas_call(
        functools.partial(local_kernel, all_heads // 2, per_seg, HALVES),
        grid=(seg_dev,),
        in_specs=[SMEM, q_spec, seg_spec, seg_spec] + [do_spec] * HALVES,
        out_specs=[part_spec, part_spec, seg_spec, seg_spec],
        out_shape=[part_shape, part_shape, head_shape, head_shape],
        scratch_shapes=[pltpu.VMEM((seg_len, full), F32)] * 2,
        compiler_params=pltpu.CompilerParams(vmem_limit_bytes=VMEM),
        cost_estimate=cost(1),
            name="local",
    )(gating, q, k, v, *do_parts)

    lists = after((o_local, dk), *lists)
    t_specs = [
        pl.BlockSpec((per_seg, width, QBLK), at_slot(i, seg_dev - 1)) for i in range(group)
    ]
    t_shape = jax.ShapeDtypeStruct((blocks, width, QBLK), BF)
    slot_shape = jax.ShapeDtypeStruct((group, blocks, width, QBLK), F32)
    slot_spec = pl.BlockSpec((1, per_seg, width, QBLK), lambda s, b, *_: (s, b, 0, 0))
    all_spec = pl.BlockSpec((group, per_seg, width, QBLK), lambda s: (0, s, 0, 0))
    stat_block = (1, per_seg, 2, heads * QBLK)
    memory_rows = 2 * mem_keys.shape[0]
    scratch = [pltpu.VMEM((memory_rows, width), BF)] * 2
    scratch += [pltpu.VMEM((per_seg + 1, pairs, 128, 256), BF)] * 2
    scratch += [pltpu.VMEM((cap, pairs, MBLK, 256), F32)]
    acc = pltpu.VMEM((per_seg + 1, pairs, DH, 256), F32)
    rows8 = pltpu.VMEM((per_seg + 1, pairs, 8, 256), F32)
    rows1 = pltpu.VMEM((per_seg + 1, pairs, 1, 256), F32)
    sems = pltpu.SemaphoreType.DMA((4,))
    limit = pltpu.CompilerParams(vmem_limit_bytes=VMEM)
    def slot_specs(half):
        return [
            pl.BlockSpec((seg_rows, width, rows), at_slot(i, seg_dev - 1, half))
            for i in range(group)
        ]

    o_home, stat_slots = [], []
    spreads = [pltpu.VMEM((per_seg + 1, pairs, 128, 256), BF)]
    for i in halves:
        outs = pl.pallas_call(
            functools.partial(memory_forward, group, pairs, i),
            grid_spec=pltpu.PrefetchScalarGridSpec(
                num_scalar_prefetch=3,
                grid=(group, seg_dev),
                in_specs=[ANY] * 4 + slot_specs(i),
                out_specs=t_specs
                + [
                    slot_spec,
                    pl.BlockSpec(
                        (1, per_seg, 1, heads * QBLK), lambda s, b, *_: (s, b, 0, 0)
                    )
                ],
                scratch_shapes=scratch[:2] + spreads + scratch[-1:] + [rows8, rows8, acc, sems],
            ),
            out_shape=[t_shape] * group
            + [slot_shape]
            + [jax.ShapeDtypeStruct((group, blocks, 1, heads * QBLK), F32)],
            compiler_params=limit,
            cost_estimate=cost(30),
            name="memory_forward",
        )(*lists, mem_keys, par_keys[i], mem_values, par_values[i], *q_slots)
        o_slots, exact, lse = list(outs[:group]), outs[-2], outs[-1]
        stats = pl.pallas_call(
            functools.partial(statistics_kernel, group, heads),
            grid=(seg_dev,),
            in_specs=[
                pl.BlockSpec((group, per_seg, 1, heads * QBLK), lambda s: (0, s, 0, 0))
            ]
            + [pl.BlockSpec((seg_rows, width, rows), lambda s: (s, 0, 0))] * group
            + [all_spec],
            out_specs=pl.BlockSpec(
                (group, per_seg, 2, heads * QBLK), lambda s: (0, s, 0, 0)
            ),
            out_shape=jax.ShapeDtypeStruct((group, blocks, 2, heads * QBLK), F32),
            compiler_params=limit,
            cost_estimate=cost(5),
            name="statistics",
        )(lse, *do_slots[i], exact)
        stat_slots.append([stats] + [shifted(stats, k) for k in range(1, group)])
        if ORDER:
            middle = range(2, group - 1)
            held = after(stat_slots[-1], *[o_slots[j] for j in middle])
            for j, x in zip(middle, held):
                o_slots[j] = x
        o_home.append([o_slots[0]] + [shifted(o_slots[k], -k) for k in range(1, group)])

    last = stat_slots[-1][0]
    dq_home = []
    for i in halves:
        (own_stats,) = after(last, stat_slots[i][0])
        sums = pl.pallas_call(
            functools.partial(memory_backward, group, pairs, i),
            grid_spec=pltpu.PrefetchScalarGridSpec(
                num_scalar_prefetch=3,
                grid=(group, seg_dev),
                in_specs=[ANY] * 4
                + slot_specs(i)
                + slot_specs(0)
                + [pl.BlockSpec(stat_block, lambda s, b, *_: (s, b, 0, 0))],
                out_specs=[slot_spec] * 2,
                scratch_shapes=scratch + [rows1, rows1, acc, acc, sems],
            ),
            out_shape=[slot_shape] * 2,
            compiler_params=limit,
            cost_estimate=cost(30),
            name="memory_backward",
        )(
            *lists, mem_keys, par_keys[i], mem_values, par_values[i],
            *q_slots, *do_slots[i], own_stats,
        )
        wide_spec = pl.BlockSpec((per_seg, width, QBLK), lambda s: (s, 0, 0))
        dq_slots = pl.pallas_call(
            functools.partial(combine_kernel, group, heads),
            grid=(seg_dev,),
            in_specs=[
                pl.BlockSpec((group, per_seg, 2, heads * QBLK), lambda s: (0, s, 0, 0))
            ]
            * group
            + [all_spec] * 2,
            out_specs=[wide_spec] * group,
            out_shape=[t_shape] * group,
            compiler_params=limit,
            cost_estimate=cost(5),
            name="combine",
        )(*stat_slots[i], *sums)
        last = dq_slots[0]
        dq_home.append([dq_slots[0]] + [shifted(dq_slots[k], -k) for k in range(1, group)])

    dk, dv = after(last, dk, dv)
    key_grad, value_grad = [side_by_side(exchange(x.reshape(4, rows, full))) for x in (dk, dv)]
    home_spec = pl.BlockSpec((per_seg, width, QBLK), lambda b: (b, 0, 0))
    home_out = pl.BlockSpec((seg_len, width), lambda b: (b, 0))
    home_shape = jax.ShapeDtypeStruct((tokens, width), BF)
    home_specs = [
        pl.BlockSpec(stat_block, lambda b, k=k: (k, b, 0, 0)) for k in range(group)
    ]
    columns = out_weight.shape[1] // n
    steps = jnp.arange(group, dtype=jnp.int32)
    dests = jnp.concatenate([(me // 2 - steps) % group, (me % 2)[None]]).astype(jnp.int32)
    token_attention, weight_rows, token_dq = [], [], []
    for i in halves:
        local_spec = pl.BlockSpec((per_seg, width, QBLK), lambda b, i=i: (b, i, 0))
        home_stats = [stat_slots[i][(group - k) % group] for k in range(group)]
        o_parts = after(last, *o_home[i])
        attention, attention_t = pl.pallas_call(
            functools.partial(attention_kernel, group, heads, i * heads),
            grid=(seg_dev,),
            in_specs=[SMEM, local_spec] + [home_spec] * group + home_specs,
            out_specs=[home_out, pl.BlockSpec((width, seg_len), lambda b: (0, b))],
            out_shape=[home_shape, jax.ShapeDtypeStruct((width, tokens), BF)],
            compiler_params=limit,
            cost_estimate=cost(3),
            name="attention",
        )(gating, o_local, *o_parts, *home_stats)
        token_attention.append(exchange(attention.reshape(4, rows, width)))
        if columns % 128:
            weight_rows.append(weight_grad_plain(attention, cot_parts, order))
            continue
        piece = (1, width, columns)
        send, keep = pl.pallas_call(
            weight_grad_kernel,
            grid_spec=pltpu.PrefetchScalarGridSpec(
                num_scalar_prefetch=2,
                grid=(group,),
                in_specs=[pl.BlockSpec((width, tokens), lambda k, *_: (0, 0))]
                + [pl.BlockSpec((rows, 2 * columns), lambda k, _, to: (0, to[k]))] * 4,
                out_specs=[pl.BlockSpec(piece, lambda k, *_: (k, 0, 0))] * 2,
            ),
            out_shape=[jax.ShapeDtypeStruct((group, width, columns), BF)] * 2,
            compiler_params=limit,
            cost_estimate=cost(5),
            name="weight_grad",
        )(order, dests, attention_t, *cot_parts)
        got = lax.ppermute(send, "mem", swap)
        sums = [
            (keep[k].astype(F32) + got[k].astype(F32)).astype(BF) for k in range(group)
        ]
        sums = after(dq_home, *sums)
        sums = [sums[0]] + [shifted(sums[k], -k) for k in range(1, group)]
        weight_rows.append(functools.reduce(jnp.add, [x.astype(F32) for x in sums]))
    projected = jnp.einsum(
        "stc,scd->td",
        jnp.concatenate(token_attention, axis=2),
        full_weight.reshape(4, full, -1),
        preferred_element_type=F32,
    ).astype(BF)
    for i in halves:
        dq_parts = after(projected, *dq_home[i])
        local_spec = pl.BlockSpec((per_seg, width, QBLK), lambda b, i=i: (b, i, 0))
        dq = pl.pallas_call(
            functools.partial(query_grad_kernel, group, heads, i * heads),
            grid=(seg_dev,),
            in_specs=[SMEM, local_spec] + [home_spec] * group,
            out_specs=home_out,
            out_shape=home_shape,
            compiler_params=limit,
            cost_estimate=cost(3),
            name="query_grad",
        )(gating, dq_local, *dq_parts)
        token_dq.append(exchange(dq.reshape(4, rows, width)))

    return (
        projected,
        side_by_side(jnp.concatenate(token_dq, axis=2)),
        key_grad,
        value_grad,
        jnp.concatenate(weight_rows, axis=0),
    )


def solution(mesh):
    in_specs = (
        P(("mem", "fsdp"), None),
        P(("mem", "fsdp"), None),
        P(("mem", "fsdp"), None),
        P("mem", "fsdp"),
        P("mem", "fsdp"),
        P(),
        P(),
        P("fsdp", None),
        P(("mem", "fsdp"), None),
    )
    out_specs = (
        P(("mem", "fsdp"), None),
        P(("mem", "fsdp"), None),
        P(("mem", "fsdp"), None),
        P(("mem", "fsdp"), None),
        P("fsdp", "mem"),
    )
    return jax.shard_map(
        per_device, mesh=mesh, in_specs=in_specs, out_specs=out_specs, check_vma=False
    )
```
